32 devices in a mesh: blk: 16 (over z, x, core), fsdp: 2 (over y).
Axes of the slice: x: 2, y: 2, z: 4, core: 2. Of those that a mesh axis runs over, the one named last changes fastest.
Arguments:
- tokens: bfloat16 [32, 2048, 768], P('blk', 'fsdp'), may hold values from -6 to 6
- cotangent: bfloat16 [32, 2048, 768], P('blk', 'fsdp'), may hold values from -6 to 6
- segments: int32 [32, 2048], P('blk', 'fsdp'), may hold values from 0 to 7, as said below
- doc_lengths: int32 [32, 8], P('blk'), may hold values from 20 to 1026, as said below
- positions: int32 [32, 2048], P('blk', 'fsdp'), may hold values from 0 to 1025, as said below
- pairing: int32 [128], P('blk'), may hold values from 0 to 127, each once
- qkv_weight: bfloat16 [768, 2304], P('fsdp'), may hold values from -0.21875 to 0.21875
- out_weight: bfloat16 [768, 768], P('fsdp'), may hold values from -1.25 to 1.25
- swiglu_weight: bfloat16 [768, 6144], P('fsdp'), may hold values from -0.21875 to 0.21875
- down_weight: bfloat16 [3072, 768], P('fsdp'), may hold values from -0.109375 to 0.109375
- attn_gain: bfloat16 [768], P('fsdp'), may hold values from 0.5 to 1.5
- ffn_gain: bfloat16 [768], P('fsdp'), may hold values from 0.5 to 1.5
Outputs:
- loss_value: float32 [], replicated
- layer_output: bfloat16 [32, 2048, 768], P('blk', 'fsdp')
- input_grad: float32 [32, 2048, 768], P('blk', 'fsdp')
- qkv_grad: float32 [768, 2304], P('fsdp')
- out_grad: float32 [768, 768], P('fsdp')
- swiglu_grad: float32 [768, 6144], P('fsdp')
- down_grad: float32 [3072, 768], P('fsdp')
- attn_gain_grad: float32 [768], P('fsdp')
- ffn_gain_grad: float32 [768], P('fsdp')
The draws below stay inside these ranges and needn't reach their ends.
Inputs may be any that keep to these rules, and one draw needn't show every extreme that they name: `doc_lengths`: in each row, one segment at a place drawn from the seed has exactly the most tokens; the 7 other segments, among them one of exactly 20 tokens, add up to 7 * ((1024 - 1) // 7), each 20 or more, and the row's lengths add up to 2048. `segments`: segment numbers never fall along a row, and segment s covers doc_lengths[r, s] tokens. `positions`: A token's place within its segment, counted from 0. `pairing`: each document number once.
All inputs are finite; a program needn't handle non-finite values.
Results may differ from the reference program's by a relative error of at most 0.024.
Values may be sent and summed in bfloat16 or wider, within the bound.
No kernel may reach another device: no remote copies, remote signals or barrier semaphores. Data moves between devices by JAX's collectives and lax.ppermute only.
A program may use at most 384 MiB of HBM per device.

```python
import math
import jax
import jax.numpy as jnp
from jax import lax

D = 768
HEADS = 12
HDIM = 64
FF = 3072
ROW = 2048
SEGS = 8
SEG_MIN = 20
SH = 1024
ROWS = 32
NQ = 128


def segment_layout(key):
    key_long = jax.random.fold_in(key, 11)
    key_vary = jax.random.fold_in(key, 12)
    base_len = (SH - 1) // (SEGS - 1)
    spread = base_len - SEG_MIN
    long_place = jax.random.randint(key_long, (ROWS,), 0, SEGS)
    shifts = jax.random.randint(key_vary, (ROWS, SEGS - 1), 0, spread + 1)
    column = jnp.arange(SEGS - 1, dtype=jnp.int32)[None, :]
    shifts = jnp.where(column == 0, 0, jnp.where(column == 1, spread, shifts))
    shorts = base_len + shifts - jnp.roll(shifts, -1, axis=1)
    long_len = ROW - (SEGS - 1) * base_len
    places = jnp.arange(SEGS, dtype=jnp.int32)
    short_index = places[None, :] - (places[None, :] > long_place[:, None]).astype(jnp.int32)
    short_index = jnp.clip(short_index, 0, SEGS - 2)
    picked = jnp.take_along_axis(shorts, short_index, axis=1)
    lengths = jnp.where(places[None, :] == long_place[:, None], long_len, picked).astype(jnp.int32)
    ends = jnp.cumsum(lengths, axis=1)
    starts = ends - lengths
    token_place = jnp.arange(ROW, dtype=jnp.int32)
    seg_number = jnp.sum((token_place[None, :, None] >= ends[:, None, :]).astype(jnp.int32), -1)
    first_token = jnp.take_along_axis(starts, seg_number, axis=1)
    rotary_place = token_place[None, :] - first_token
    return (lengths, seg_number.astype(jnp.int32), rotary_place.astype(jnp.int32))


def draw_segments(key, part):
    layout = segment_layout(key)
    return layout[1]


def draw_doc_lengths(key, part):
    layout = segment_layout(key)
    return layout[0]


def draw_positions(key, part):
    layout = segment_layout(key)
    return layout[2]


def levels(rng, shape, pieces, least, high):
    factor_of, own = 1.0, jax.random.fold_in(rng, 6)
    for position, shards_of in pieces:
        steps = jnp.exp(jax.random.uniform(jax.random.fold_in(own, position), (shards_of,), jnp.float32, least / len(pieces), high / len(pieces)))
        factor_of = factor_of * jnp.repeat(steps, shape[position] // shards_of).reshape([-1 if axis == position else 1 for axis in range(len(shape))])
    return factor_of


def gaussian(rng, extent, width, limit, split=(), kind=jnp.bfloat16):
    level = levels(rng, extent, split, -0.22, 0.18) if split else 1.0
    values = jax.random.normal(rng, extent, jnp.float32) * width * level
    return jnp.minimum(jnp.maximum(values, -limit), limit).astype(kind)


def setup_inputs(seed: int = 0) -> dict:
    keys = jax.random.split(jax.random.key(seed), 13)
    tokens = gaussian(keys[0], (ROWS, ROW, D), 1.0, 6.0, ((0, 16), (1, 2)))
    cotangent = gaussian(keys[1], (ROWS, ROW, D), 1.0, 6.0, ((0, 16), (1, 2)))
    segments = draw_segments(jax.random.fold_in(keys[12], 71), 0)
    doc_lengths = draw_doc_lengths(jax.random.fold_in(keys[12], 71), 0)
    positions = draw_positions(jax.random.fold_in(keys[12], 71), 0)
    pairing = jax.random.permutation(keys[5], NQ).astype(jnp.int32)
    qkv_weight = gaussian(keys[6], (D, 3 * D), D ** -0.5, 0.21875, ((0, 2),))
    out_weight = gaussian(keys[7], (D, D), (D // 32) ** -0.5, 1.25, ((0, 2),))
    swiglu_weight = gaussian(keys[8], (D, 2 * FF), D ** -0.5, 0.21875, ((0, 2),))
    down_weight = gaussian(keys[9], (FF, D), FF ** -0.5, 0.109375, ((0, 2),))
    attn_gain = jnp.clip(1.0 + 0.1 * jax.random.normal(keys[10], (D,), jnp.float32), 0.5, 1.5).astype(jnp.bfloat16)
    ffn_gain = jnp.clip(1.0 + 0.1 * jax.random.normal(keys[11], (D,), jnp.float32), 0.5, 1.5).astype(jnp.bfloat16)
    return dict(tokens=tokens, cotangent=cotangent, segments=segments, doc_lengths=doc_lengths, positions=positions, pairing=pairing, qkv_weight=qkv_weight, out_weight=out_weight, swiglu_weight=swiglu_weight, down_weight=down_weight, attn_gain=attn_gain, ffn_gain=ffn_gain)


EPSILON = 1e-05
EMB_EPSILON = 1e-06
SOFTMAX_WARMTH = 0.05
ROPE_BASE = 1000.0
CONTRAST_WEIGHT = 512.0
NEGATIVE = -1e+30
TOP_PRECISION = lax.Precision.HIGHEST

@jax.custom_vjp
def low(v):
    return lax.optimization_barrier(v.astype(jnp.bfloat16)).astype(jnp.float32)

@jax.custom_vjp
def reduced_backward(v):
    return v

def low_keep(v):
    return (low(v), None)

def low_pass(kept, grad):
    return (grad,)

def back_keep(v):
    return (v, None)

def back_low(kept, grad):
    return (low(grad),)
low.defvjp(low_keep, low_pass)
reduced_backward.defvjp(back_keep, back_low)

def rope_tables(positions):
    half_dim = HDIM // 2
    frequency = ROPE_BASE ** (-2.0 * jnp.arange(half_dim, dtype=jnp.float32) / HDIM)
    angles = positions.astype(jnp.float32)[..., None] * frequency
    return (jnp.cos(angles), jnp.sin(angles))

def rotate(heads_in, cosine, sine):
    half_dim = HDIM // 2
    first_half = heads_in[..., :half_dim]
    second_half = heads_in[..., half_dim:]
    cosine = cosine[..., None, :]
    sine = sine[..., None, :]
    return jnp.concatenate([first_half * cosine - second_half * sine, second_half * cosine + first_half * sine], axis=-1)

def layer_norm(hidden_in, gain):
    average = lax.optimization_barrier(jnp.mean(hidden_in, -1, keepdims=True))
    centred = hidden_in - average
    variance = lax.optimization_barrier(jnp.mean(centred * centred, -1, keepdims=True))
    return centred * lax.rsqrt(variance + EPSILON) * gain

def attend_row(row_inputs):
    query_row, key_row, value_row, seg_row = row_inputs
    query_rows = math.gcd(ROW, 512)
    scale = 1.0 / math.sqrt(HDIM)

    def one_block(block_inputs):
        query_block, seg_block = block_inputs
        scores = jnp.einsum('qhd,khd->hqk', query_block, key_row, precision=TOP_PRECISION) * scale
        scores = reduced_backward(scores)
        allowed = (seg_block[:, None] == seg_row[None, :])[None]
        soft = jax.nn.softmax(jnp.where(allowed, scores, NEGATIVE), axis=-1)
        return jnp.einsum('hqk,khd->qhd', low(soft), value_row, precision=TOP_PRECISION)
    blocks = lax.map(jax.checkpoint(one_block), (query_row.reshape(ROW // query_rows, query_rows, HEADS, HDIM), seg_row.reshape(ROW // query_rows, query_rows)))
    return blocks.reshape(ROW, HEADS, HDIM)

def forward(inputs, qkv_w, out_w, swiglu_w, down_w, attn_g, ffn_g, segments, doc_lengths, positions, pairing):
    projected = reduced_backward(jnp.einsum('rtd,de->rte', inputs, qkv_w, precision=TOP_PRECISION))
    query = projected[..., :D].reshape(ROWS, ROW, HEADS, HDIM)
    key_heads = projected[..., D:2 * D].reshape(ROWS, ROW, HEADS, HDIM)
    value_heads = projected[..., 2 * D:].reshape(ROWS, ROW, HEADS, HDIM)
    cosine, sine = rope_tables(positions)
    query = low(rotate(query, cosine, sine))
    key_heads = low(rotate(key_heads, cosine, sine))
    value_heads = low(value_heads)
    mixed = lax.map(attend_row, (query, key_heads, value_heads, segments))
    attended = low(reduced_backward(mixed.reshape(ROWS, ROW, D)))
    branch = reduced_backward(jnp.einsum('rtd,de->rte', attended, out_w, precision=TOP_PRECISION))
    normed = layer_norm(inputs + branch, attn_g)
    gate_up = reduced_backward(jnp.einsum('rtd,de->rte', low(normed), swiglu_w, precision=TOP_PRECISION))
    gate_value = gate_up[..., :FF]
    up_value = gate_up[..., FF:]
    hidden = low(jax.nn.silu(gate_value) * up_value)
    ffn_out = reduced_backward(jnp.einsum('rtf,fd->rtd', hidden, down_w, precision=TOP_PRECISION))
    output = layer_norm(normed + ffn_out, ffn_g)
    member = (segments[..., None] == jnp.arange(SEGS, dtype=jnp.int32)).astype(output.dtype)
    pooled = jnp.einsum('rts,rtd->rsd', member, output, precision=TOP_PRECISION) / doc_lengths.astype(output.dtype)[..., None]
    embedded = pooled * lax.rsqrt(lax.optimization_barrier(jnp.sum(pooled * pooled, -1, keepdims=True)) + EMB_EPSILON)
    embedded = low(embedded)
    query_vectors = embedded[:, 0::2].reshape(NQ, D)
    document_rows = embedded[:, 1::2].reshape(NQ, D)
    similarity_matrix = reduced_backward(jnp.dot(query_vectors, document_rows.T, precision=TOP_PRECISION) / SOFTMAX_WARMTH)
    target = (pairing[:, None] == jnp.arange(NQ, dtype=jnp.int32)[None, :]).astype(similarity_matrix.dtype)
    loss_sum = jnp.sum(jax.nn.logsumexp(similarity_matrix, axis=-1) - lax.optimization_barrier(jnp.sum(target * similarity_matrix, -1)))
    return (output, loss_sum)

def reference(tokens, cotangent, segments, doc_lengths, positions, pairing, qkv_weight, out_weight, swiglu_weight, down_weight, attn_gain, ffn_gain):
    single_document = jnp.float32

    def wrapped(inputs, qkv_w, out_w, swiglu_w, down_w, attn_g, ffn_g):
        return forward(inputs, qkv_w, out_w, swiglu_w, down_w, attn_g, ffn_g, segments, doc_lengths, positions, pairing)
    results, pullback = jax.vjp(wrapped, tokens.astype(single_document), qkv_weight.astype(single_document), out_weight.astype(single_document), swiglu_weight.astype(single_document), down_weight.astype(single_document), attn_gain.astype(single_document), ffn_gain.astype(single_document))
    output, loss_sum = results
    grads = pullback((cotangent.astype(single_document), jnp.full_like(loss_sum, CONTRAST_WEIGHT)))
    return (loss_sum / NQ, output.astype(jnp.bfloat16), grads[0], grads[1], grads[2], grads[3], grads[4], grads[5], grads[6])
```

```python
import functools
import math

import jax
import jax.numpy as jnp
from jax import lax
from jax.experimental import pallas as pl
from jax.experimental.pallas import tpu as pltpu
from jax.sharding import PartitionSpec as P

HEADS = 12
HDIM = 64
PAIRS = HEADS // 2
LANES = 128
SEG = 8

EPSILON = 1e-05
EMB_EPSILON = 1e-06
SOFTMAX_WARMTH = 0.05
ROPE_BASE = 1000.0
CONTRAST_WEIGHT = 512.0
NEGATIVE = -1e30

BF = jnp.bfloat16
F32 = jnp.float32
MIB = 1 << 20


def dot(a, b):
    return lax.dot_general(a, b, (((1,), (0,)), ((), ())), preferred_element_type=F32)


def dot_bt(a, b):
    return lax.dot_general(a, b, (((1,), (1,)), ((), ())), preferred_element_type=F32)


def dot_at(a, b):
    return lax.dot_general(a, b, (((0,), (0,)), ((), ())), preferred_element_type=F32)


def lane_iota(shape):
    return lax.broadcasted_iota(jnp.int32, shape, len(shape) - 1)


def halves_swapped(block):
    low = lane_iota(block.shape) % HDIM < HDIM // 2
    return jnp.where(low, pltpu.roll(block, LANES - 32, 1), pltpu.roll(block, 32, 1))


def weight_pieces(weight, flip):
    rows, cols = weight.shape
    shards = lax.axis_size("fsdp")
    mine = lax.axis_index("fsdp")
    blocks = lax.axis_size("blk")
    if shards != 2 or blocks % 4:
        return [lax.all_gather(weight, "fsdp", axis=0, tiled=True)], [(0, 0)]
    place = lax.axis_index("blk")
    core, side = place % 2, (place // 2) % 2
    r2, c2 = rows // 2, cols // 2
    piece = lax.dynamic_slice(weight, (side * r2, core * c2), (r2, c2))
    first = lax.ppermute(piece, "fsdp", [(0, 1), (1, 0)])
    second = lax.ppermute(first, "blk", [(i, i ^ 2) for i in range(blocks)])
    over = [(i, i ^ 1) for i in range(blocks)]
    third = lax.ppermute(first, "blk", over)
    fourth = lax.ppermute(second, "blk", over)
    other = (1 - mine) * rows
    return [weight, first, second, third, fourth], [
        (mine * rows, 0),
        (other + side * r2, core * c2),
        (other + (1 - side) * r2, core * c2),
        (other + side * r2, (1 - core) * c2),
        (other + (1 - side) * r2, (1 - core) * c2),
    ]


def as_table(offsets):
    return jnp.stack([jnp.asarray(v, jnp.int32) for pair in offsets for v in pair])


def weight_copies(table, base, pieces, whole, sems):
    copies = []
    for n, piece in enumerate(pieces):
        rows, cols = piece.shape
        row = pl.multiple_of(table[2 * (base + n)], 16)
        col = pl.multiple_of(table[2 * (base + n) + 1], LANES)
        copies.append(
            pltpu.make_async_copy(
                piece, whole.at[pl.ds(row, rows), pl.ds(col, cols)], sems.at[base + n]
            )
        )
    return copies


ANY = pl.BlockSpec(memory_space=pl.ANY)


def params(limit_mib):
    return pltpu.CompilerParams(vmem_limit_bytes=limit_mib * MIB)


def qkv_kernel(count, table, x_ref, cos_ref, sin_ref, *rest):
    pieces, (q_ref, k_ref, v_ref, whole, sems) = rest[:count], rest[count:]
    width = q_ref.shape[1]

    @pl.when(pl.program_id(0) == 0)
    def _():
        copies = weight_copies(table, 0, pieces, whole, sems)
        for copy in copies:
            copy.start()
        for copy in copies:
            copy.wait()

    x = x_ref[...]
    cosine, sine = cos_ref[...], sin_ref[...]
    for ref, start, factor in ((q_ref, 0, 1.0 / math.sqrt(HDIM)), (k_ref, width, 1.0)):
        projected = dot(x, whole[:, start : start + width])
        for b in range(0, width, LANES):
            block = projected[:, b : b + LANES]
            turned = block * cosine + halves_swapped(block) * sine
            ref[:, b : b + LANES] = turned.astype(BF) * jnp.asarray(factor, BF)
    v_ref[...] = dot(x, whole[:, 2 * width :]).astype(BF)


def project(x, cosine, sine, weight, tile):
    pieces, offsets = weight
    tokens, width = x.shape
    row = lambda i, *_: (i, 0)
    return pl.pallas_call(
        functools.partial(qkv_kernel, len(pieces)),
        grid_spec=pltpu.PrefetchScalarGridSpec(
            num_scalar_prefetch=1,
            grid=(tokens // tile,),
            in_specs=[
                pl.BlockSpec((tile, width), row),
                pl.BlockSpec((tile, LANES), row),
                pl.BlockSpec((tile, LANES), row),
            ]
            + [ANY] * len(pieces),
            out_specs=[pl.BlockSpec((tile, width), row)] * 3,
            scratch_shapes=[
                pltpu.VMEM((width, 3 * width), BF),
                pltpu.SemaphoreType.DMA((len(pieces),)),
            ],
        ),
        out_shape=[jax.ShapeDtypeStruct((tokens, width), BF)] * 3,
        compiler_params=params(40),
        cost_estimate=pl.CostEstimate(
            flops=6 * tokens * width * width, bytes_accessed=16 * MIB, transcendentals=0
        ),
    )(as_table(offsets), x, cosine, sine, *pieces)


def input_grad_kernel(count, table, dbr_ref, dq_ref, dk_ref, dv_ref, *rest):
    pieces, (out_ref, whole, sems) = rest[:count], rest[count:]
    width = dq_ref.shape[1]

    @pl.when(pl.program_id(0) == 0)
    def _():
        copies = weight_copies(table, 1, pieces, whole, sems)
        for copy in copies:
            copy.start()
        for copy in copies:
            copy.wait()

    total = dbr_ref[...].astype(F32)
    for n, ref in enumerate((dq_ref, dk_ref, dv_ref)):
        total += dot_bt(ref[...], whole[:, n * width : (n + 1) * width])
    out_ref[...] = total.astype(out_ref.dtype)


def input_grad_part(dbr, dq, dk, dv, weight, start, tokens, dtype, tile):
    pieces, offsets = weight
    width = dq.shape[1]
    table = as_table([(start // tile, 0), *offsets])
    shifted = lambda i, t: (i + t[0], 0)
    return pl.pallas_call(
        functools.partial(input_grad_kernel, len(pieces)),
        grid_spec=pltpu.PrefetchScalarGridSpec(
            num_scalar_prefetch=1,
            grid=(tokens // tile,),
            in_specs=[pl.BlockSpec((tile, width), shifted)] * 4 + [ANY] * len(pieces),
            out_specs=pl.BlockSpec((tile, width), lambda i, t: (i, 0)),
            scratch_shapes=[
                pltpu.VMEM((width, 3 * width), BF),
                pltpu.SemaphoreType.DMA((len(pieces) + 1,)),
            ],
        ),
        out_shape=jax.ShapeDtypeStruct((tokens, width), dtype),
        compiler_params=params(40),
        cost_estimate=pl.CostEstimate(
            flops=6 * tokens * width * width, bytes_accessed=16 * MIB, transcendentals=0
        ),
    )(table, dbr, dq, dk, dv, *pieces)


BQ = 256
BK = 256


def attend_kernel(spans, q_ref, k_ref, v_ref, kf_ref, qf_ref, o_ref, lse_ref, kx, vte, vto):
    block = pl.program_id(2)
    where = (pl.program_id(0) * pl.num_programs(2) + block) * 2
    row_len = k_ref.shape[0]

    @pl.when(block == 0)
    def _():
        kx[:, :LANES] = k_ref[...]
        kx[:, LANES:] = kf_ref[...]
        for b in range(0, row_len, BK):
            turned = v_ref[b : b + BK, :].astype(F32).T
            upper = lax.broadcasted_iota(jnp.int32, turned.shape, 0) < HDIM
            vte[:, b : b + BK] = jnp.where(upper, turned, 1.0).astype(BF)
            vto[:, b : b + BK] = jnp.where(upper, 1.0, turned).astype(BF)

    q, qf = q_ref[...], qf_ref[...]
    even = lane_iota(q.shape) < HDIM
    zero = jnp.zeros_like(q)
    queries = (
        jnp.concatenate([jnp.where(even, q, zero), qf], axis=1),
        jnp.concatenate([jnp.where(even, zero, q), qf], axis=1),
    )
    first, count = spans[where], spans[where + 1]

    def step(j, state):
        at = pl.multiple_of(first + j * BK, LANES)
        keys = kx[pl.ds(at, BK), :]
        values = (vte[:, pl.ds(at, BK)], vto[:, pl.ds(at, BK)])
        out = []
        for h in range(2):
            best, accum = state[2 * h], state[2 * h + 1]
            scores = dot_bt(keys, queries[h])
            new = jnp.maximum(best, jnp.max(scores, axis=0, keepdims=True))
            soft = jnp.exp(scores - new).astype(BF)
            accum = accum * jnp.exp(best - new) + dot(values[h], soft)
            out += [new, accum]
        return tuple(out)

    start = (jnp.full((1, BQ), NEGATIVE, F32), jnp.zeros((LANES, BQ), F32)) * 2
    best_e, acc_e, best_o, acc_o = lax.fori_loop(0, count, step, start)
    sum_e, sum_o = acc_e[HDIM : HDIM + 1], acc_o[0:1]
    turned = jnp.concatenate([acc_e[:HDIM] / sum_e, acc_o[HDIM:] / sum_o], axis=0)
    o_ref[...] = turned.T.astype(BF)
    lse_ref[0, 0:1, :] = best_e + jnp.log(sum_e)
    lse_ref[0, 1:2, :] = best_o + jnp.log(sum_o)


def attend(q, k, v, key_feat, query_feat, spans, rows):
    tokens, width = q.shape
    row_len = k.shape[0] // rows
    blocks = tokens // rows // BQ
    of_q = lambda r, p, i, *_: (r * blocks + i, p)
    of_k = lambda r, p, i, *_: (r, p)
    return pl.pallas_call(
        attend_kernel,
        grid_spec=pltpu.PrefetchScalarGridSpec(
            num_scalar_prefetch=1,
            grid=(rows, PAIRS, blocks),
            in_specs=[
                pl.BlockSpec((BQ, LANES), of_q),
                pl.BlockSpec((row_len, LANES), of_k),
                pl.BlockSpec((row_len, LANES), of_k),
                pl.BlockSpec((row_len, LANES), lambda r, p, i, *_: (r, 0)),
                pl.BlockSpec((BQ, LANES), lambda r, p, i, *_: (r * blocks + i, 0)),
            ],
            out_specs=[
                pl.BlockSpec((BQ, LANES), of_q),
                pl.BlockSpec((1, 2, BQ), lambda r, p, i, *_: (p, 0, r * blocks + i)),
            ],
            scratch_shapes=[
                pltpu.VMEM((row_len, 2 * LANES), BF),
                pltpu.VMEM((LANES, row_len), BF),
                pltpu.VMEM((LANES, row_len), BF),
            ],
        ),
        out_shape=[
            jax.ShapeDtypeStruct((tokens, width), BF),
            jax.ShapeDtypeStruct((PAIRS, 2, tokens), F32),
        ],
        compiler_params=params(40),
        cost_estimate=pl.CostEstimate(
            flops=tokens * row_len * width * 4, bytes_accessed=16 * MIB, transcendentals=0
        ),
    )(spans, q, k, v, key_feat, query_feat)


def attend_back_kernel(
    spans, q_ref, do_ref, k_ref, v_ref, kf_ref, qf_ref, cq_ref, sq_ref, ck_ref, sk_ref,
    dq_ref, dk_ref, dv_ref, kx, vx, kt, dk_acc, dv_acc,
):
    pair, block = pl.program_id(1), pl.program_id(2)
    where = (pl.program_id(0) * pl.num_programs(2) + block) * 2
    row_len = k_ref.shape[0]

    @pl.when(block == 0)
    def _():
        kx[:, :LANES] = k_ref[...]
        kx[:, LANES:] = kf_ref[...]
        vx[:, :LANES] = v_ref[...]
        vx[:, LANES:] = kf_ref[...]
        for b in range(0, row_len, BK):
            kt[:, b : b + BK] = k_ref[b : b + BK, :].astype(F32).T.astype(BF)
        dk_acc[...] = jnp.zeros_like(dk_acc)
        dv_acc[...] = jnp.zeros_like(dv_acc)

    q, do, qf = q_ref[...], do_ref[...], qf_ref[...]
    lanes = lane_iota(q.shape)
    even = lanes < HDIM
    zero = jnp.zeros_like(q)
    split_q = (jnp.where(even, q, zero), jnp.where(even, zero, q))
    split_do = (jnp.where(even, do, zero), jnp.where(even, zero, do))
    queries, upstream = [], []
    for h in range(2):
        lane = lanes - (2 * pair + h)
        of_lse = (lanes < SEG) | (lane == 8) | (lane == 20) | (lane == 32)
        of_delta = (lane == 44) | (lane == 56) | (lane == 68)
        queries.append(jnp.concatenate([split_q[h], jnp.where(of_lse, qf, zero)], axis=1))
        upstream.append(jnp.concatenate([split_do[h], jnp.where(of_delta, qf, zero)], axis=1))
    stacked_q = jnp.concatenate(split_q, axis=0)
    stacked_do = jnp.concatenate(split_do, axis=0)
    first, count = spans[where], spans[where + 1]

    def step(j, state):
        at = pl.multiple_of(first + j * BK, LANES)
        keys, values = kx[pl.ds(at, BK), :], vx[pl.ds(at, BK), :]
        turned_keys = kt[:, pl.ds(at, BK)]
        soft, grads, out = [], [], []
        for h in range(2):
            probs = jnp.exp(dot_bt(keys, queries[h]))
            grad = (probs * dot_bt(values, upstream[h])).astype(BF)
            soft.append(probs.astype(BF))
            grads.append(grad)
            out.append(state[h] + dot(turned_keys[h * HDIM : (h + 1) * HDIM], grad))
        dv_acc[pl.ds(at, BK), :] += dot(jnp.concatenate(soft, axis=1), stacked_do)
        dk_acc[pl.ds(at, BK), :] += dot(jnp.concatenate(grads, axis=1), stacked_q)
        return tuple(out)

    start = (jnp.zeros((HDIM, BQ), F32),) * 2
    turned = jnp.concatenate(lax.fori_loop(0, count, step, start), axis=0)
    dq = turned.T * (1.0 / math.sqrt(HDIM))
    dq_ref[...] = (dq * cq_ref[...] - halves_swapped(dq) * sq_ref[...]).astype(BF)

    @pl.when(block == pl.num_programs(2) - 1)
    def _():
        for b in range(0, row_len, BK):
            part = pl.ds(b, BK)
            dk = dk_acc[part, :]
            dk_ref[part, :] = (dk * ck_ref[part, :] - halves_swapped(dk) * sk_ref[part, :]).astype(BF)
            dv_ref[part, :] = dv_acc[part, :].astype(BF)


def attend_back(q, do, k, v, key_feat, query_feat, spans, tables_q, tables_k, rows):
    tokens, width = q.shape
    row_len = k.shape[0] // rows
    blocks = tokens // rows // BQ
    of_q = lambda r, p, i, *_: (r * blocks + i, p)
    of_k = lambda r, p, i, *_: (r, p)
    per_q = pl.BlockSpec((BQ, LANES), lambda r, p, i, *_: (r * blocks + i, 0))
    per_k = pl.BlockSpec((row_len, LANES), lambda r, p, i, *_: (r, 0))
    return pl.pallas_call(
        attend_back_kernel,
        grid_spec=pltpu.PrefetchScalarGridSpec(
            num_scalar_prefetch=1,
            grid=(rows, PAIRS, blocks),
            in_specs=[
                pl.BlockSpec((BQ, LANES), of_q),
                pl.BlockSpec((BQ, LANES), of_q),
                pl.BlockSpec((row_len, LANES), of_k),
                pl.BlockSpec((row_len, LANES), of_k),
                per_k,
                per_q,
                per_q,
                per_q,
                per_k,
                per_k,
            ],
            out_specs=[
                pl.BlockSpec((BQ, LANES), of_q),
                pl.BlockSpec((row_len, LANES), of_k),
                pl.BlockSpec((row_len, LANES), of_k),
            ],
            scratch_shapes=[
                pltpu.VMEM((row_len, 2 * LANES), BF),
                pltpu.VMEM((row_len, 2 * LANES), BF),
                pltpu.VMEM((LANES, row_len), BF),
                pltpu.VMEM((row_len, LANES), F32),
                pltpu.VMEM((row_len, LANES), F32),
            ],
        ),
        out_shape=[
            jax.ShapeDtypeStruct((tokens, width), BF),
            jax.ShapeDtypeStruct((rows * row_len, width), BF),
            jax.ShapeDtypeStruct((rows * row_len, width), BF),
        ],
        compiler_params=params(48),
        cost_estimate=pl.CostEstimate(
            flops=tokens * row_len * width * 10, bytes_accessed=24 * MIB, transcendentals=0
        ),
    )(spans, q, do, k, v, key_feat, query_feat, *tables_q, *tables_k)


FF_CHUNK = 512


def normalize(hidden):
    average = jnp.mean(hidden, -1, keepdims=True)
    centred = hidden - average
    inverse = lax.rsqrt(jnp.mean(centred * centred, -1, keepdims=True) + EPSILON)
    return centred * inverse, inverse


def norm_back(scaled, normalized, inverse):
    return inverse * (
        scaled
        - jnp.mean(scaled, -1, keepdims=True)
        - normalized * jnp.mean(scaled * normalized, -1, keepdims=True)
    )


def split_two(value):
    high = value.astype(BF)
    return high, (value - high.astype(F32)).astype(BF)


def mix_kernel(counts, table, att_ref, x_ref, qf_ref, g1_ref, g2_ref, *rest):
    total = sum(counts)
    pieces, (nl_ref, stat_ref, gu_ref, out_ref, pool_ref, wo, ws, wd, sems) = rest[:total], rest[total:]
    groups, base = [], 0
    for count, whole in zip(counts, (wo, ws, wd)):
        groups.append(weight_copies(table, base, pieces[base : base + count], whole, sems))
        base += count
    step, begin = pl.program_id(1), (pl.program_id(0) == 0) & (pl.program_id(1) == 0)

    @pl.when(begin)
    def _():
        for group in groups:
            for copy in group:
                copy.start()
        for copy in groups[0]:
            copy.wait()

    branch = dot(att_ref[...], wo[...])
    unit, inverse1 = normalize(x_ref[...].astype(F32) + branch)
    normed = unit * g1_ref[...]
    low = normed.astype(BF)
    nl_ref[...] = low

    @pl.when(begin)
    def _():
        for group in groups[1:]:
            for copy in group:
                copy.wait()

    ff = wd.shape[0]
    hidden_sum = normed
    for c in range(0, ff, FF_CHUNK):
        gate = dot(low, ws[:, c : c + FF_CHUNK])
        up = dot(low, ws[:, ff + c : ff + c + FF_CHUNK])
        gu_ref[:, c : c + FF_CHUNK] = gate.astype(BF)
        gu_ref[:, ff + c : ff + c + FF_CHUNK] = up.astype(BF)
        hidden = (gate * (0.5 + 0.5 * jnp.tanh(0.5 * gate)) * up).astype(BF)
        hidden_sum = hidden_sum + dot(hidden, wd[c : c + FF_CHUNK, :])
    unit2, inverse2 = normalize(hidden_sum)
    output = unit2 * g2_ref[...]
    out_ref[...] = output.astype(BF)
    lanes = lane_iota(stat_ref.shape)
    stat_ref[...] = jnp.where(lanes == 0, inverse1, inverse2)
    high, rest_low = split_two(output)
    member = qf_ref[...]
    sums = (dot_at(member, high) + dot_at(member, rest_low))[:SEG]

    @pl.when(step == 0)
    def _():
        pool_ref[0] = sums

    @pl.when(step > 0)
    def _():
        pool_ref[0] += sums


def mix(attended, x, query_feat, gain1, gain2, weights, rows, tile):
    tokens, width = x.shape
    counts = [len(w[0]) for w in weights]
    pieces = [p for w in weights for p in w[0]]
    offsets = [o for w in weights for o in w[1]]
    steps = tokens // rows // tile
    ff = sum_rows(weights[2])
    row = lambda r, i, *_: (r * steps + i, 0)
    fixed = lambda r, i, *_: (0, 0)
    return pl.pallas_call(
        functools.partial(mix_kernel, counts),
        grid_spec=pltpu.PrefetchScalarGridSpec(
            num_scalar_prefetch=1,
            grid=(rows, steps),
            in_specs=[
                pl.BlockSpec((tile, width), row),
                pl.BlockSpec((tile, width), row),
                pl.BlockSpec((tile, LANES), row),
                pl.BlockSpec((1, width), fixed),
                pl.BlockSpec((1, width), fixed),
            ]
            + [ANY] * len(pieces),
            out_specs=[
                pl.BlockSpec((tile, width), row),
                pl.BlockSpec((tile, LANES), row),
                pl.BlockSpec((tile, 2 * ff), row),
                pl.BlockSpec((tile, width), row),
                pl.BlockSpec((1, SEG, width), lambda r, i, *_: (r, 0, 0)),
            ],
            scratch_shapes=[
                pltpu.VMEM((width, width), BF),
                pltpu.VMEM((width, 2 * ff), BF),
                pltpu.VMEM((ff, width), BF),
                pltpu.SemaphoreType.DMA((len(pieces),)),
            ],
        ),
        out_shape=[
            jax.ShapeDtypeStruct((tokens, width), BF),
            jax.ShapeDtypeStruct((tokens, LANES), F32),
            jax.ShapeDtypeStruct((tokens, 2 * ff), BF),
            jax.ShapeDtypeStruct((tokens, width), BF),
            jax.ShapeDtypeStruct((rows, SEG, width), F32),
        ],
        compiler_params=params(56),
        cost_estimate=pl.CostEstimate(
            flops=2 * tokens * width * (width + 3 * ff), bytes_accessed=64 * MIB, transcendentals=0
        ),
    )(as_table(offsets), attended, x, query_feat, gain1, gain2, *pieces)


def sum_rows(weight):
    pieces, offsets = weight
    return pieces[0].shape[0] * (1 if len(pieces) == 1 else 2)


def mix_back_kernel(
    counts, table, cot_ref, out_ref, nl_ref, stat_ref, qf_ref, dp_ref, gu_ref, att_ref, lse_ref, g1_ref, g2_ref, head_ref,
    *rest,
):
    total = sum(counts)
    pieces = rest[:total]
    dffn_ref, hid_ref, dgu_ref, dbr_ref, datt_ref, feat_ref, ga_ref, gf_ref, wo, ws, wd, sems = rest[total:]
    groups, base = [], 0
    for count, whole in zip(counts, (wo, ws, wd)):
        groups.append(weight_copies(table, base, pieces[base : base + count], whole, sems))
        base += count
    begin = (pl.program_id(0) == 0) & (pl.program_id(1) == 0)

    @pl.when(begin)
    def _():
        for group in groups[::-1]:
            for copy in group:
                copy.start()

    stat = stat_ref[...]
    inverse1, inverse2 = stat[:, 0:1], stat[:, 1:2]
    member = qf_ref[...]
    high, rest_low = split_two(dp_ref[0])
    upstream = cot_ref[...].astype(F32) + dot(member, high) + dot(member, rest_low)
    gain2 = g2_ref[...]
    unit2 = out_ref[...].astype(F32) / gain2
    second = norm_back(upstream * gain2, unit2, inverse2)
    gain2_part = upstream * unit2
    dffn = second.astype(BF)
    dffn_ref[...] = dffn

    @pl.when(begin)
    def _():
        ga_ref[...] = jnp.zeros_like(ga_ref)
        gf_ref[...] = jnp.zeros_like(gf_ref)
        for group in groups:
            for copy in group:
                copy.wait()

    ff = wd.shape[0]
    dnormed = second
    for c in range(0, ff, FF_CHUNK):
        dhid = dot_bt(dffn, wd[c : c + FF_CHUNK, :])
        gate = gu_ref[:, c : c + FF_CHUNK].astype(F32)
        up = gu_ref[:, ff + c : ff + c + FF_CHUNK].astype(F32)
        sig = 0.5 + 0.5 * jnp.tanh(0.5 * gate)
        silu = gate * sig
        hid_ref[:, c : c + FF_CHUNK] = (silu * up).astype(BF)
        dgate = (dhid * up * (sig + silu * (1.0 - sig))).astype(BF)
        dup = (dhid * silu).astype(BF)
        dgu_ref[:, c : c + FF_CHUNK] = dgate
        dgu_ref[:, ff + c : ff + c + FF_CHUNK] = dup
        dnormed = dnormed + dot_bt(dgate, ws[:, c : c + FF_CHUNK])
        dnormed = dnormed + dot_bt(dup, ws[:, ff + c : ff + c + FF_CHUNK])
    gain1 = g1_ref[...]
    unit1 = nl_ref[...].astype(F32) / gain1
    first = norm_back(dnormed * gain1, unit1, inverse1)
    gain1_part = dnormed * unit1
    dbr = first.astype(BF)
    dbr_ref[...] = dbr
    datt = dot_bt(dbr, wo[...]).astype(BF)
    datt_ref[...] = datt
    tile, width = datt.shape
    ga_ref[...] += jnp.sum(gain1_part.reshape(tile // 8, 8, width), axis=0)
    gf_ref[...] += jnp.sum(gain2_part.reshape(tile // 8, 8, width), axis=0)

    high, rest_low = split_two(datt.astype(F32) * att_ref[...].astype(F32))
    heads = head_ref[...]
    delta = dot(high, heads) + dot(rest_low, heads)
    feat = member.astype(F32)
    for value, start in ((lse_ref[...], 8), (delta, 44)):
        left = -value
        for n in range(3):
            part = left.astype(BF).astype(F32)
            left = left - part
            feat = feat + pltpu.roll(part, start + HEADS * n, 1)
    feat_ref[...] = feat.astype(BF)


def mix_back(cot, output, low, stat, query_feat, dpool, gate_up, attended, lse, gain1, gain2, weights, rows, tile):
    tokens, width = cot.shape
    counts = [len(w[0]) for w in weights]
    pieces = [p for w in weights for p in w[0]]
    offsets = [o for w in weights for o in w[1]]
    steps = tokens // rows // tile
    ff = sum_rows(weights[2])
    row = lambda r, i, *_: (r * steps + i, 0)
    fixed = lambda r, i, *_: (0, 0)
    wide, narrow = pl.BlockSpec((tile, width), row), pl.BlockSpec((tile, LANES), row)
    heads = (jnp.arange(width)[:, None] // HDIM == jnp.arange(LANES)[None, :]).astype(BF)
    return pl.pallas_call(
        functools.partial(mix_back_kernel, counts),
        grid_spec=pltpu.PrefetchScalarGridSpec(
            num_scalar_prefetch=1,
            grid=(rows, steps),
            in_specs=[
                wide,
                wide,
                wide,
                narrow,
                narrow,
                pl.BlockSpec((1, LANES, width), lambda r, i, *_: (r, 0, 0)),
                pl.BlockSpec((tile, 2 * ff), row),
                wide,
                narrow,
                pl.BlockSpec((1, width), fixed),
                pl.BlockSpec((1, width), fixed),
                pl.BlockSpec((width, LANES), fixed),
            ]
            + [ANY] * len(pieces),
            out_specs=[
                wide,
                pl.BlockSpec((tile, ff), row),
                pl.BlockSpec((tile, 2 * ff), row),
                wide,
                wide,
                narrow,
                pl.BlockSpec((8, width), fixed),
                pl.BlockSpec((8, width), fixed),
            ],
            scratch_shapes=[
                pltpu.VMEM((width, width), BF),
                pltpu.VMEM((width, 2 * ff), BF),
                pltpu.VMEM((ff, width), BF),
                pltpu.SemaphoreType.DMA((len(pieces),)),
            ],
        ),
        out_shape=[
            jax.ShapeDtypeStruct((tokens, width), BF),
            jax.ShapeDtypeStruct((tokens, ff), BF),
            jax.ShapeDtypeStruct((tokens, 2 * ff), BF),
            jax.ShapeDtypeStruct((tokens, width), BF),
            jax.ShapeDtypeStruct((tokens, width), BF),
            jax.ShapeDtypeStruct((tokens, LANES), BF),
            jax.ShapeDtypeStruct((8, width), F32),
            jax.ShapeDtypeStruct((8, width), F32),
        ],
        compiler_params=params(56),
        cost_estimate=pl.CostEstimate(
            flops=2 * tokens * width * (width + 3 * ff), bytes_accessed=96 * MIB, transcendentals=0
        ),
    )(
        as_table(offsets), cot, output, low, stat, query_feat, dpool, gate_up, attended, lse, gain1, gain2, heads, *pieces,
    )


def flipped(block, axis, bit):
    route = [(i, i ^ bit) for i in range(lax.axis_size(axis))]
    return lax.ppermute(block, axis, route)


def bits_of(axis):
    size, bit = lax.axis_size(axis), 1
    while bit < size:
        yield bit
        bit *= 2


def summed_everywhere(value):
    for axis in ("fsdp", "blk"):
        for bit in bits_of(axis):
            value = value + flipped(value, axis, bit)
    return value


def contrast(sums, lengths, pairing, row_mode, row_ids):
    rows, segs, width = sums.shape
    lengths = lengths.astype(F32)[..., None]
    pooled = sums / lengths
    inverse = lax.rsqrt(jnp.sum(pooled * pooled, -1, keepdims=True) + EMB_EPSILON)
    embedded = pooled * inverse
    own = rows * segs
    pair = jnp.stack([pairing, jnp.zeros_like(pairing)], axis=-1).reshape(own, 1)
    spare = jnp.concatenate([pair // 128, pair % 128, jnp.zeros((own, 126), jnp.int32)], axis=1)
    buffer = jnp.concatenate([embedded.reshape(own, width).astype(BF), spare.astype(BF)], axis=1)
    ids = row_ids
    for axis in ("fsdp", "blk") if row_mode else ("blk",):
        for bit in bits_of(axis):
            buffer = jnp.concatenate([buffer, flipped(buffer, axis, bit)], axis=0)
            if axis == "fsdp":
                ids = jnp.concatenate([ids, ids ^ bit])
            else:
                ids = jnp.concatenate([ids, ids ^ (bit * ROWS_PER_BLOCK)])
    total = buffer.shape[0]
    every = buffer[:, :width]
    pair_all = (buffer[:, width].astype(jnp.int32) * 128 + buffer[:, width + 1].astype(jnp.int32))[:, None]
    seg = jnp.arange(total, dtype=jnp.int32) % segs
    number = jnp.repeat(ids, segs, total_repeat_length=total) * (segs // 2) + seg // 2
    is_query = (seg % 2 == 0)[:, None]
    is_doc = (seg % 2 == 1)[None, :]
    target = is_query & is_doc & (pair_all == number[None, :])
    sims = dot_bt(every, every) / SOFTMAX_WARMTH
    masked = jnp.where(is_doc, sims, NEGATIVE)
    best = jnp.max(masked, -1, keepdims=True)
    log_total = best + jnp.log(jnp.sum(jnp.exp(masked - best), -1, keepdims=True))
    positive = jnp.sum(jnp.where(target, sims, 0.0), -1, keepdims=True)
    loss = jnp.sum(jnp.where(is_query[:own], log_total[:own] - positive[:own], 0.0))
    d_sims = CONTRAST_WEIGHT * (jnp.exp(masked - log_total) - target.astype(F32))
    d_sims = jnp.where(is_query, d_sims, 0.0).astype(BF)
    grad = (dot(d_sims[:own], every) + dot_at(d_sims[:, :own], every)) / SOFTMAX_WARMTH
    grad = grad.reshape(rows, segs, width)
    along = jnp.sum(embedded * grad, -1, keepdims=True)
    return loss, inverse * (grad - embedded * along) / lengths


ROWS_PER_BLOCK = 2


def half_row(kept, moved, first):
    return jnp.concatenate([jnp.where(first, kept, moved), jnp.where(first, moved, kept)], axis=0)


def shards(
    tokens,
    cotangent,
    segments,
    doc_lengths,
    positions,
    pairing,
    qkv_weight,
    out_weight,
    swiglu_weight,
    down_weight,
    attn_gain,
    ffn_gain,
):
    rows_here, shard_len, width = tokens.shape
    split = lax.axis_size("fsdp")
    mine = lax.axis_index("fsdp")
    place = lax.axis_index("blk")
    row_len = shard_len * split
    row_mode = split == rows_here == 2
    swap = [(0, 1), (1, 0)]

    if row_mode:

        def to_rows(array):
            kept = lax.dynamic_index_in_dim(array, mine, 0, keepdims=False)
            moved = lax.dynamic_index_in_dim(array, 1 - mine, 0, keepdims=False)
            return half_row(kept, lax.ppermute(moved, "fsdp", swap), mine == 0)

        def to_shards(kept, moved):
            came = lax.ppermute(moved, "fsdp", swap).astype(kept.dtype)
            first = mine == 0
            return jnp.stack([jnp.where(first, kept, came), jnp.where(first, came, kept)])

        rows, per_row, query_start = 1, row_len, 0
        lengths = lax.dynamic_slice_in_dim(doc_lengths, mine, 1, 0)
        own_pairing = lax.dynamic_slice_in_dim(pairing.reshape(rows_here, -1), mine, 1, 0)
        row_ids = (place * rows_here + mine)[None]
    else:

        def to_rows(array):
            return array.reshape(-1, width)

        rows, per_row, query_start = rows_here, shard_len, mine * shard_len
        lengths, own_pairing = doc_lengths, pairing.reshape(rows_here, -1)
        row_ids = place * rows_here + jnp.arange(rows_here, dtype=jnp.int32)
    tokens_here = rows * per_row
    tile = 256

    order = jnp.arange(SEG, dtype=jnp.int32)
    ends = jnp.sum(jnp.where(order[None, :] <= order[:, None], lengths[:, None, :], 0), -1)
    starts = ends - lengths
    token = jnp.arange(row_len, dtype=jnp.int32)
    at = token[None, :, None]
    member = (at >= starts[:, None, :]) & (at < ends[:, None, :])
    first_of = jnp.max(jnp.where(at >= starts[:, None, :], starts[:, None, :], 0), -1)
    lane = jnp.arange(LANES, dtype=jnp.int32)
    frequency = ROPE_BASE ** (-2.0 * (lane % 32).astype(F32) / HDIM)
    angles = (token[None, :] - first_of).astype(F32)[..., None] * frequency
    cosine = jnp.cos(angles).reshape(-1, LANES)
    sine = (jnp.sin(angles) * jnp.where(lane % HDIM < 32, -1.0, 1.0)).reshape(-1, LANES)
    key_feat = jnp.where(member, 0.0, NEGATIVE)
    key_feat = jnp.concatenate([key_feat, jnp.ones((rows, row_len, 120), F32)], -1)
    key_feat = key_feat.astype(BF).reshape(-1, LANES)
    query_feat = jnp.pad(member.astype(BF), ((0, 0), (0, 0), (0, 120))).reshape(-1, LANES)

    def of_queries(table):
        if row_mode:
            return table
        table = table.reshape(rows, row_len, LANES)
        return lax.dynamic_slice_in_dim(table, query_start, per_row, 1).reshape(-1, LANES)

    tables_k = (cosine, sine)
    tables_q = (of_queries(cosine), of_queries(sine))
    query_feat = of_queries(query_feat)
    block_first = query_start + BQ * jnp.arange(per_row // BQ, dtype=jnp.int32)[None, :, None]
    low = jnp.max(jnp.where(block_first >= starts[:, None, :], starts[:, None, :], 0), -1)
    high = jnp.min(jnp.where(block_first + BQ - 1 < ends[:, None, :], ends[:, None, :], row_len), -1)
    low = low // LANES * LANES
    count = (high - low + BK - 1) // BK
    low = jnp.minimum(low, row_len - count * BK)
    spans = jnp.stack([low, count], axis=-1).reshape(-1).astype(jnp.int32)

    qkv = weight_pieces(qkv_weight, 0)
    x = to_rows(tokens)
    out_w, swiglu_w, down_w = lax.optimization_barrier((out_weight, swiglu_weight, down_weight, x))[:3]
    outer = weight_pieces(out_w, 0)
    swiglu = weight_pieces(swiglu_w, 0)
    down = weight_pieces(down_w, 0)
    gains = jnp.stack([attn_gain, ffn_gain])
    if row_mode:
        other = lax.ppermute(gains, "fsdp", swap)
        gains = jnp.where(mine == 0, jnp.concatenate([gains, other], 1), jnp.concatenate([other, gains], 1))
    else:
        gains = lax.all_gather(gains, "fsdp", axis=1, tiled=True)
    gain1, gain2 = gains[0:1].astype(F32), gains[1:2].astype(F32)

    query, key, value = project(x, *tables_q, qkv, tile)
    if row_mode:
        key_all, value_all = key, value
    else:

        def along_row(part):
            part = part.reshape(rows, per_row, width)
            return lax.all_gather(part, "fsdp", axis=1, tiled=True).reshape(-1, width)

        key_all, value_all = along_row(key), along_row(value)
    attended, lse = attend(query, key_all, value_all, key_feat, query_feat, spans, rows)
    cot = to_rows(lax.optimization_barrier((cotangent, query))[0])
    low_normed, stat, gate_up, output, sums = mix(
        attended, x, query_feat, gain1, gain2, (outer, swiglu, down), rows, tile
    )
    if not row_mode:
        sums = lax.psum(sums, "fsdp")
    loss, d_pool = contrast(sums, lengths, own_pairing, row_mode, row_ids)
    d_pool = jnp.pad(d_pool, ((0, 0), (0, LANES - SEG), (0, 0)))
    lse_columns = jnp.pad(lse.reshape(HEADS, tokens_here).T, ((0, 0), (0, LANES - HEADS)))
    d_ffn, hidden, d_gate_up, d_branch, d_attended, back_feat, gain1_part, gain2_part = mix_back(
        cot, output, low_normed, stat, query_feat, d_pool, gate_up, attended, lse_columns, gain1, gain2,
        (outer, swiglu, down), rows, tile,
    )
    down_part = dot_at(hidden, d_ffn).astype(BF)
    swiglu_part = dot_at(low_normed, d_gate_up).astype(BF)
    out_part = dot_at(attended, d_branch).astype(BF)
    if not row_mode:
        loss = loss / split
    small = jnp.concatenate([jnp.sum(gain1_part, 0), jnp.sum(gain2_part, 0), jnp.full((LANES,), loss)])
    small = summed_everywhere(small.reshape(-1, LANES))
    d_query, d_key, d_value = attend_back(
        query, d_attended, key_all, value_all, key_feat, back_feat, spans, tables_q, tables_k, rows
    )
    if not row_mode:

        def own_part(grad):
            grad = grad.reshape(rows, row_len, width)
            return lax.psum_scatter(grad, "fsdp", scatter_dimension=1, tiled=True).reshape(-1, width)

        d_key, d_value = own_part(d_key), own_part(d_value)
    grads_in = (d_branch, d_query, d_key, d_value, qkv)
    if row_mode:
        moved = input_grad_part(*grads_in, (1 - mine) * shard_len, shard_len, BF, tile)
        kept = input_grad_part(*grads_in, mine * shard_len, shard_len, F32, tile)
        input_grad = to_shards(kept, moved)
        halves = [lax.dynamic_slice_in_dim(output, h * shard_len, shard_len, 0) for h in (mine, 1 - mine)]
        layer_output = to_shards(*halves)
    else:
        input_grad = input_grad_part(*grads_in, 0, tokens_here, F32, tile).reshape(tokens.shape)
        layer_output = output.reshape(tokens.shape)
    qkv_part = jnp.concatenate([dot_at(x, g).astype(BF) for g in (d_query, d_key, d_value)], axis=1)

    def reduced(part):
        part = lax.psum_scatter(part, "fsdp", scatter_dimension=0, tiled=True)
        return lax.psum(part, "blk").astype(F32)

    small = small.reshape(-1)
    half = width // split
    gain1_grad = lax.dynamic_slice_in_dim(small, mine * half, half, 0)
    gain2_grad = lax.dynamic_slice_in_dim(small, width + mine * half, half, 0)
    queries = lax.axis_size("blk") * pairing.shape[0]
    return (
        small[2 * width] / queries,
        layer_output,
        input_grad,
        reduced(qkv_part),
        reduced(out_part),
        reduced(swiglu_part),
        reduced(down_part),
        gain1_grad,
        gain2_grad,
    )


def solution(mesh):
    in_specs = (
        P("blk", "fsdp", None),
        P("blk", "fsdp", None),
        P("blk", "fsdp"),
        P("blk", None),
        P("blk", "fsdp"),
        P("blk"),
        P("fsdp", None),
        P("fsdp", None),
        P("fsdp", None),
        P("fsdp", None),
        P("fsdp"),
        P("fsdp"),
    )
    out_specs = (
        P(),
        P("blk", "fsdp", None),
        P("blk", "fsdp", None),
        P("fsdp", None),
        P("fsdp", None),
        P("fsdp", None),
        P("fsdp", None),
        P("fsdp"),
        P("fsdp"),
    )
    return jax.shard_map(shards, mesh=mesh, in_specs=in_specs, out_specs=out_specs, check_vma=False)
```

```python
import functools
import math

import jax
import jax.numpy as jnp
from jax import lax
from jax.experimental import pallas as pl
from jax.experimental.pallas import tpu as pltpu
from jax.sharding import PartitionSpec as P

HEADS = 12
HDIM = 64
PAIRS = HEADS // 2
LANES = 128
SEG = 8

EPSILON = 1e-05
EMB_EPSILON = 1e-06
SOFTMAX_WARMTH = 0.05
ROPE_BASE = 1000.0
CONTRAST_WEIGHT = 512.0
NEGATIVE = -1e30

BF = jnp.bfloat16
F32 = jnp.float32
MIB = 1 << 20
CHEAP = pl.CostEstimate(flops=1024, bytes_accessed=1024, transcendentals=0)


def cost(flops):
    return pl.CostEstimate(flops=4 * flops, bytes_accessed=MIB, transcendentals=0)


def dot(a, b):
    return lax.dot_general(a, b, (((1,), (0,)), ((), ())), preferred_element_type=F32)


def dot_bt(a, b):
    return lax.dot_general(a, b, (((1,), (1,)), ((), ())), preferred_element_type=F32)


def dot_at(a, b):
    return lax.dot_general(a, b, (((0,), (0,)), ((), ())), preferred_element_type=F32)


def lane_iota(shape):
    return lax.broadcasted_iota(jnp.int32, shape, len(shape) - 1)


def halves_swapped(block):
    low = lane_iota(block.shape) % HDIM < HDIM // 2
    return jnp.where(low, pltpu.roll(block, LANES - 32, 1), pltpu.roll(block, 32, 1))


def flipped(block, axis, bit):
    route = [(i, i ^ bit) for i in range(lax.axis_size(axis))]
    return lax.ppermute(block, axis, route)


def take(array, index, dim):
    return lax.dynamic_index_in_dim(array, index, dim, keepdims=False)


class Weight:
    def __init__(self, pieces, offsets, shape):
        self.pieces, self.offsets, self.shape = pieces, offsets, shape


def whole_weight(weight):
    rows, cols = weight.shape
    shape = (rows * lax.axis_size("fsdp"), cols)
    return Weight([lax.all_gather(weight, "fsdp", axis=0, tiled=True)], [(0, 0)], shape)


def half_of(weight, shift):
    half = weight.shape[0] // 2
    return lax.dynamic_slice_in_dim(weight, lax.axis_index("blk") % 2 * half + shift, half, 0)


def from_halves(weight, first):
    rows, cols = weight.shape
    core, mine = lax.axis_index("blk") % 2, lax.axis_index("fsdp")
    second = flipped(first, "blk", 1)
    other = (1 - mine) * rows
    offsets = [
        (mine * rows, 0),
        (other + core * (rows // 2), 0),
        (other + (1 - core) * (rows // 2), 0),
    ]
    return Weight([weight, first, second], offsets, (2 * rows, cols))


def share_of(weight, shift=0):
    share = weight.shape[0] // lax.axis_size("blk")
    return lax.dynamic_slice_in_dim(weight, lax.axis_index("blk") * share + shift, share, 0)


def from_shares(weight, share):
    rows, cols = weight.shape
    mine = lax.axis_index("fsdp")
    other = lax.all_gather(share, "blk", axis=0, tiled=True)
    return Weight([weight, other], [(mine * rows, 0), ((1 - mine) * rows, 0)], (2 * rows, cols))


def as_table(offsets):
    return jnp.stack([jnp.asarray(v, jnp.int32) for pair in offsets for v in pair])


def weight_copies(table, base, pieces, whole, sems):
    copies = []
    for n, piece in enumerate(pieces):
        rows, cols = piece.shape
        row = pl.multiple_of(table[2 * (base + n)], 16)
        col = pl.multiple_of(table[2 * (base + n) + 1], LANES)
        copies.append(
            pltpu.make_async_copy(
                piece, whole.at[pl.ds(row, rows), pl.ds(col, cols)], sems.at[base + n]
            )
        )
    return copies


def grouped_copies(counts, table, pieces, wholes, sems):
    groups, base = [], 1
    for count, whole in zip(counts, wholes):
        groups.append(weight_copies(table, base, pieces[base - 1 : base - 1 + count], whole, sems))
        base += count
    return groups


def start_all(*groups):
    for group in groups:
        for copy in group:
            copy.start()


def wait_all(*groups):
    for group in groups:
        for copy in group:
            copy.wait()


def weight_operands(weights, lead, after=()):
    counts = [len(w.pieces) for w in weights] + [len(after)]
    pieces = [p for w in weights for p in w.pieces]
    table = as_table([lead] + [o for w in weights for o in w.offsets])
    scratch = [pltpu.VMEM(w.shape, BF) for w in weights]
    return counts, pieces + list(after), table, scratch + [pltpu.SemaphoreType.DMA((len(pieces) + 1,))]


def zero_after(array):
    return jnp.minimum(jnp.abs(array[(0,) * array.ndim].astype(F32)), 0.0).astype(jnp.int32)


ANY = pl.BlockSpec(memory_space=pl.ANY)


def params(limit_mib):
    return pltpu.CompilerParams(vmem_limit_bytes=limit_mib * MIB)


def tied_kernel(*refs):
    del refs


def tied(values, after=()):
    if len(values) + len(after) < 2:
        return list(values)
    return pl.pallas_call(
        tied_kernel,
        in_specs=[ANY] * (len(values) + len(after)),
        out_specs=[ANY] * len(values),
        out_shape=[jax.ShapeDtypeStruct(v.shape, v.dtype) for v in values],
        input_output_aliases={n: n for n in range(len(values))},
        cost_estimate=CHEAP,
    )(*values, *after)


def row_specs(parts, tile, width, steps):
    if len(parts) == 1:
        return [pl.BlockSpec((tile, width), lambda r, i, *_: (r * steps + i, 0))]
    half = steps // 2

    def kept(r, i, t):
        return jnp.where(i // half == t[0], i % half, jnp.where(t[0] == 0, half - 1, 0)), 0

    def moved(r, i, t):
        return jnp.where(i // half != t[0], i % half, jnp.where(t[0] == 0, 0, half - 1)), 0

    return [pl.BlockSpec((tile, width), kept), pl.BlockSpec((tile, width), moved)]


def row_tile(table, refs):
    if len(refs) == 1:
        return refs[0][...]
    own = pl.program_id(1) // (pl.num_programs(1) // 2) == table[0]
    return jnp.where(own, refs[0][...], refs[1][...])


def qkv_kernel(counts, old, table, cos_ref, sin_ref, in_ref, *rest):
    pieces, rest = rest[: sum(counts)], rest[sum(counts) + old :]
    q_ref, k_ref, v_ref, x_ref, whole, sems = rest
    width = q_ref.shape[1]

    @pl.when(pl.program_id(0) == 0)
    def _():
        groups = grouped_copies(counts, table, pieces, [whole], sems)
        start_all(*groups)
        wait_all(*groups)

    x = in_ref[...]
    x_ref[...] = x
    cosine, sine = cos_ref[...], sin_ref[...]
    for ref, start, factor in ((q_ref, 0, 1.0 / math.sqrt(HDIM)), (k_ref, width, 1.0)):
        projected = dot(x, whole[:, start : start + width])
        for b in range(0, width, LANES):
            block = projected[:, b : b + LANES]
            turned = block * cosine + halves_swapped(block) * sine
            ref[:, b : b + LANES] = turned.astype(BF) * jnp.asarray(factor, BF)
    v_ref[...] = dot(x, whole[:, 2 * width :]).astype(BF)


def project(x, start, cosine, sine, weight, old, tile, after=()):
    tokens, width = cosine.shape[0], weight.shape[0]
    counts, pieces, table, scratch = weight_operands([weight], (start // tile, 0), after)
    shifted = lambda i, t: (i + t[0], 0)
    narrow, wide = pl.BlockSpec((tile, LANES), shifted), pl.BlockSpec((tile, width), shifted)
    first = 4 + len(pieces)
    return pl.pallas_call(
        functools.partial(qkv_kernel, counts, len(old)),
        grid_spec=pltpu.PrefetchScalarGridSpec(
            num_scalar_prefetch=1,
            grid=(x.shape[0] // tile,),
            in_specs=[narrow, narrow, pl.BlockSpec((tile, width), lambda i, t: (i, 0))] + [ANY] * (len(pieces) + len(old)),
            out_specs=[wide] * 4,
            scratch_shapes=scratch,
        ),
        out_shape=[jax.ShapeDtypeStruct((tokens, width), BF)] * 4,
        input_output_aliases={first + n: n for n in range(len(old))},
        compiler_params=params(48),
        cost_estimate=cost(6 * x.shape[0] * width * width),
    )(table, cosine, sine, x, *pieces, *old)


def input_grad_kernel(counts, groups, table, dbr_ref, *rest):
    grads, rest = rest[: 3 * groups], rest[3 * groups :]
    pieces, (out_ref, whole, sems) = rest[: sum(counts)], rest[sum(counts) :]
    width = dbr_ref.shape[1]

    @pl.when(pl.program_id(0) == 0)
    def _():
        copies = grouped_copies(counts, table, pieces, [whole], sems)
        start_all(*copies)
        wait_all(*copies)

    total = dbr_ref[...].astype(F32)
    for n, ref in enumerate(grads):
        wide = ref.shape[1]
        start = n % 3 * width + n // 3 * wide
        total += dot_bt(ref[...], whole[:, start : start + wide])
    out_ref[...] = total.astype(out_ref.dtype)


def input_grad_part(dbr, grads, weight, start, tokens, dtype, tile, after=()):
    width = dbr.shape[1]
    counts, pieces, table, scratch = weight_operands([weight], (start // tile, 0), after)
    shifted = lambda i, t: (i + t[0], 0)
    return pl.pallas_call(
        functools.partial(input_grad_kernel, counts, len(grads) // 3),
        grid_spec=pltpu.PrefetchScalarGridSpec(
            num_scalar_prefetch=1,
            grid=(tokens // tile,),
            in_specs=[pl.BlockSpec((tile, width), shifted)]
            + [pl.BlockSpec((tile, g.shape[1]), shifted) for g in grads]
            + [ANY] * len(pieces),
            out_specs=pl.BlockSpec((tile, width), lambda i, t: (i, 0)),
            scratch_shapes=scratch,
        ),
        out_shape=jax.ShapeDtypeStruct((tokens, width), dtype),
        compiler_params=params(48),
        cost_estimate=cost(6 * tokens * width * width),
    )(table, dbr, *grads, *pieces)


BQ = 256
BK_FWD = 512
BK_BACK = 256
VROWS = HDIM + 16


def spread_pairs(whole, source, features, group):
    for g in range(group):
        whole[:, 2 * g * LANES : (2 * g + 1) * LANES] = source[:, g * LANES : (g + 1) * LANES]
        whole[:, (2 * g + 1) * LANES : (2 * g + 2) * LANES] = features[...]


def staggered(count, load, work, finish):
    loaded, worked = load(0), None
    for g in range(count):
        ahead = load(g + 1) if g + 1 < count else None
        result = work(g, loaded)
        if worked is not None:
            finish(g - 1, worked)
        worked, loaded = result, ahead
    finish(count - 1, worked)


def attend_kernel(group, extra, spans, q_ref, k_ref, v_ref, kf_ref, qf_ref, *rest):
    o_ref, lse_ref, kx, vt, qx, best, accum = rest[extra:]
    block = pl.program_id(2)
    where = (pl.program_id(0) * pl.num_programs(2) + block) * 2
    row_len = k_ref.shape[0]

    @pl.when(block == 0)
    def _():
        spread_pairs(kx, k_ref, kf_ref, group)
        for g in range(group):
            for b in range(0, row_len, 256):
                turned = v_ref[b : b + 256, g * LANES : (g + 1) * LANES].astype(F32).T.astype(BF)
                for h in range(2):
                    vt[2 * g + h, :HDIM, b : b + 256] = turned[h * HDIM : (h + 1) * HDIM]
                    vt[2 * g + h, HDIM:, b : b + 256] = jnp.ones((16, 256), BF)

    qf = qf_ref[...]
    even = lane_iota(qf.shape) < HDIM
    zero = jnp.zeros_like(qf)
    for g in range(group):
        q = q_ref[:, g * LANES : (g + 1) * LANES]
        qx[g, :BQ, :LANES] = jnp.where(even, q, zero)
        qx[g, BQ:, :LANES] = jnp.where(even, zero, q)
        qx[g, :BQ, LANES:] = qf
        qx[g, BQ:, LANES:] = qf
    best[...] = jnp.full_like(best, NEGATIVE)
    accum[...] = jnp.zeros_like(accum)
    first, count = spans[where], spans[where + 1]

    def step(j, state):
        at = pl.multiple_of(first + j * BK_FWD, LANES)

        def load(g):
            return dot_bt(kx[pl.ds(at, BK_FWD), 2 * g * LANES : 2 * (g + 1) * LANES], qx[g])

        def work(g, scores):
            old = best[g]
            new = jnp.maximum(old, jnp.max(scores, axis=0, keepdims=True))
            best[g] = new
            return jnp.exp(scores - new).astype(BF), jnp.exp(old - new)

        def finish(g, worked):
            soft, factor = worked
            for h in range(2):
                cols = slice(h * BQ, (h + 1) * BQ)
                values = vt[2 * g + h, :, pl.ds(at, BK_FWD)]
                accum[g, :, cols] = accum[g, :, cols] * factor[:, cols] + dot(values, soft[:, cols])

        staggered(group, load, work, finish)
        return state

    lax.fori_loop(0, count, step, 0)
    for g in range(group):
        total = accum[g, HDIM : HDIM + 1]
        lse = best[g] + jnp.log(total)
        lse_ref[2 * g] = lse[:, :BQ]
        lse_ref[2 * g + 1] = lse[:, BQ:]
        turned = accum[g, :HDIM] / total
        turned = jnp.concatenate([turned[:, :BQ], turned[:, BQ:]], axis=0)
        o_ref[:, g * LANES : (g + 1) * LANES] = turned.T.astype(BF)


def attend(q, k, v, key_feat, query_feat, spans, rows, group, after=()):
    tokens, width = q.shape
    row_len = k.shape[0] // rows
    blocks = tokens // rows // BQ
    of_q = lambda r, p, i, *_: (r * blocks + i, p)
    of_k = lambda r, p, i, *_: (r, p)
    wide = group * LANES
    return pl.pallas_call(
        functools.partial(attend_kernel, group, len(after)),
        grid_spec=pltpu.PrefetchScalarGridSpec(
            num_scalar_prefetch=1,
            grid=(rows, PAIRS // group, blocks),
            in_specs=[
                pl.BlockSpec((BQ, wide), of_q),
                pl.BlockSpec((row_len, wide), of_k),
                pl.BlockSpec((row_len, wide), of_k),
                pl.BlockSpec((row_len, LANES), lambda r, p, i, *_: (r, 0)),
                pl.BlockSpec((BQ, LANES), lambda r, p, i, *_: (r * blocks + i, 0)),
            ]
            + [ANY] * len(after),
            out_specs=[
                pl.BlockSpec((BQ, wide), of_q),
                pl.BlockSpec((2 * group, 1, BQ), lambda r, p, i, *_: (p, 0, r * blocks + i)),
            ],
            scratch_shapes=[
                pltpu.VMEM((row_len, 2 * wide), BF),
                pltpu.VMEM((2 * group, VROWS, row_len), BF),
                pltpu.VMEM((group, 2 * BQ, 2 * LANES), BF),
                pltpu.VMEM((group, 1, 2 * BQ), F32),
                pltpu.VMEM((group, VROWS, 2 * BQ), F32),
            ],
        ),
        out_shape=[
            jax.ShapeDtypeStruct((tokens, width), BF),
            jax.ShapeDtypeStruct((HEADS, 1, tokens), F32),
        ],
        compiler_params=params(56),
        cost_estimate=cost(4 * tokens * row_len * width),
    )(spans, q, k, v, key_feat, query_feat, *after)


def attend_back_kernel(
    group, base, extra, spans, q_ref, do_ref, k_ref, v_ref, kf_ref, qf_ref, cq_ref, sq_ref, ck_ref, sk_ref, *rest,
):
    dq_ref, dk_ref, dv_ref, kx, vx, kt, qx, dox, dq_acc, dk_acc, dv_acc = rest[extra:]
    block = pl.program_id(2)
    pair = base + pl.program_id(1) * group
    where = (pl.program_id(0) * pl.num_programs(2) + block) * 2
    row_len = k_ref.shape[0]

    @pl.when(block == 0)
    def _():
        spread_pairs(kx, k_ref, kf_ref, group)
        spread_pairs(vx, v_ref, kf_ref, group)
        for g in range(group):
            for b in range(0, row_len, 256):
                turned = k_ref[b : b + 256, g * LANES : (g + 1) * LANES].astype(F32).T.astype(BF)
                kt[g * LANES : (g + 1) * LANES, b : b + 256] = turned
        dk_acc[...] = jnp.zeros_like(dk_acc)
        dv_acc[...] = jnp.zeros_like(dv_acc)

    qf = qf_ref[...]
    lanes = lane_iota(qf.shape)
    even = lanes < HDIM
    zero = jnp.zeros_like(qf)
    for g in range(group):
        cols = slice(g * LANES, (g + 1) * LANES)
        for whole, source in ((qx, q_ref[:, cols]), (dox, do_ref[:, cols])):
            whole[g, :BQ, :LANES] = jnp.where(even, source, zero)
            whole[g, BQ:, :LANES] = jnp.where(even, zero, source)
        for h in range(2):
            lane = lanes - (2 * (pair + g) + h)
            of_lse = (lanes < SEG) | (lane == 8) | (lane == 20) | (lane == 32)
            of_delta = (lane == 44) | (lane == 56) | (lane == 68)
            qx[g, h * BQ : (h + 1) * BQ, LANES:] = jnp.where(of_lse, qf, zero)
            dox[g, h * BQ : (h + 1) * BQ, LANES:] = jnp.where(of_delta, qf, zero)
    dq_acc[...] = jnp.zeros_like(dq_acc)
    first, count = spans[where], spans[where + 1]

    def step(j, state):
        at = pl.multiple_of(first + j * BK_BACK, LANES)

        def load(g):
            twice = slice(2 * g * LANES, (2 * g + 2) * LANES)
            return dot_bt(kx[pl.ds(at, BK_BACK), twice], qx[g]), dot_bt(vx[pl.ds(at, BK_BACK), twice], dox[g])

        def work(g, loaded):
            probs = jnp.exp(loaded[0])
            return probs.astype(BF), (probs * loaded[1]).astype(BF)

        def finish(g, worked):
            probs, grad = worked
            cols = slice(g * LANES, (g + 1) * LANES)
            dv_acc[pl.ds(at, BK_BACK), cols] += dot(probs, dox[g, :, :LANES])
            dk_acc[pl.ds(at, BK_BACK), cols] += dot(grad, qx[g, :, :LANES])
            for h in range(2):
                rows = slice(g * LANES + h * HDIM, g * LANES + (h + 1) * HDIM)
                dq_acc[rows] += dot(kt[rows, pl.ds(at, BK_BACK)], grad[:, h * BQ : (h + 1) * BQ])

        staggered(group, load, work, finish)
        return state

    lax.fori_loop(0, count, step, 0)
    for g in range(group):
        cols = slice(g * LANES, (g + 1) * LANES)
        dq = dq_acc[cols].T * (1.0 / math.sqrt(HDIM))
        dq_ref[:, cols] = (dq * cq_ref[...] - halves_swapped(dq) * sq_ref[...]).astype(BF)

    @pl.when(block == pl.num_programs(2) - 1)
    def _():
        for b in range(0, row_len, 256):
            part = pl.ds(b, 256)
            cosine, sine = ck_ref[part, :], sk_ref[part, :]
            for g in range(group):
                cols = slice(g * LANES, (g + 1) * LANES)
                dk = dk_acc[part, cols]
                dk_ref[part, cols] = (dk * cosine - halves_swapped(dk) * sine).astype(BF)
            dv_ref[part, :] = dv_acc[part, :].astype(BF)


def attend_back(q, do, k, v, key_feat, query_feat, spans, tables_q, tables_k, rows, group, base, pairs, after=()):
    tokens, width = q.shape
    row_len = k.shape[0] // rows
    blocks = tokens // rows // BQ
    start = base // group
    of_q = lambda r, p, i, *_: (r * blocks + i, start + p)
    of_k = lambda r, p, i, *_: (r, start + p)
    per_q = pl.BlockSpec((BQ, LANES), lambda r, p, i, *_: (r * blocks + i, 0))
    per_k = pl.BlockSpec((row_len, LANES), lambda r, p, i, *_: (r, 0))
    wide = group * LANES
    return pl.pallas_call(
        functools.partial(attend_back_kernel, group, base, len(after)),
        grid_spec=pltpu.PrefetchScalarGridSpec(
            num_scalar_prefetch=1,
            grid=(rows, pairs // group, blocks),
            in_specs=[
                pl.BlockSpec((BQ, wide), of_q),
                pl.BlockSpec((BQ, wide), of_q),
                pl.BlockSpec((row_len, wide), of_k),
                pl.BlockSpec((row_len, wide), of_k),
                per_k,
                per_q,
                per_q,
                per_q,
                per_k,
                per_k,
            ]
            + [ANY] * len(after),
            out_specs=[
                pl.BlockSpec((BQ, wide), lambda r, p, i, *_: (r * blocks + i, p)),
                pl.BlockSpec((row_len, wide), lambda r, p, i, *_: (r, p)),
                pl.BlockSpec((row_len, wide), lambda r, p, i, *_: (r, p)),
            ],
            scratch_shapes=[
                pltpu.VMEM((row_len, 2 * wide), BF),
                pltpu.VMEM((row_len, 2 * wide), BF),
                pltpu.VMEM((wide, row_len), BF),
                pltpu.VMEM((group, 2 * BQ, 2 * LANES), BF),
                pltpu.VMEM((group, 2 * BQ, 2 * LANES), BF),
                pltpu.VMEM((wide, BQ), F32),
                pltpu.VMEM((row_len, wide), F32),
                pltpu.VMEM((row_len, wide), F32),
            ],
        ),
        out_shape=[
            jax.ShapeDtypeStruct((tokens, pairs * LANES), BF),
            jax.ShapeDtypeStruct((rows * row_len, pairs * LANES), BF),
            jax.ShapeDtypeStruct((rows * row_len, pairs * LANES), BF),
        ],
        compiler_params=params(56),
        cost_estimate=cost(8 * tokens * row_len * pairs * LANES),
    )(spans, q, do, k, v, key_feat, query_feat, *tables_q, *tables_k, *after)


FF_CHUNK = 512


def normalize(hidden):
    average = jnp.mean(hidden, -1, keepdims=True)
    centred = hidden - average
    inverse = lax.rsqrt(jnp.mean(centred * centred, -1, keepdims=True) + EPSILON)
    return centred * inverse, inverse


def norm_back(scaled, normalized, inverse):
    return inverse * (
        scaled
        - jnp.mean(scaled, -1, keepdims=True)
        - normalized * jnp.mean(scaled * normalized, -1, keepdims=True)
    )


def split_two(value):
    high = value.astype(BF)
    return high, (value - high.astype(F32)).astype(BF)


def mix_kernel(counts, table, att_ref, x_ref, qf_ref, g1_ref, g2_ref, *rest):
    pieces, rest = rest[: sum(counts)], rest[sum(counts) :]
    nl_ref, stat_ref, hid_ref, fg_ref, fu_ref, out_ref, pool_ref, wo, ws, wd, sems = rest
    groups = grouped_copies(counts, table, pieces, (wo, ws, wd), sems)
    step, begin = pl.program_id(1), (pl.program_id(0) == 0) & (pl.program_id(1) == 0)

    @pl.when(begin)
    def _():
        start_all(*groups)
        wait_all(groups[0])

    branch = dot(att_ref[...], wo[...])
    unit, inverse1 = normalize(x_ref[...].astype(F32) + branch)
    normed = unit * g1_ref[...]
    low = normed.astype(BF)
    nl_ref[...] = low

    @pl.when(begin)
    def _():
        wait_all(*groups[1:])

    ff = wd.shape[0]
    hidden_sum = [normed]

    def load(c):
        cols = slice(c * FF_CHUNK, (c + 1) * FF_CHUNK)
        return dot(low, ws[:, cols]), dot(low, ws[:, ff + c * FF_CHUNK : ff + (c + 1) * FF_CHUNK])

    def work(c, loaded):
        cols = slice(c * FF_CHUNK, (c + 1) * FF_CHUNK)
        gate, up = loaded
        sig = 0.5 + 0.5 * jnp.tanh(0.5 * gate)
        silu = gate * sig
        hidden = (silu * up).astype(BF)
        hid_ref[:, cols] = hidden
        fg_ref[:, cols] = (up * (sig + silu * (1.0 - sig))).astype(BF)
        fu_ref[:, cols] = silu.astype(BF)
        return hidden

    def finish(c, hidden):
        hidden_sum[0] = hidden_sum[0] + dot(hidden, wd[c * FF_CHUNK : (c + 1) * FF_CHUNK, :])

    staggered(ff // FF_CHUNK, load, work, finish)
    unit2, inverse2 = normalize(hidden_sum[0])
    output = unit2 * g2_ref[...]
    out_ref[...] = output.astype(BF)
    lanes = lane_iota(stat_ref.shape)
    stat_ref[...] = jnp.where(lanes == 0, inverse1, inverse2)
    high, rest_low = split_two(output)
    member = qf_ref[...]
    sums = (dot_at(member, high) + dot_at(member, rest_low))[:SEG]

    @pl.when(step == 0)
    def _():
        pool_ref[0] = sums

    @pl.when(step > 0)
    def _():
        pool_ref[0] += sums


def mix(attended, x, query_feat, gain1, gain2, weights, rows, tile, after):
    tokens, width = x.shape
    steps = tokens // rows // tile
    ff = weights[2].shape[0]
    counts, pieces, table, scratch = weight_operands(weights, (0, 0), after)
    wide, narrow = row_specs([None], tile, width, steps), row_specs([None], tile, LANES, steps)
    hidden, fixed = row_specs([None], tile, ff, steps), [pl.BlockSpec((1, width), lambda r, i, *_: (0, 0))]
    return pl.pallas_call(
        functools.partial(mix_kernel, counts),
        grid_spec=pltpu.PrefetchScalarGridSpec(
            num_scalar_prefetch=1,
            grid=(rows, steps),
            in_specs=wide * 2 + narrow + fixed * 2 + [ANY] * len(pieces),
            out_specs=wide + narrow + hidden * 3 + wide + [pl.BlockSpec((1, SEG, width), lambda r, i, *_: (r, 0, 0))],
            scratch_shapes=scratch,
        ),
        out_shape=[
            jax.ShapeDtypeStruct((tokens, width), BF),
            jax.ShapeDtypeStruct((tokens, LANES), F32),
            jax.ShapeDtypeStruct((tokens, ff), BF),
            jax.ShapeDtypeStruct((tokens, ff), BF),
            jax.ShapeDtypeStruct((tokens, ff), BF),
            jax.ShapeDtypeStruct((tokens, width), BF),
            jax.ShapeDtypeStruct((rows, SEG, width), F32),
        ],
        compiler_params=params(58),
        cost_estimate=cost(2 * tokens * width * (width + 3 * ff)),
    )(table, attended, x, query_feat, gain1, gain2, *pieces)


def hidden_back_kernel(counts, parts, table, *rest):
    cot_refs, rest = rest[:parts], rest[parts:]
    out_ref, stat_ref, qf_ref, dp_ref, fg_ref, fu_ref, g2_ref = rest[:7]
    pieces, rest = rest[7 : 7 + sum(counts)], rest[7 + sum(counts) :]
    dffn_ref, dgate_ref, dup_ref, gf_ref, wd, sems = rest
    groups = grouped_copies(counts, table, pieces, [wd], sems)
    begin = (pl.program_id(0) == 0) & (pl.program_id(1) == 0)

    @pl.when(begin)
    def _():
        start_all(*groups)
        gf_ref[...] = jnp.zeros_like(gf_ref)

    inverse2 = stat_ref[:, 1:2]
    member = qf_ref[...]
    high, rest_low = split_two(dp_ref[0])
    upstream = row_tile(table, cot_refs).astype(F32) + dot(member, high) + dot(member, rest_low)
    gain2 = g2_ref[...]
    unit2 = out_ref[...].astype(F32) / gain2
    dffn = norm_back(upstream * gain2, unit2, inverse2).astype(BF)
    dffn_ref[...] = dffn
    tile, width = dffn.shape
    gf_ref[...] += jnp.sum((upstream * unit2).reshape(tile // 8, 8, width), axis=0)

    @pl.when(begin)
    def _():
        wait_all(*groups)

    def load(c):
        return dot_bt(dffn, wd[c * FF_CHUNK : (c + 1) * FF_CHUNK, :])

    def work(c, dhid):
        cols = slice(c * FF_CHUNK, (c + 1) * FF_CHUNK)
        dgate_ref[:, cols] = (dhid * fg_ref[:, cols].astype(F32)).astype(BF)
        dup_ref[:, cols] = (dhid * fu_ref[:, cols].astype(F32)).astype(BF)

    staggered(wd.shape[0] // FF_CHUNK, load, work, lambda c, worked: None)


def hidden_back(cots, lead, output, stat, query_feat, dpool, factors, gain2, down, rows, tile):
    tokens, width = output.shape
    ff = down.shape[0]
    steps = tokens // rows // tile
    counts, pieces, table, scratch = weight_operands([down], (lead, 0))
    wide, narrow = row_specs([None], tile, width, steps), row_specs([None], tile, LANES, steps)
    hidden = row_specs([None], tile, ff, steps)
    return pl.pallas_call(
        functools.partial(hidden_back_kernel, counts, len(cots)),
        grid_spec=pltpu.PrefetchScalarGridSpec(
            num_scalar_prefetch=1,
            grid=(rows, steps),
            in_specs=row_specs(cots, tile, width, steps)
            + wide
            + narrow * 2
            + [pl.BlockSpec((1, LANES, width), lambda r, i, *_: (r, 0, 0))]
            + hidden * 2
            + [pl.BlockSpec((1, width), lambda r, i, *_: (0, 0))]
            + [ANY] * len(pieces),
            out_specs=wide + hidden * 2 + [pl.BlockSpec((8, width), lambda r, i, *_: (0, 0))],
            scratch_shapes=scratch,
        ),
        out_shape=[
            jax.ShapeDtypeStruct((tokens, width), BF),
            jax.ShapeDtypeStruct((tokens, ff), BF),
            jax.ShapeDtypeStruct((tokens, ff), BF),
            jax.ShapeDtypeStruct((8, width), F32),
        ],
        compiler_params=params(58),
        cost_estimate=cost(4 * tokens * width * ff),
    )(table, *cots, output, stat, query_feat, dpool, *factors, gain2, *pieces)


def branch_back_kernel(counts, table, *refs):
    dffn_ref, nl_ref, stat_ref, qf_ref, dgate_ref, dup_ref, att_ref, lse_ref, g1_ref, head_ref = refs[:10]
    rest = refs[10:]
    pieces, rest = rest[: sum(counts)], rest[sum(counts) :]
    dbr_ref, datt_ref, feat_ref, ga_ref, wo, ws, sems = rest
    groups = grouped_copies(counts, table, pieces, (wo, ws), sems)
    begin = (pl.program_id(0) == 0) & (pl.program_id(1) == 0)

    @pl.when(begin)
    def _():
        start_all(*groups)
        ga_ref[...] = jnp.zeros_like(ga_ref)
        wait_all(*groups)

    ff = dgate_ref.shape[1]
    dnormed = dffn_ref[...].astype(F32) + dot_bt(dgate_ref[...], ws[:, :ff]) + dot_bt(dup_ref[...], ws[:, ff:])
    gain1 = g1_ref[...]
    unit1 = nl_ref[...].astype(F32) / gain1
    dbr = norm_back(dnormed * gain1, unit1, stat_ref[:, 0:1]).astype(BF)
    dbr_ref[...] = dbr
    datt = dot_bt(dbr, wo[...]).astype(BF)
    datt_ref[...] = datt
    tile, width = datt.shape
    ga_ref[...] += jnp.sum((dnormed * unit1).reshape(tile // 8, 8, width), axis=0)

    high, rest_low = split_two(datt.astype(F32) * att_ref[...].astype(F32))
    heads = head_ref[...]
    delta = dot(high, heads) + dot(rest_low, heads)
    feat = qf_ref[...].astype(F32)
    for value, start in ((lse_ref[...], 8), (delta, 44)):
        left = -value
        for n in range(3):
            part = left.astype(BF).astype(F32)
            left = left - part
            feat = feat + pltpu.roll(part, start + HEADS * n, 1)
    feat_ref[...] = feat.astype(BF)


def branch_back(dffn, low, stat, query_feat, dgate, dup, attended, lse, gain1, weights, rows, tile, after=()):
    tokens, width = low.shape
    ff = dgate.shape[1]
    steps = tokens // rows // tile
    counts, pieces, table, scratch = weight_operands(weights, (0, 0), after)
    wide, narrow = row_specs([None], tile, width, steps), row_specs([None], tile, LANES, steps)
    hidden = row_specs([None], tile, ff, steps)
    heads = (jnp.arange(width)[:, None] // HDIM == jnp.arange(LANES)[None, :]).astype(BF)
    return pl.pallas_call(
        functools.partial(branch_back_kernel, counts),
        grid_spec=pltpu.PrefetchScalarGridSpec(
            num_scalar_prefetch=1,
            grid=(rows, steps),
            in_specs=wide * 2
            + narrow * 2
            + hidden * 2
            + wide
            + narrow
            + [pl.BlockSpec((1, width), lambda r, i, *_: (0, 0))]
            + [pl.BlockSpec((width, LANES), lambda r, i, *_: (0, 0))]
            + [ANY] * len(pieces),
            out_specs=wide * 2 + narrow + [pl.BlockSpec((8, width), lambda r, i, *_: (0, 0))],
            scratch_shapes=scratch,
        ),
        out_shape=[
            jax.ShapeDtypeStruct((tokens, width), BF),
            jax.ShapeDtypeStruct((tokens, width), BF),
            jax.ShapeDtypeStruct((tokens, LANES), BF),
            jax.ShapeDtypeStruct((8, width), F32),
        ],
        compiler_params=params(58),
        cost_estimate=cost(2 * tokens * width * (width + 2 * ff)),
    )(table, dffn, low, stat, query_feat, dgate, dup, attended, lse, gain1, heads, *pieces)


def bits_of(axis):
    size, bit = lax.axis_size(axis), 1
    while bit < size:
        yield bit
        bit *= 2


def in_order(parts, index):
    shape = (2,) + (1,) * parts[0].ndim
    first = lax.broadcasted_iota(jnp.int32, shape, 0) == index
    return jnp.where(first, parts[0][None], parts[1][None])


def add(first, *others):
    total = first.astype(F32)
    for other in others:
        total = total + other.astype(F32)
    return total.astype(BF)


def reduction(part, short):
    rows, cols = part.shape
    shards = lax.axis_size("fsdp")
    mine, place = lax.axis_index("fsdp"), lax.axis_index("blk")
    core, side = place % 2, place // 2 % 2
    now = part.reshape(shards, 2, rows // shards // 2, cols)
    (came,) = yield [take(now, 1 - core, 1)], [("blk", 1)]
    now = add(take(now, core, 1), came)
    bit = shards // 2
    while bit:
        now = now.reshape(2, bit, -1, cols)
        own = mine // bit % 2
        (came,) = yield [take(now, 1 - own, 0)], [("fsdp", bit)]
        now = add(take(now, own, 0), came)
        bit //= 2
    now = now.reshape(2, -1, cols)
    (came,) = yield [take(now, 1 - side, 0)], [("blk", 2)]
    now = add(take(now, side, 0), came)
    bits = [bit for bit in bits_of("blk") if bit > 2]
    if short:
        for bit in bits:
            (came,) = yield [now], [("blk", bit)]
            now = add(now, came)
    else:
        for bit in bits:
            now = now.reshape(2, -1, cols)
            own = place // bit % 2
            (came,) = yield [take(now, 1 - own, 0)], [("blk", bit)]
            now = add(take(now, own, 0), came)
        for bit in bits[::-1]:
            (came,) = yield [now], [("blk", bit)]
            now = in_order([now, came], place // bit % 2).reshape(-1, cols)
    now = now.reshape(-1, cols)
    (came,) = yield [now], [("blk", 2)]
    now = in_order([now, came], side).reshape(-1, cols)
    (came,) = yield [now], [("blk", 1)]
    yield [now, came], None


class Reduction:
    def __init__(self, part, short=False):
        self.stages = reduction(part, short)
        self.sends, self.routes = next(self.stages)

    @property
    def done(self):
        return self.routes is None

    @property
    def result(self):
        return self.sends

    def launch(self):
        came = [flipped(a, *route) for a, route in zip(self.sends, self.routes)]
        return self.sends, came

    def take_in(self, came):
        self.sends, self.routes = self.stages.send(came)


def beside(work, launches, joins=None):
    sent, flights = [], []
    for r in launches:
        if not r.done:
            sends, came = r.launch()
            sent += sends
            flights.append((r, came))
    values = list(work(sent))
    late = []
    if joins is not None:
        late = [f for f in flights if f[0] not in [j for j in joins if isinstance(j, Reduction)]]
        flights = [f for f in flights if f not in late] + [j for j in joins if not isinstance(j, Reduction)]
    count = len(values)
    both = tied(values + [a for _, came in flights for a in came])
    at = count
    for r, came in flights:
        r.take_in(both[at : at + len(came)])
        at += len(came)
    return both[:count], late


def reduced(part):
    part = lax.psum_scatter(part, ("fsdp", "blk"), scatter_dimension=0, tiled=True)
    return lax.all_gather(part, "blk", axis=0, tiled=True)


def weight_grad(pairs, beside_it=None):
    arrays, left = [], []
    for a, b in pairs:
        place = [n for n, other in enumerate(arrays) if other is a]
        if not place:
            arrays.append(a)
            place = [len(arrays) - 1]
        arrays.append(b)
        left.append((place[0], len(arrays) - 1))
    cols = sum(b.shape[1] for _, b in pairs)
    last = []
    if beside_it is not None:
        last = [beside_it]
        cols += beside_it.shape[1]

    def kernel(*refs):
        out_ref, at = refs[-1], 0
        for a, b in left:
            part = dot_at(refs[a][...], refs[b][...]).astype(BF)
            out_ref[:, at : at + part.shape[1]] = part
            at += part.shape[1]
        if last:
            out_ref[:, at:] = refs[-2][...]

    return pl.pallas_call(
        kernel,
        out_shape=jax.ShapeDtypeStruct((pairs[0][0].shape[1], cols), BF),
        compiler_params=params(56),
        cost_estimate=cost(2 * pairs[0][0].shape[0] * pairs[0][0].shape[1] * cols),
    )(*arrays, *last)


def unfold_kernel(columns, table, *refs):
    pairs = 2 * (1 + max(n for parts in columns for n, _, _ in parts))
    own = pl.program_id(0) == table[0]
    values = [jnp.where(own, refs[n][...], refs[n + 1][...]) for n in range(0, pairs, 2)]
    for ref, parts in zip(refs[pairs:], columns):
        at = 0
        for n, start, wide in parts:
            ref[:, at : at + wide] = values[n][:, start : start + wide].astype(F32)
            at += wide


def unfold(pairs, columns):
    rows = pairs[0][0].shape[0]
    block = rows // 2 if rows % 32 == 0 else rows
    steps = rows // block
    return pl.pallas_call(
        functools.partial(unfold_kernel, columns),
        grid_spec=pltpu.PrefetchScalarGridSpec(
            num_scalar_prefetch=1,
            grid=(2, steps),
            in_specs=[pl.BlockSpec((block, a.shape[1]), lambda c, i, t: (i, 0)) for pair in pairs for a in pair],
            out_specs=[pl.BlockSpec((block, sum(p[2] for p in parts)), lambda c, i, t: (c * steps + i, 0)) for parts in columns],
        ),
        out_shape=[jax.ShapeDtypeStruct((2 * rows, sum(p[2] for p in parts)), F32) for parts in columns],
        compiler_params=params(40),
        cost_estimate=CHEAP,
    )((lax.axis_index("blk") % 2).reshape(1), *[a for pair in pairs for a in pair])


def contrast(sums, lengths, pairing, row_mode, row_ids):
    rows, segs, width = sums.shape
    lengths = lengths.astype(F32)[..., None]
    pooled = sums / lengths
    inverse = lax.rsqrt(jnp.sum(pooled * pooled, -1, keepdims=True) + EMB_EPSILON)
    embedded = pooled * inverse
    own = rows * segs
    pair = jnp.stack([pairing, jnp.zeros_like(pairing)], axis=-1).reshape(own, 1)
    spare = jnp.concatenate([pair // 128, pair % 128, jnp.zeros((own, 126), jnp.int32)], axis=1)
    buffer = jnp.concatenate([embedded.reshape(own, width).astype(BF), spare.astype(BF)], axis=1)
    ids = row_ids
    for axis in ("fsdp", "blk") if row_mode else ("blk",):
        for bit in bits_of(axis):
            buffer = jnp.concatenate([buffer, flipped(buffer, axis, bit)], axis=0)
            if axis == "fsdp":
                ids = jnp.concatenate([ids, ids ^ bit])
            else:
                ids = jnp.concatenate([ids, ids ^ (bit * ROWS_PER_BLOCK)])
    total = buffer.shape[0]
    every = buffer[:, :width]
    pair_all = (buffer[:, width].astype(jnp.int32) * 128 + buffer[:, width + 1].astype(jnp.int32))[:, None]
    seg = jnp.arange(total, dtype=jnp.int32) % segs
    number = jnp.broadcast_to(ids[:, None], (total // segs, segs)).reshape(total) * (segs // 2) + seg // 2
    is_query = (seg % 2 == 0)[:, None]
    is_doc = (seg % 2 == 1)[None, :]
    target = is_query & is_doc & (pair_all == number[None, :])
    sims = dot_bt(every, every) / SOFTMAX_WARMTH
    masked = jnp.where(is_doc, sims, NEGATIVE)
    best = jnp.max(masked, -1, keepdims=True)
    log_total = best + jnp.log(jnp.sum(jnp.exp(masked - best), -1, keepdims=True))
    positive = jnp.sum(jnp.where(target, sims, 0.0), -1, keepdims=True)
    loss = jnp.sum(jnp.where(is_query[:own], log_total[:own] - positive[:own], 0.0))
    d_sims = CONTRAST_WEIGHT * (jnp.exp(masked - log_total) - target.astype(F32))
    d_sims = jnp.where(is_query, d_sims, 0.0).astype(BF)
    grad = (dot(d_sims[:own], every) + dot_at(d_sims[:, :own], every)) / SOFTMAX_WARMTH
    grad = grad.reshape(rows, segs, width)
    along = jnp.sum(embedded * grad, -1, keepdims=True)
    return loss, inverse * (grad - embedded * along) / lengths


ROWS_PER_BLOCK = 2


def shards(
    tokens,
    cotangent,
    segments,
    doc_lengths,
    positions,
    pairing,
    qkv_weight,
    out_weight,
    swiglu_weight,
    down_weight,
    attn_gain,
    ffn_gain,
):
    rows_here, shard_len, width = tokens.shape
    split = lax.axis_size("fsdp")
    mine = lax.axis_index("fsdp")
    place = lax.axis_index("blk")
    row_len = shard_len * split
    row_mode = split == rows_here == 2

    if row_mode:
        rows, per_row, query_start, lead = 1, row_len, 0, mine
        lengths = lax.dynamic_slice_in_dim(doc_lengths, mine, 1, 0)
        own_pairing = lax.dynamic_slice_in_dim(pairing.reshape(rows_here, -1), mine, 1, 0)
        row_ids = (place * rows_here + mine)[None]
    else:
        rows, per_row, query_start, lead = rows_here, shard_len, mine * shard_len, 0
        lengths, own_pairing = doc_lengths, pairing.reshape(rows_here, -1)
        row_ids = place * rows_here + jnp.arange(rows_here, dtype=jnp.int32)
    tokens_here = rows * per_row
    tile = min(512, per_row)
    small_tile = min(256, per_row)

    gains = jnp.stack([attn_gain, ffn_gain])
    if row_mode:
        qkv_share = flipped(share_of(qkv_weight), "fsdp", 1)
        qkv = from_shares(qkv_weight, qkv_share)
        moved = flipped(take(tokens, 1 - mine + zero_after(qkv_share), 0), "fsdp", 1)
        swiglu_share = flipped(share_of(swiglu_weight, zero_after(moved)), "fsdp", 1)
        swiglu = from_shares(swiglu_weight, swiglu_share)
        gains = in_order([gains, flipped(gains, "fsdp", 1)], mine)
        gains = jnp.concatenate([gains[0], gains[1]], axis=1)
    else:
        qkv, swiglu = whole_weight(qkv_weight), whole_weight(swiglu_weight)
        gains = lax.all_gather(gains, "fsdp", axis=1, tiled=True)
    gain1, gain2 = gains[0:1].astype(F32), gains[1:2].astype(F32)

    order = jnp.arange(SEG, dtype=jnp.int32)
    ends = jnp.sum(jnp.where(order[None, :] <= order[:, None], lengths[:, None, :], 0), -1)
    starts = ends - lengths
    token = jnp.arange(row_len, dtype=jnp.int32)
    at = token[None, :, None]
    member = (at >= starts[:, None, :]) & (at < ends[:, None, :])
    first_of = jnp.max(jnp.where(at >= starts[:, None, :], starts[:, None, :], 0), -1)
    lane = jnp.arange(LANES, dtype=jnp.int32)
    frequency = ROPE_BASE ** (-2.0 * (lane % 32).astype(F32) / HDIM)
    angles = (token[None, :] - first_of).astype(F32)[..., None] * frequency
    cosine = jnp.cos(angles).reshape(-1, LANES)
    sine = (jnp.sin(angles) * jnp.where(lane % HDIM < 32, -1.0, 1.0)).reshape(-1, LANES)
    key_feat = jnp.where(member, 0.0, NEGATIVE)
    key_feat = jnp.concatenate([key_feat, jnp.ones((rows, row_len, 120), F32)], -1)
    key_feat = key_feat.astype(BF).reshape(-1, LANES)
    query_feat = jnp.pad(member.astype(BF), ((0, 0), (0, 0), (0, 120))).reshape(-1, LANES)

    def of_queries(table):
        if row_mode:
            return table
        table = table.reshape(rows, row_len, LANES)
        return lax.dynamic_slice_in_dim(table, query_start, per_row, 1).reshape(-1, LANES)

    tables_k = (cosine, sine)
    tables_q = (of_queries(cosine), of_queries(sine))
    query_feat = of_queries(query_feat)
    block_first = query_start + BQ * jnp.arange(per_row // BQ, dtype=jnp.int32)[None, :, None]
    low = jnp.max(jnp.where(block_first >= starts[:, None, :], starts[:, None, :], 0), -1)
    high = jnp.min(jnp.where(block_first + BQ - 1 < ends[:, None, :], ends[:, None, :], row_len), -1)
    low = low // LANES * LANES

    def spans_of(size):
        count = (high - low + size - 1) // size
        return jnp.stack([jnp.minimum(low, row_len - count * size), count], axis=-1).reshape(-1).astype(jnp.int32)

    spans, spans_back = spans_of(BK_FWD), spans_of(BK_BACK)

    if row_mode:
        tables = (*tables_q, qkv)
        shift = zero_after(moved)
        halves = [half_of(w, shift) for w in (out_weight, down_weight)]
        firsts = [flipped(h, "fsdp", 1) for h in halves]
        query, key, value, x = project(take(tokens, mine, 0), mine * shard_len, *tables, [], small_tile, halves)
        old = [query, key, value, x]
        query, key, value, x = project(moved, (1 - mine) * shard_len, *tables, old, small_tile)
        key_all, value_all = key, value
    else:
        query, key, value, x = project(tokens.reshape(-1, width), 0, *tables_q, qkv, [], small_tile)

        def along_row(part):
            part = part.reshape(rows, per_row, width)
            return lax.all_gather(part, "fsdp", axis=1, tiled=True).reshape(-1, width)

        key_all, value_all = along_row(key), along_row(value)
    attended, lse = attend(query, key_all, value_all, key_feat, query_feat, spans, rows, PAIRS)
    if row_mode:
        attended, *firsts = tied([attended, *firsts], [lse])
        outer, down = from_halves(out_weight, firsts[0]), from_halves(down_weight, firsts[1])
        cot_send = take(cotangent, 1 - mine + zero_after(firsts[1]), 0)
        cots = [take(cotangent, mine, 0), flipped(cot_send, "fsdp", 1)]
        after = [cot_send]
    else:
        outer, down = whole_weight(out_weight), whole_weight(down_weight)
        cots, after = [cotangent.reshape(-1, width)], []
    low_normed, stat, hidden, *factors, output, sums = mix(
        attended, x, query_feat, gain1, gain2, (outer, swiglu, down), rows, small_tile, after
    )
    if row_mode:
        sums, cots[1] = tied([sums, cots[1]])
        output_came = flipped(lax.dynamic_slice_in_dim(output, (1 - mine) * shard_len, shard_len, 0), "fsdp", 1)
    else:
        layer_output = output.reshape(tokens.shape)
        sums = lax.psum(sums, "fsdp")
    loss, d_pool = contrast(sums, lengths, own_pairing, row_mode, row_ids)
    d_pool = jnp.pad(d_pool, ((0, 0), (0, LANES - SEG), (0, 0)))
    lse_columns = jnp.pad(lse.reshape(HEADS, tokens_here).T, ((0, 0), (0, LANES - HEADS)))

    d_ffn, d_gate, d_up, gain2_part = hidden_back(
        cots, lead, output, stat, query_feat, d_pool, factors, gain2, down, rows, small_tile
    )
    if row_mode:
        d_gate, output_came = tied([d_gate, output_came])
        layer_output = lax.dynamic_slice_in_dim(output, mine * shard_len, shard_len, 0)
        layer_output = in_order([layer_output, output_came], mine)
    down_rows = reduced(dot_at(hidden, d_ffn).astype(BF))
    gate_rows = reduced(dot_at(low_normed, d_gate).astype(BF))
    up_sum = Reduction(dot_at(low_normed, d_up).astype(BF))
    (d_branch, d_attended, back_feat, gain1_part), _ = beside(
        lambda sent: branch_back(
            d_ffn, low_normed, stat, query_feat, d_gate, d_up, attended, lse_columns, gain1, (outer, swiglu), rows,
            small_tile, sent,
        ),
        [up_sum],
    )
    part_rows = jnp.arange(width, dtype=jnp.int32) % (width // split)
    losses = jnp.where(part_rows == place, loss if row_mode else loss / split, 0.0)
    losses_high = lax.reduce_precision(losses, 8, 7)
    small = jnp.stack([jnp.sum(gain1_part, 0), jnp.sum(gain2_part, 0), losses_high, losses - losses_high], axis=1)
    small = jnp.pad(small, ((0, 0), (0, LANES - 4))).astype(BF)
    grads, qkv_sums = [], []
    running = [up_sum]
    for n in range(PAIRS // BACK_PAIRS):
        columns, _ = beside(
            lambda sent: attend_back(
                query, d_attended, key_all, value_all, key_feat, back_feat, spans_back, tables_q, tables_k, rows,
                BACK_PAIRS, n * BACK_PAIRS, BACK_PAIRS, sent,
            ),
            running,
        )
        if not row_mode:

            def own_part(grad):
                grad = grad.reshape(rows, row_len, -1)
                grad = lax.psum_scatter(grad, "fsdp", scatter_dimension=1, tiled=True)
                return grad.reshape(tokens_here, -1)

            columns = [columns[0], own_part(columns[1]), own_part(columns[2])]
        grads += columns
        pairs = [(x, g) for g in columns]
        if n == 0:
            qkv_sums.append(Reduction(weight_grad([*pairs, (attended, d_branch)], small), True))
        else:
            qkv_sums.append(Reduction(weight_grad(pairs), True))
        running = [up_sum, *qkv_sums]
    if row_mode:
        (moved,), _ = beside(
            lambda sent: [
                input_grad_part(d_branch, grads, qkv, (1 - mine) * shard_len, shard_len, BF, small_tile, sent)
            ],
            running,
        )
        came = flipped(moved, "fsdp", 1)
        (kept,), _ = beside(
            lambda sent: [input_grad_part(d_branch, grads, qkv, mine * shard_len, shard_len, F32, small_tile, sent)],
            running,
        )
        input_grad = in_order([kept, came.astype(F32)], mine)
    else:
        input_grad = input_grad_part(d_branch, grads, qkv, 0, tokens_here, F32, small_tile).reshape(tokens.shape)
    while any(not r.done for r in running):
        beside(lambda _: [], running)
    wide, groups = BACK_PAIRS * LANES, PAIRS // BACK_PAIRS
    ff = d_gate.shape[1]
    half = width // split // 2
    up_rows = in_order(up_sum.result, place % 2).reshape(2 * half, ff)
    swiglu_grad = jnp.concatenate([gate_rows, up_rows], axis=1).astype(F32)
    qkv_columns = [(g, part * wide, wide) for part in range(3) for g in range(groups)]
    qkv_grad, out_grad, small = unfold(
        [r.result for r in qkv_sums], [qkv_columns, [(0, 3 * wide, width)], [(0, 3 * wide + width, LANES)]]
    )
    queries = lax.axis_size("blk") * pairing.shape[0]
    return (
        jnp.sum(small[:, 2:4]) / queries,
        layer_output,
        input_grad,
        qkv_grad,
        out_grad,
        swiglu_grad,
        down_rows.astype(F32),
        small[:, 0],
        small[:, 1],
    )


BACK_PAIRS = 2


def solution(mesh):
    in_specs = (
        P("blk", "fsdp", None),
        P("blk", "fsdp", None),
        P("blk", "fsdp"),
        P("blk", None),
        P("blk", "fsdp"),
        P("blk"),
        P("fsdp", None),
        P("fsdp", None),
        P("fsdp", None),
        P("fsdp", None),
        P("fsdp"),
        P("fsdp"),
    )
    out_specs = (
        P(),
        P("blk", "fsdp", None),
        P("blk", "fsdp", None),
        P("fsdp", None),
        P("fsdp", None),
        P("fsdp", None),
        P("fsdp", None),
        P("fsdp"),
        P("fsdp"),
    )
    return jax.shard_map(shards, mesh=mesh, in_specs=in_specs, out_specs=out_specs, check_vma=False)
```

```python
import functools
import math

import jax
import jax.numpy as jnp
from jax import lax
from jax.experimental import pallas as pl
from jax.experimental.pallas import tpu as pltpu
from jax.sharding import PartitionSpec as P

HEADS = 12
HDIM = 64
PAIRS = HEADS // 2
LANES = 128
SEG = 8

EPSILON = 1e-05
EMB_EPSILON = 1e-06
SOFTMAX_WARMTH = 0.05
ROPE_BASE = 1000.0
CONTRAST_WEIGHT = 512.0
NEGATIVE = -1e30

BF = jnp.bfloat16
F32 = jnp.float32
MIB = 1 << 20
CHEAP = pl.CostEstimate(flops=1024, bytes_accessed=1024, transcendentals=0)


def cost(flops):
    return pl.CostEstimate(flops=4 * flops, bytes_accessed=MIB, transcendentals=0)


def dot(a, b):
    return lax.dot_general(a, b, (((1,), (0,)), ((), ())), preferred_element_type=F32)


def dot_bt(a, b):
    return lax.dot_general(a, b, (((1,), (1,)), ((), ())), preferred_element_type=F32)


def dot_at(a, b):
    return lax.dot_general(a, b, (((0,), (0,)), ((), ())), preferred_element_type=F32)


def lane_iota(shape):
    return lax.broadcasted_iota(jnp.int32, shape, len(shape) - 1)


def halves_swapped(block):
    low = lane_iota(block.shape) % HDIM < HDIM // 2
    return jnp.where(low, pltpu.roll(block, LANES - 32, 1), pltpu.roll(block, 32, 1))


def flipped(block, axis, bit):
    route = [(i, i ^ bit) for i in range(lax.axis_size(axis))]
    return lax.ppermute(block, axis, route)


def take(array, index, dim):
    return lax.dynamic_index_in_dim(array, index, dim, keepdims=False)


class Weight:
    def __init__(self, pieces, offsets, shape):
        self.pieces, self.offsets, self.shape = pieces, offsets, shape


def whole_weight(weight):
    rows, cols = weight.shape
    shape = (rows * lax.axis_size("fsdp"), cols)
    return Weight([lax.all_gather(weight, "fsdp", axis=0, tiled=True)], [(0, 0)], shape)


def half_of(weight, shift):
    half = weight.shape[0] // 2
    return lax.dynamic_slice_in_dim(weight, lax.axis_index("blk") % 2 * half + shift, half, 0)


def from_halves(weight, first):
    rows, cols = weight.shape
    core, mine = lax.axis_index("blk") % 2, lax.axis_index("fsdp")
    second = flipped(first, "blk", 1)
    other = (1 - mine) * rows
    offsets = [
        (mine * rows, 0),
        (other + core * (rows // 2), 0),
        (other + (1 - core) * (rows // 2), 0),
    ]
    return Weight([weight, first, second], offsets, (2 * rows, cols))


def share_of(weight, shift=0):
    share = weight.shape[0] // lax.axis_size("blk")
    return lax.dynamic_slice_in_dim(weight, lax.axis_index("blk") * share + shift, share, 0)


def from_shares(weight, share):
    rows, cols = weight.shape
    mine = lax.axis_index("fsdp")
    other = lax.all_gather(share, "blk", axis=0, tiled=True)
    return Weight([weight, other], [(mine * rows, 0), ((1 - mine) * rows, 0)], (2 * rows, cols))


def as_table(offsets):
    return jnp.stack([jnp.asarray(v, jnp.int32) for pair in offsets for v in pair])


def weight_copies(table, base, pieces, whole, sems):
    copies = []
    for n, piece in enumerate(pieces):
        rows, cols = piece.shape
        row = pl.multiple_of(table[2 * (base + n)], 16)
        col = pl.multiple_of(table[2 * (base + n) + 1], LANES)
        copies.append(
            pltpu.make_async_copy(
                piece, whole.at[pl.ds(row, rows), pl.ds(col, cols)], sems.at[base + n]
            )
        )
    return copies


def grouped_copies(counts, table, pieces, wholes, sems):
    groups, base = [], 1
    for count, whole in zip(counts, wholes):
        groups.append(weight_copies(table, base, pieces[base - 1 : base - 1 + count], whole, sems))
        base += count
    return groups


def start_all(*groups):
    for group in groups:
        for copy in group:
            copy.start()


def wait_all(*groups):
    for group in groups:
        for copy in group:
            copy.wait()


def weight_operands(weights, lead, after=()):
    counts = [len(w.pieces) for w in weights] + [len(after)]
    pieces = [p for w in weights for p in w.pieces]
    table = as_table([lead] + [o for w in weights for o in w.offsets])
    scratch = [pltpu.VMEM(w.shape, BF) for w in weights]
    return counts, pieces + list(after), table, scratch + [pltpu.SemaphoreType.DMA((len(pieces) + 1,))]


def zero_after(array):
    return jnp.minimum(jnp.abs(array[(0,) * array.ndim].astype(F32)), 0.0).astype(jnp.int32)


ANY = pl.BlockSpec(memory_space=pl.ANY)


def params(limit_mib):
    return pltpu.CompilerParams(vmem_limit_bytes=limit_mib * MIB)


def tied_kernel(*refs):
    del refs


def tied(values, after=()):
    if len(values) + len(after) < 2:
        return list(values)
    return pl.pallas_call(
        tied_kernel,
        in_specs=[ANY] * (len(values) + len(after)),
        out_specs=[ANY] * len(values),
        out_shape=[jax.ShapeDtypeStruct(v.shape, v.dtype) for v in values],
        input_output_aliases={n: n for n in range(len(values))},
        cost_estimate=CHEAP,
    )(*values, *after)


def row_specs(parts, tile, width, steps):
    if len(parts) == 1:
        return [pl.BlockSpec((tile, width), lambda r, i, *_: (r * steps + i, 0))]
    half = steps // 2

    def kept(r, i, t):
        return jnp.where(i // half == t[0], i % half, jnp.where(t[0] == 0, half - 1, 0)), 0

    def moved(r, i, t):
        return jnp.where(i // half != t[0], i % half, jnp.where(t[0] == 0, 0, half - 1)), 0

    return [pl.BlockSpec((tile, width), kept), pl.BlockSpec((tile, width), moved)]


def row_tile(table, refs):
    if len(refs) == 1:
        return refs[0][...]
    own = pl.program_id(1) // (pl.num_programs(1) // 2) == table[0]
    return jnp.where(own, refs[0][...], refs[1][...])


def qkv_kernel(counts, old, table, cos_ref, sin_ref, in_ref, *rest):
    pieces, rest = rest[: sum(counts)], rest[sum(counts) + old :]
    q_ref, k_ref, v_ref, x_ref, whole, sems = rest
    width = q_ref.shape[1]

    @pl.when(pl.program_id(0) == 0)
    def _():
        groups = grouped_copies(counts, table, pieces, [whole], sems)
        start_all(*groups)
        wait_all(*groups)

    x = in_ref[...]
    x_ref[...] = x
    cosine, sine = cos_ref[...], sin_ref[...]
    for ref, start, factor in ((q_ref, 0, 1.0 / math.sqrt(HDIM)), (k_ref, width, 1.0)):
        projected = dot(x, whole[:, start : start + width])
        for b in range(0, width, LANES):
            block = projected[:, b : b + LANES]
            turned = block * cosine + halves_swapped(block) * sine
            ref[:, b : b + LANES] = turned.astype(BF) * jnp.asarray(factor, BF)
    v_ref[...] = dot(x, whole[:, 2 * width :]).astype(BF)


def project(x, start, cosine, sine, weight, old, tile, after=()):
    tokens, width = cosine.shape[0], weight.shape[0]
    counts, pieces, table, scratch = weight_operands([weight], (start // tile, 0), after)
    shifted = lambda i, t: (i + t[0], 0)
    narrow, wide = pl.BlockSpec((tile, LANES), shifted), pl.BlockSpec((tile, width), shifted)
    first = 4 + len(pieces)
    return pl.pallas_call(
        functools.partial(qkv_kernel, counts, len(old)),
        grid_spec=pltpu.PrefetchScalarGridSpec(
            num_scalar_prefetch=1,
            grid=(x.shape[0] // tile,),
            in_specs=[narrow, narrow, pl.BlockSpec((tile, width), lambda i, t: (i, 0))] + [ANY] * (len(pieces) + len(old)),
            out_specs=[wide] * 4,
            scratch_shapes=scratch,
        ),
        out_shape=[jax.ShapeDtypeStruct((tokens, width), BF)] * 4,
        input_output_aliases={first + n: n for n in range(len(old))},
        compiler_params=params(48),
        cost_estimate=cost(6 * x.shape[0] * width * width),
    )(table, cosine, sine, x, *pieces, *old)


def input_grad_kernel(counts, groups, table, dbr_ref, *rest):
    grads, rest = rest[: 3 * groups], rest[3 * groups :]
    pieces, (out_ref, whole, sems) = rest[: sum(counts)], rest[sum(counts) :]
    width = dbr_ref.shape[1]

    @pl.when(pl.program_id(0) == 0)
    def _():
        copies = grouped_copies(counts, table, pieces, [whole], sems)
        start_all(*copies)
        wait_all(*copies)

    total = dbr_ref[...].astype(F32)
    for n, ref in enumerate(grads):
        wide = ref.shape[1]
        start = n % 3 * width + n // 3 * wide
        total += dot_bt(ref[...], whole[:, start : start + wide])
    out_ref[...] = total.astype(out_ref.dtype)


def input_grad_part(dbr, grads, weight, start, tokens, dtype, tile, after=(), whole=False):
    width = dbr.shape[1]
    counts, pieces, table, scratch = weight_operands([weight], (start // tile, 0), after)
    shifted = lambda i, t: (i + t[0], 0)
    return pl.pallas_call(
        functools.partial(input_grad_kernel, counts, len(grads) // 3),
        grid_spec=pltpu.PrefetchScalarGridSpec(
            num_scalar_prefetch=1,
            grid=(tokens // tile,),
            in_specs=[pl.BlockSpec((tile, width), shifted)]
            + [pl.BlockSpec((tile, g.shape[1]), shifted) for g in grads]
            + [ANY] * len(pieces),
            out_specs=pl.BlockSpec((tile, width), shifted if whole else lambda i, t: (i, 0)),
            scratch_shapes=scratch,
        ),
        out_shape=jax.ShapeDtypeStruct((dbr.shape[0] if whole else tokens, width), dtype),
        compiler_params=params(48),
        cost_estimate=cost(6 * tokens * width * width),
    )(table, dbr, *grads, *pieces)


def place_kernel(table, in_ref, old_ref, out_ref):
    del table, old_ref
    out_ref[...] = in_ref[...].astype(out_ref.dtype)


def placed(part, array, start, tile):
    rows, width = part.shape
    return pl.pallas_call(
        place_kernel,
        grid_spec=pltpu.PrefetchScalarGridSpec(
            num_scalar_prefetch=1,
            grid=(rows // tile,),
            in_specs=[pl.BlockSpec((tile, width), lambda i, t: (i, 0)), ANY],
            out_specs=pl.BlockSpec((tile, width), lambda i, t: (i + t[0], 0)),
        ),
        out_shape=jax.ShapeDtypeStruct(array.shape, array.dtype),
        input_output_aliases={2: 0},
        cost_estimate=CHEAP,
    )((start // tile).astype(jnp.int32).reshape(1), part, array)


BQ = 256
BK_FWD = 512
BK_BACK = 256
VROWS = HDIM + 16


def lanes_where(condition):
    return jnp.where(condition(lane_iota((1, LANES))), 1.0, 0.0).astype(BF)


def spread_pairs(whole, source, features, group):
    for g in range(group):
        whole[:, 2 * g * LANES : (2 * g + 1) * LANES] = source[:, g * LANES : (g + 1) * LANES]
        whole[:, (2 * g + 1) * LANES : (2 * g + 2) * LANES] = features[...]


def staggered(count, load, work, finish):
    loaded, worked = load(0), None
    for g in range(count):
        ahead = load(g + 1) if g + 1 < count else None
        result = work(g, loaded)
        if worked is not None:
            finish(g - 1, worked)
        worked, loaded = result, ahead
    finish(count - 1, worked)


def attend_kernel(group, extra, spans, q_ref, k_ref, v_ref, kf_ref, qf_ref, *rest):
    o_ref, lse_ref, kx, vt, qx, best, accum = rest[extra:]
    block = pl.program_id(2)
    where = (pl.program_id(0) * pl.num_programs(2) + block) * 2
    row_len = k_ref.shape[0]

    @pl.when(block == 0)
    def _():
        spread_pairs(kx, k_ref, kf_ref, group)
        for g in range(group):
            for b in range(0, row_len, 256):
                turned = v_ref[b : b + 256, g * LANES : (g + 1) * LANES].astype(F32).T.astype(BF)
                for h in range(2):
                    vt[2 * g + h, :HDIM, b : b + 256] = turned[h * HDIM : (h + 1) * HDIM]
                    vt[2 * g + h, HDIM:, b : b + 256] = jnp.ones((16, 256), BF)

    qf = qf_ref[...]
    even, odd = lanes_where(lambda lane: lane < HDIM), lanes_where(lambda lane: lane >= HDIM)
    for g in range(group):
        q = q_ref[:, g * LANES : (g + 1) * LANES]
        qx[g, :BQ, :LANES] = q * even
        qx[g, BQ:, :LANES] = q * odd
        qx[g, :BQ, LANES:] = qf
        qx[g, BQ:, LANES:] = qf
    best[...] = jnp.full_like(best, NEGATIVE)
    accum[...] = jnp.zeros_like(accum)
    first, count = spans[where], spans[where + 1]

    def step(j, state):
        at = pl.multiple_of(first + j * BK_FWD, LANES)

        def load(g):
            return dot_bt(kx[pl.ds(at, BK_FWD), 2 * g * LANES : 2 * (g + 1) * LANES], qx[g])

        def work(g, scores):
            old = best[g]
            new = jnp.maximum(old, jnp.max(scores, axis=0, keepdims=True))
            best[g] = new
            return jnp.exp(scores - new).astype(BF), jnp.exp(old - new)

        def finish(g, worked):
            soft, factor = worked
            for h in range(2):
                cols = slice(h * BQ, (h + 1) * BQ)
                values = vt[2 * g + h, :, pl.ds(at, BK_FWD)]
                accum[g, :, cols] = accum[g, :, cols] * factor[:, cols] + dot(values, soft[:, cols])

        staggered(group, load, work, finish)
        return state

    lax.fori_loop(0, count, step, 0)
    for g in range(group):
        total = accum[g, HDIM : HDIM + 1]
        lse = best[g] + jnp.log(total)
        lse_ref[2 * g] = lse[:, :BQ]
        lse_ref[2 * g + 1] = lse[:, BQ:]
        turned = accum[g, :HDIM] / total
        turned = jnp.concatenate([turned[:, :BQ], turned[:, BQ:]], axis=0)
        o_ref[:, g * LANES : (g + 1) * LANES] = turned.T.astype(BF)


def attend(q, k, v, key_feat, query_feat, spans, rows, group, after=()):
    tokens, width = q.shape
    row_len = k.shape[0] // rows
    blocks = tokens // rows // BQ
    of_q = lambda r, p, i, *_: (r * blocks + i, p)
    of_k = lambda r, p, i, *_: (r, p)
    wide = group * LANES
    return pl.pallas_call(
        functools.partial(attend_kernel, group, len(after)),
        grid_spec=pltpu.PrefetchScalarGridSpec(
            num_scalar_prefetch=1,
            grid=(rows, PAIRS // group, blocks),
            in_specs=[
                pl.BlockSpec((BQ, wide), of_q),
                pl.BlockSpec((row_len, wide), of_k),
                pl.BlockSpec((row_len, wide), of_k),
                pl.BlockSpec((row_len, LANES), lambda r, p, i, *_: (r, 0)),
                pl.BlockSpec((BQ, LANES), lambda r, p, i, *_: (r * blocks + i, 0)),
            ]
            + [ANY] * len(after),
            out_specs=[
                pl.BlockSpec((BQ, wide), of_q),
                pl.BlockSpec((2 * group, 1, BQ), lambda r, p, i, *_: (p, 0, r * blocks + i)),
            ],
            scratch_shapes=[
                pltpu.VMEM((row_len, 2 * wide), BF),
                pltpu.VMEM((2 * group, VROWS, row_len), BF),
                pltpu.VMEM((group, 2 * BQ, 2 * LANES), BF),
                pltpu.VMEM((group, 1, 2 * BQ), F32),
                pltpu.VMEM((group, VROWS, 2 * BQ), F32),
            ],
        ),
        out_shape=[
            jax.ShapeDtypeStruct((tokens, width), BF),
            jax.ShapeDtypeStruct((HEADS, 1, tokens), F32),
        ],
        compiler_params=params(56),
        cost_estimate=cost(4 * tokens * row_len * width),
    )(spans, q, k, v, key_feat, query_feat, *after)


def attend_back_kernel(
    group, base, extra, spans, q_ref, do_ref, k_ref, v_ref, kf_ref, qf_ref, cq_ref, sq_ref, ck_ref, sk_ref, *rest,
):
    dq_ref, dk_ref, dv_ref, kx, vx, kt, qx, dox, dq_acc, dk_acc, dv_acc = rest[extra:]
    block = pl.program_id(2)
    pair = base + pl.program_id(1) * group
    where = (pl.program_id(0) * pl.num_programs(2) + block) * 2
    row_len = k_ref.shape[0]

    @pl.when(block == 0)
    def _():
        spread_pairs(kx, k_ref, kf_ref, group)
        spread_pairs(vx, v_ref, kf_ref, group)
        for g in range(group):
            for b in range(0, row_len, 256):
                turned = k_ref[b : b + 256, g * LANES : (g + 1) * LANES].astype(F32).T.astype(BF)
                kt[g * LANES : (g + 1) * LANES, b : b + 256] = turned
        dk_acc[...] = jnp.zeros_like(dk_acc)
        dv_acc[...] = jnp.zeros_like(dv_acc)

    qf = qf_ref[...]
    even, odd = lanes_where(lambda lane: lane < HDIM), lanes_where(lambda lane: lane >= HDIM)
    for g in range(group):
        cols = slice(g * LANES, (g + 1) * LANES)
        for whole, source in ((qx, q_ref[:, cols]), (dox, do_ref[:, cols])):
            whole[g, :BQ, :LANES] = source * even
            whole[g, BQ:, :LANES] = source * odd
        for h in range(2):
            head = 2 * (pair + g) + h

            def at(lane, starts):
                return functools.reduce(jnp.logical_or, [lane == start + head for start in starts])

            of_lse = lanes_where(lambda lane: (lane < SEG) | at(lane, (8, 20, 32)))
            of_delta = lanes_where(lambda lane: at(lane, (44, 56, 68)))
            qx[g, h * BQ : (h + 1) * BQ, LANES:] = qf * of_lse
            dox[g, h * BQ : (h + 1) * BQ, LANES:] = qf * of_delta
    dq_acc[...] = jnp.zeros_like(dq_acc)
    first, count = spans[where], spans[where + 1]

    def step(j, state):
        at = pl.multiple_of(first + j * BK_BACK, LANES)

        def load(g):
            twice = slice(2 * g * LANES, (2 * g + 2) * LANES)
            return dot_bt(kx[pl.ds(at, BK_BACK), twice], qx[g]), dot_bt(vx[pl.ds(at, BK_BACK), twice], dox[g])

        def work(g, loaded):
            probs = jnp.exp(loaded[0])
            return probs.astype(BF), (probs * loaded[1]).astype(BF)

        def finish(g, worked):
            probs, grad = worked
            cols = slice(g * LANES, (g + 1) * LANES)
            dv_acc[pl.ds(at, BK_BACK), cols] += dot(probs, dox[g, :, :LANES])
            dk_acc[pl.ds(at, BK_BACK), cols] += dot(grad, qx[g, :, :LANES])
            for h in range(2):
                rows = slice(g * LANES + h * HDIM, g * LANES + (h + 1) * HDIM)
                dq_acc[rows] += dot(kt[rows, pl.ds(at, BK_BACK)], grad[:, h * BQ : (h + 1) * BQ])

        staggered(group, load, work, finish)
        return state

    lax.fori_loop(0, count, step, 0)
    for g in range(group):
        cols = slice(g * LANES, (g + 1) * LANES)
        dq = dq_acc[cols].T * (1.0 / math.sqrt(HDIM))
        dq_ref[:, cols] = (dq * cq_ref[...] - halves_swapped(dq) * sq_ref[...]).astype(BF)

    @pl.when(block == pl.num_programs(2) - 1)
    def _():
        for b in range(0, row_len, 256):
            part = pl.ds(b, 256)
            cosine, sine = ck_ref[part, :], sk_ref[part, :]
            for g in range(group):
                cols = slice(g * LANES, (g + 1) * LANES)
                dk = dk_acc[part, cols]
                dk_ref[part, cols] = (dk * cosine - halves_swapped(dk) * sine).astype(BF)
            dv_ref[part, :] = dv_acc[part, :].astype(BF)


def attend_back(q, do, k, v, key_feat, query_feat, spans, tables_q, tables_k, rows, group, base, pairs, after=()):
    tokens, width = q.shape
    row_len = k.shape[0] // rows
    blocks = tokens // rows // BQ
    start = base // group
    of_q = lambda r, p, i, *_: (r * blocks + i, start + p)
    of_k = lambda r, p, i, *_: (r, start + p)
    per_q = pl.BlockSpec((BQ, LANES), lambda r, p, i, *_: (r * blocks + i, 0))
    per_k = pl.BlockSpec((row_len, LANES), lambda r, p, i, *_: (r, 0))
    wide = group * LANES
    return pl.pallas_call(
        functools.partial(attend_back_kernel, group, base, len(after)),
        grid_spec=pltpu.PrefetchScalarGridSpec(
            num_scalar_prefetch=1,
            grid=(rows, pairs // group, blocks),
            in_specs=[
                pl.BlockSpec((BQ, wide), of_q),
                pl.BlockSpec((BQ, wide), of_q),
                pl.BlockSpec((row_len, wide), of_k),
                pl.BlockSpec((row_len, wide), of_k),
                per_k,
                per_q,
                per_q,
                per_q,
                per_k,
                per_k,
            ]
            + [ANY] * len(after),
            out_specs=[
                pl.BlockSpec((BQ, wide), lambda r, p, i, *_: (r * blocks + i, p)),
                pl.BlockSpec((row_len, wide), lambda r, p, i, *_: (r, p)),
                pl.BlockSpec((row_len, wide), lambda r, p, i, *_: (r, p)),
            ],
            scratch_shapes=[
                pltpu.VMEM((row_len, 2 * wide), BF),
                pltpu.VMEM((row_len, 2 * wide), BF),
                pltpu.VMEM((wide, row_len), BF),
                pltpu.VMEM((group, 2 * BQ, 2 * LANES), BF),
                pltpu.VMEM((group, 2 * BQ, 2 * LANES), BF),
                pltpu.VMEM((wide, BQ), F32),
                pltpu.VMEM((row_len, wide), F32),
                pltpu.VMEM((row_len, wide), F32),
            ],
        ),
        out_shape=[
            jax.ShapeDtypeStruct((tokens, pairs * LANES), BF),
            jax.ShapeDtypeStruct((rows * row_len, pairs * LANES), BF),
            jax.ShapeDtypeStruct((rows * row_len, pairs * LANES), BF),
        ],
        compiler_params=params(56),
        cost_estimate=cost(8 * tokens * row_len * pairs * LANES),
    )(spans, q, do, k, v, key_feat, query_feat, *tables_q, *tables_k, *after)


FF_CHUNK = 512


def normalize(hidden):
    average = jnp.mean(hidden, -1, keepdims=True)
    centred = hidden - average
    inverse = lax.rsqrt(jnp.mean(centred * centred, -1, keepdims=True) + EPSILON)
    return centred * inverse, inverse


def norm_back(scaled, normalized, inverse):
    return inverse * (
        scaled
        - jnp.mean(scaled, -1, keepdims=True)
        - normalized * jnp.mean(scaled * normalized, -1, keepdims=True)
    )


def split_two(value):
    high = value.astype(BF)
    return high, (value - high.astype(F32)).astype(BF)


def mix_kernel(counts, table, att_ref, x_ref, qf_ref, g1_ref, g2_ref, *rest):
    pieces, rest = rest[: sum(counts)], rest[sum(counts) :]
    nl_ref, stat_ref, hid_ref, fg_ref, fu_ref, out_ref, pool_ref, wo, ws, wd, sems = rest
    groups = grouped_copies(counts, table, pieces, (wo, ws, wd), sems)
    step, begin = pl.program_id(1), (pl.program_id(0) == 0) & (pl.program_id(1) == 0)

    @pl.when(begin)
    def _():
        start_all(*groups)
        wait_all(groups[0])

    branch = dot(att_ref[...], wo[...])
    unit, inverse1 = normalize(x_ref[...].astype(F32) + branch)
    normed = unit * g1_ref[...]
    low = normed.astype(BF)
    nl_ref[...] = low

    @pl.when(begin)
    def _():
        wait_all(*groups[1:])

    ff = wd.shape[0]
    hidden_sum = [normed]

    def load(c):
        cols = slice(c * FF_CHUNK, (c + 1) * FF_CHUNK)
        return dot(low, ws[:, cols]), dot(low, ws[:, ff + c * FF_CHUNK : ff + (c + 1) * FF_CHUNK])

    def work(c, loaded):
        cols = slice(c * FF_CHUNK, (c + 1) * FF_CHUNK)
        gate, up = loaded
        sig = 0.5 + 0.5 * jnp.tanh(0.5 * gate)
        silu = gate * sig
        hidden = (silu * up).astype(BF)
        hid_ref[:, cols] = hidden
        fg_ref[:, cols] = (up * (sig + silu * (1.0 - sig))).astype(BF)
        fu_ref[:, cols] = silu.astype(BF)
        return hidden

    def finish(c, hidden):
        hidden_sum[0] = hidden_sum[0] + dot(hidden, wd[c * FF_CHUNK : (c + 1) * FF_CHUNK, :])

    staggered(ff // FF_CHUNK, load, work, finish)
    unit2, inverse2 = normalize(hidden_sum[0])
    output = unit2 * g2_ref[...]
    out_ref[...] = output.astype(BF)
    lanes = lane_iota(stat_ref.shape)
    stat_ref[...] = jnp.where(lanes == 0, inverse1, inverse2)
    high, rest_low = split_two(output)
    member = qf_ref[...]
    sums = (dot_at(member, high) + dot_at(member, rest_low))[:SEG]

    @pl.when(step == 0)
    def _():
        pool_ref[0] = sums

    @pl.when(step > 0)
    def _():
        pool_ref[0] += sums


def mix(attended, x, query_feat, gain1, gain2, weights, rows, tile, after):
    tokens, width = x.shape
    steps = tokens // rows // tile
    ff = weights[2].shape[0]
    counts, pieces, table, scratch = weight_operands(weights, (0, 0), after)
    wide, narrow = row_specs([None], tile, width, steps), row_specs([None], tile, LANES, steps)
    hidden, fixed = row_specs([None], tile, ff, steps), [pl.BlockSpec((1, width), lambda r, i, *_: (0, 0))]
    return pl.pallas_call(
        functools.partial(mix_kernel, counts),
        grid_spec=pltpu.PrefetchScalarGridSpec(
            num_scalar_prefetch=1,
            grid=(rows, steps),
            in_specs=wide * 2 + narrow + fixed * 2 + [ANY] * len(pieces),
            out_specs=wide + narrow + hidden * 3 + wide + [pl.BlockSpec((1, SEG, width), lambda r, i, *_: (r, 0, 0))],
            scratch_shapes=scratch,
        ),
        out_shape=[
            jax.ShapeDtypeStruct((tokens, width), BF),
            jax.ShapeDtypeStruct((tokens, LANES), F32),
            jax.ShapeDtypeStruct((tokens, ff), BF),
            jax.ShapeDtypeStruct((tokens, ff), BF),
            jax.ShapeDtypeStruct((tokens, ff), BF),
            jax.ShapeDtypeStruct((tokens, width), BF),
            jax.ShapeDtypeStruct((rows, SEG, width), F32),
        ],
        compiler_params=params(58),
        cost_estimate=cost(2 * tokens * width * (width + 3 * ff)),
    )(table, attended, x, query_feat, gain1, gain2, *pieces)


def hidden_back_kernel(counts, parts, table, *rest):
    cot_refs, rest = rest[:parts], rest[parts:]
    out_ref, stat_ref, qf_ref, dp_ref, fg_ref, fu_ref, g2_ref = rest[:7]
    pieces, rest = rest[7 : 7 + sum(counts)], rest[7 + sum(counts) :]
    dffn_ref, dgu_ref, gf_ref, wd, sems = rest
    groups = grouped_copies(counts, table, pieces, [wd], sems)
    begin = (pl.program_id(0) == 0) & (pl.program_id(1) == 0)

    @pl.when(begin)
    def _():
        start_all(*groups)
        gf_ref[...] = jnp.zeros_like(gf_ref)

    inverse2 = stat_ref[:, 1:2]
    member = qf_ref[...]
    high, rest_low = split_two(dp_ref[0])
    upstream = row_tile(table, cot_refs).astype(F32) + dot(member, high) + dot(member, rest_low)
    gain2 = g2_ref[...]
    unit2 = out_ref[...].astype(F32) / gain2
    dffn = norm_back(upstream * gain2, unit2, inverse2).astype(BF)
    dffn_ref[...] = dffn
    tile, width = dffn.shape
    gf_ref[...] += jnp.sum((upstream * unit2).reshape(tile // 8, 8, width), axis=0)

    @pl.when(begin)
    def _():
        wait_all(*groups)

    ff = wd.shape[0]

    def load(c):
        return dot_bt(dffn, wd[c * FF_CHUNK : (c + 1) * FF_CHUNK, :])

    def work(c, dhid):
        cols = slice(c * FF_CHUNK, (c + 1) * FF_CHUNK)
        dgu_ref[:, cols] = (dhid * fg_ref[:, cols].astype(F32)).astype(BF)
        after = slice(ff + c * FF_CHUNK, ff + (c + 1) * FF_CHUNK)
        dgu_ref[:, after] = (dhid * fu_ref[:, cols].astype(F32)).astype(BF)

    staggered(ff // FF_CHUNK, load, work, lambda c, worked: None)


def hidden_back(cots, lead, output, stat, query_feat, dpool, factors, gain2, down, rows, tile):
    tokens, width = output.shape
    ff = down.shape[0]
    steps = tokens // rows // tile
    counts, pieces, table, scratch = weight_operands([down], (lead, 0))
    wide, narrow = row_specs([None], tile, width, steps), row_specs([None], tile, LANES, steps)
    hidden = row_specs([None], tile, ff, steps)
    return pl.pallas_call(
        functools.partial(hidden_back_kernel, counts, len(cots)),
        grid_spec=pltpu.PrefetchScalarGridSpec(
            num_scalar_prefetch=1,
            grid=(rows, steps),
            in_specs=row_specs(cots, tile, width, steps)
            + wide
            + narrow * 2
            + [pl.BlockSpec((1, LANES, width), lambda r, i, *_: (r, 0, 0))]
            + hidden * 2
            + [pl.BlockSpec((1, width), lambda r, i, *_: (0, 0))]
            + [ANY] * len(pieces),
            out_specs=wide + row_specs([None], tile, 2 * ff, steps) + [pl.BlockSpec((8, width), lambda r, i, *_: (0, 0))],
            scratch_shapes=scratch,
        ),
        out_shape=[
            jax.ShapeDtypeStruct((tokens, width), BF),
            jax.ShapeDtypeStruct((tokens, 2 * ff), BF),
            jax.ShapeDtypeStruct((8, width), F32),
        ],
        compiler_params=params(58),
        cost_estimate=cost(4 * tokens * width * ff),
    )(table, *cots, output, stat, query_feat, dpool, *factors, gain2, *pieces)


def branch_back_kernel(counts, table, *refs):
    dffn_ref, nl_ref, stat_ref, qf_ref, dgu_ref, att_ref, lse_ref, g1_ref, head_ref = refs[:9]
    rest = refs[9:]
    pieces, rest = rest[: sum(counts)], rest[sum(counts) :]
    dbr_ref, datt_ref, feat_ref, ga_ref, wo, ws, sems = rest
    groups = grouped_copies(counts, table, pieces, (wo, ws), sems)
    begin = (pl.program_id(0) == 0) & (pl.program_id(1) == 0)

    @pl.when(begin)
    def _():
        start_all(*groups)
        ga_ref[...] = jnp.zeros_like(ga_ref)
        wait_all(*groups)

    dnormed = dffn_ref[...].astype(F32) + dot_bt(dgu_ref[...], ws[...])
    gain1 = g1_ref[...]
    unit1 = nl_ref[...].astype(F32) / gain1
    dbr = norm_back(dnormed * gain1, unit1, stat_ref[:, 0:1]).astype(BF)
    dbr_ref[...] = dbr
    datt = dot_bt(dbr, wo[...]).astype(BF)
    datt_ref[...] = datt
    tile, width = datt.shape
    ga_ref[...] += jnp.sum((dnormed * unit1).reshape(tile // 8, 8, width), axis=0)

    high, rest_low = split_two(datt.astype(F32) * att_ref[...].astype(F32))
    heads = head_ref[...]
    delta = dot(high, heads) + dot(rest_low, heads)
    feat = qf_ref[...].astype(F32)
    for value, start in ((lse_ref[...], 8), (delta, 44)):
        left = -value
        for n in range(3):
            part = left.astype(BF).astype(F32)
            left = left - part
            feat = feat + pltpu.roll(part, start + HEADS * n, 1)
    feat_ref[...] = feat.astype(BF)


def branch_back(dffn, low, stat, query_feat, dgu, attended, lse, gain1, weights, rows, tile, after=()):
    tokens, width = low.shape
    ff = dgu.shape[1] // 2
    steps = tokens // rows // tile
    counts, pieces, table, scratch = weight_operands(weights, (0, 0), after)
    wide, narrow = row_specs([None], tile, width, steps), row_specs([None], tile, LANES, steps)
    hidden = row_specs([None], tile, 2 * ff, steps)
    heads = (jnp.arange(width)[:, None] // HDIM == jnp.arange(LANES)[None, :]).astype(BF)
    return pl.pallas_call(
        functools.partial(branch_back_kernel, counts),
        grid_spec=pltpu.PrefetchScalarGridSpec(
            num_scalar_prefetch=1,
            grid=(rows, steps),
            in_specs=wide * 2
            + narrow * 2
            + hidden
            + wide
            + narrow
            + [pl.BlockSpec((1, width), lambda r, i, *_: (0, 0))]
            + [pl.BlockSpec((width, LANES), lambda r, i, *_: (0, 0))]
            + [ANY] * len(pieces),
            out_specs=wide * 2 + narrow + [pl.BlockSpec((8, width), lambda r, i, *_: (0, 0))],
            scratch_shapes=scratch,
        ),
        out_shape=[
            jax.ShapeDtypeStruct((tokens, width), BF),
            jax.ShapeDtypeStruct((tokens, width), BF),
            jax.ShapeDtypeStruct((tokens, LANES), BF),
            jax.ShapeDtypeStruct((8, width), F32),
        ],
        compiler_params=params(58),
        cost_estimate=cost(2 * tokens * width * (width + 2 * ff)),
    )(table, dffn, low, stat, query_feat, dgu, attended, lse, gain1, heads, *pieces)


def bits_of(axis):
    size, bit = lax.axis_size(axis), 1
    while bit < size:
        yield bit
        bit *= 2


def in_order(parts, index):
    shape = (2,) + (1,) * parts[0].ndim
    first = lax.broadcasted_iota(jnp.int32, shape, 0) == index
    return jnp.where(first, parts[0][None], parts[1][None])


def add(first, *others):
    total = first.astype(F32)
    for other in others:
        total = total + other.astype(F32)
    return total.astype(BF)


def reduction(part, short):
    rows, cols = part.shape
    shards = lax.axis_size("fsdp")
    mine, place = lax.axis_index("fsdp"), lax.axis_index("blk")
    core, side = place % 2, place // 2 % 2
    now = part.reshape(shards, 2, rows // shards // 2, cols)
    (came,) = yield [take(now, 1 - core, 1)], [("blk", 1)]
    now = add(take(now, core, 1), came)
    bit = shards // 2
    while bit:
        now = now.reshape(2, bit, -1, cols)
        own = mine // bit % 2
        (came,) = yield [take(now, 1 - own, 0)], [("fsdp", bit)]
        now = add(take(now, own, 0), came)
        bit //= 2
    now = now.reshape(2, -1, cols)
    (came,) = yield [take(now, 1 - side, 0)], [("blk", 2)]
    now = add(take(now, side, 0), came)
    bits = [bit for bit in bits_of("blk") if bit > 2]
    if short:
        for bit in bits:
            (came,) = yield [now], [("blk", bit)]
            now = add(now, came)
    else:
        for bit in bits:
            now = now.reshape(2, -1, cols)
            own = place // bit % 2
            (came,) = yield [take(now, 1 - own, 0)], [("blk", bit)]
            now = add(take(now, own, 0), came)
        for bit in bits[::-1]:
            (came,) = yield [now], [("blk", bit)]
            now = in_order([now, came], place // bit % 2).reshape(-1, cols)
    now = now.reshape(-1, cols)
    (came,) = yield [now], [("blk", 2)]
    now = in_order([now, came], side).reshape(-1, cols)
    (came,) = yield [now], [("blk", 1)]
    yield [now, came], None


class Reduction:
    def __init__(self, part, short=False):
        fsdp_bits, lines = len(list(bits_of("fsdp"))), len(list(bits_of("blk"))) - 2
        self.left = 4 + fsdp_bits + lines * (1 if short else 2)
        self.stages = reduction(part, short)
        self.sends, self.routes = next(self.stages)

    @property
    def done(self):
        return self.routes is None

    @property
    def result(self):
        return self.sends

    def launch(self):
        came = [flipped(a, *route) for a, route in zip(self.sends, self.routes)]
        return self.sends, came

    def take_in(self, came):
        self.left -= 1
        self.sends, self.routes = self.stages.send(came)


def beside(work, launches, joins=None):
    sent, flights = [], []
    for r in launches:
        if not r.done:
            sends, came = r.launch()
            sent += sends
            flights.append((r, came))
    values = list(work(sent))
    late = []
    if joins is not None:
        late = [f for f in flights if f[0] not in [j for j in joins if isinstance(j, Reduction)]]
        flights = [f for f in flights if f not in late] + [j for j in joins if not isinstance(j, Reduction)]
    count = len(values)
    both = tied(values + [a for _, came in flights for a in came])
    at = count
    for r, came in flights:
        r.take_in(both[at : at + len(came)])
        at += len(came)
    return both[:count], late


def turned(block):
    return block.astype(F32).T.astype(BF)


def swiglu_part_kernel(low_ref, grad_ref, out_ref, low_turned):
    tokens = low_ref.shape[0]

    @pl.when(pl.program_id(0) == 0)
    def _():
        for b in range(0, tokens, 256):
            low_turned[:, b : b + 256] = turned(low_ref[b : b + 256, :])

    part = dot(low_turned[...], grad_ref[...]).astype(BF)
    rows = out_ref.shape[2]
    for f in range(out_ref.shape[1]):
        out_ref[0, f] = part[f * rows : (f + 1) * rows]


def down_part_kernel(hidden_ref, dffn_ref, old_ref, out_ref):
    del old_ref
    part = dot(turned(hidden_ref[...]), dffn_ref[...]).astype(BF)
    rows, cols = out_ref.shape[2:]
    across = part.shape[1] // cols
    for n in range(out_ref.shape[0]):
        down, along = n // across * rows, n % across * cols
        out_ref[n, 0] = part[down : down + rows, along : along + cols]


def shares_fit(low, hidden):
    blocks, split = lax.axis_size("blk"), lax.axis_size("fsdp")
    width, ff = low.shape[1], hidden.shape[1]
    cols = 2 * ff // blocks
    return cols % LANES == 0 and width % cols == 0 and ff * width // (split * blocks * cols) * 2 == width // split


def feed_forward_shares(low, d_gate_up, hidden, d_ffn):
    blocks, split = lax.axis_size("blk"), lax.axis_size("fsdp")
    tokens, width = low.shape
    ff = hidden.shape[1]
    cols, rows = 2 * ff // blocks, width // split
    down_rows = rows // 2
    across = width // cols
    shape = jax.ShapeDtypeStruct((blocks, split, rows + down_rows, cols), BF)
    whole = lambda a: pl.BlockSpec(a.shape, lambda *_: (0, 0))
    shares = pl.pallas_call(
        swiglu_part_kernel,
        grid=(blocks,),
        in_specs=[whole(low), pl.BlockSpec((tokens, cols), lambda j: (0, j))],
        out_specs=pl.BlockSpec((1, split, rows, cols), lambda j: (j, 0, 0, 0)),
        out_shape=shape,
        scratch_shapes=[pltpu.VMEM((width, tokens), BF)],
        compiler_params=params(48),
        cost_estimate=cost(4 * tokens * width * ff),
    )(low, d_gate_up)
    taken = 2 * down_rows
    steps = ff // split // taken
    return pl.pallas_call(
        down_part_kernel,
        grid=(split, steps),
        in_specs=[pl.BlockSpec((tokens, taken), lambda f, j: (0, f * steps + j)), whole(d_ffn), ANY],
        out_specs=pl.BlockSpec((2 * across, 1, down_rows, cols), lambda f, j: (j, f, 2, 0)),
        out_shape=shape,
        input_output_aliases={2: 0},
        compiler_params=params(48),
        cost_estimate=cost(2 * tokens * width * ff),
    )(hidden, d_ffn, shares)


def plain_sum(part):
    part = lax.psum_scatter(part, "fsdp", scatter_dimension=0, tiled=True)
    return lax.psum(part, "blk").astype(F32)


def weight_grad(pairs, beside_it=None, after=()):
    arrays, left = [], []
    for a, b in pairs:
        place = [n for n, other in enumerate(arrays) if other is a]
        if not place:
            arrays.append(a)
            place = [len(arrays) - 1]
        arrays.append(b)
        left.append((place[0], len(arrays) - 1))
    cols = sum(b.shape[1] for _, b in pairs)
    last = []
    if beside_it is not None:
        last = [beside_it]
        cols += beside_it.shape[1]

    def kernel(*refs):
        out_ref, at = refs[-1], 0
        for a, b in left:
            part = dot_at(refs[a][...], refs[b][...]).astype(BF)
            out_ref[:, at : at + part.shape[1]] = part
            at += part.shape[1]
        if last:
            out_ref[:, at:] = refs[len(arrays)][...]

    whole = pl.BlockSpec(memory_space=pltpu.VMEM)
    return pl.pallas_call(
        kernel,
        in_specs=[whole] * (len(arrays) + len(last)) + [ANY] * len(after),
        out_shape=jax.ShapeDtypeStruct((pairs[0][0].shape[1], cols), BF),
        compiler_params=params(56),
        cost_estimate=cost(2 * pairs[0][0].shape[0] * pairs[0][0].shape[1] * cols),
    )(*arrays, *last, *after)


def unfold_kernel(kinds, columns, table, *refs):
    own = pl.program_id(0) == table[0]
    values, at = [], 0
    for kind in kinds:
        values.append(refs[at][...] if kind == 1 else jnp.where(own, refs[at][...], refs[at + 1][...]))
        at += kind
    for ref, parts in zip(refs[at:], columns):
        to = 0
        for n, start, wide in parts:
            ref[:, to : to + wide] = values[n][:, start : start + wide].astype(F32)
            to += wide


def unfold(results, columns):
    rows = sum(a.shape[0] for a in results[0]) // 2
    block = rows // 2 if rows % 32 == 0 else rows
    steps = rows // block
    maps = {2: lambda c, i, t: (i, 0), 1: lambda c, i, t: (c * steps + i, 0)}
    return pl.pallas_call(
        functools.partial(unfold_kernel, [len(r) for r in results], columns),
        grid_spec=pltpu.PrefetchScalarGridSpec(
            num_scalar_prefetch=1,
            grid=(2, steps),
            in_specs=[pl.BlockSpec((block, a.shape[1]), maps[len(r)]) for r in results for a in r],
            out_specs=[pl.BlockSpec((block, sum(p[2] for p in parts)), maps[1]) for parts in columns],
        ),
        out_shape=[jax.ShapeDtypeStruct((2 * rows, sum(p[2] for p in parts)), F32) for parts in columns],
        compiler_params=params(40),
        cost_estimate=CHEAP,
    )((lax.axis_index("blk") % 2).reshape(1), *[a for r in results for a in r])


def spread_kernel(both_ref, swiglu_ref, down_ref):
    rows = swiglu_ref.shape[0]
    swiglu_ref[...] = both_ref[0, :rows, :].astype(F32)
    down_ref[...] = both_ref[0, rows:, :].astype(F32)


def spread(both, width):
    blocks, height, cols = both.shape
    rows = height * 2 // 3
    across = width // cols
    return pl.pallas_call(
        spread_kernel,
        grid=(blocks,),
        in_specs=[pl.BlockSpec((1, height, cols), lambda n: (n, 0, 0))],
        out_specs=[
            pl.BlockSpec((rows, cols), lambda n: (0, n)),
            pl.BlockSpec((rows // 2, cols), lambda n: (n // across, n % across)),
        ],
        out_shape=[
            jax.ShapeDtypeStruct((rows, blocks * cols), F32),
            jax.ShapeDtypeStruct((blocks // across * (rows // 2), width), F32),
        ],
        compiler_params=params(40),
        cost_estimate=CHEAP,
    )(both)


def contrast(sums, lengths, pairing, row_mode, row_ids):
    rows, segs, width = sums.shape
    lengths = lengths.astype(F32)[..., None]
    pooled = sums / lengths
    inverse = lax.rsqrt(jnp.sum(pooled * pooled, -1, keepdims=True) + EMB_EPSILON)
    embedded = pooled * inverse
    own = rows * segs
    pair = jnp.stack([pairing, jnp.zeros_like(pairing)], axis=-1).reshape(own, 1)
    spare = jnp.concatenate([pair // 128, pair % 128, jnp.zeros((own, 126), jnp.int32)], axis=1)
    buffer = jnp.concatenate([embedded.reshape(own, width).astype(BF), spare.astype(BF)], axis=1)
    ids = row_ids
    for axis in ("fsdp", "blk") if row_mode else ("blk",):
        for bit in bits_of(axis):
            buffer = jnp.concatenate([buffer, flipped(buffer, axis, bit)], axis=0)
            if axis == "fsdp":
                ids = jnp.concatenate([ids, ids ^ bit])
            else:
                ids = jnp.concatenate([ids, ids ^ (bit * ROWS_PER_BLOCK)])
    total = buffer.shape[0]
    every = buffer[:, :width]
    pair_all = (buffer[:, width].astype(jnp.int32) * 128 + buffer[:, width + 1].astype(jnp.int32))[:, None]
    seg = jnp.arange(total, dtype=jnp.int32) % segs
    number = jnp.broadcast_to(ids[:, None], (total // segs, segs)).reshape(total) * (segs // 2) + seg // 2
    is_query = (seg % 2 == 0)[:, None]
    is_doc = (seg % 2 == 1)[None, :]
    target = is_query & is_doc & (pair_all == number[None, :])
    sims = dot_bt(every, every) / SOFTMAX_WARMTH
    masked = jnp.where(is_doc, sims, NEGATIVE)
    best = jnp.max(masked, -1, keepdims=True)
    log_total = best + jnp.log(jnp.sum(jnp.exp(masked - best), -1, keepdims=True))
    positive = jnp.sum(jnp.where(target, sims, 0.0), -1, keepdims=True)
    loss = jnp.sum(jnp.where(is_query[:own], log_total[:own] - positive[:own], 0.0))
    d_sims = CONTRAST_WEIGHT * (jnp.exp(masked - log_total) - target.astype(F32))
    d_sims = jnp.where(is_query, d_sims, 0.0).astype(BF)
    grad = (dot(d_sims[:own], every) + dot_at(d_sims[:, :own], every)) / SOFTMAX_WARMTH
    grad = grad.reshape(rows, segs, width)
    along = jnp.sum(embedded * grad, -1, keepdims=True)
    return loss, inverse * (grad - embedded * along) / lengths


ROWS_PER_BLOCK = 2


def shards(
    tokens,
    cotangent,
    segments,
    doc_lengths,
    positions,
    pairing,
    qkv_weight,
    out_weight,
    swiglu_weight,
    down_weight,
    attn_gain,
    ffn_gain,
):
    rows_here, shard_len, width = tokens.shape
    split = lax.axis_size("fsdp")
    mine = lax.axis_index("fsdp")
    place = lax.axis_index("blk")
    row_len = shard_len * split
    row_mode = split == rows_here == 2

    if row_mode:
        rows, per_row, query_start, lead = 1, row_len, 0, mine
        lengths = lax.dynamic_slice_in_dim(doc_lengths, mine, 1, 0)
        own_pairing = lax.dynamic_slice_in_dim(pairing.reshape(rows_here, -1), mine, 1, 0)
        row_ids = (place * rows_here + mine)[None]
    else:
        rows, per_row, query_start, lead = rows_here, shard_len, mine * shard_len, 0
        lengths, own_pairing = doc_lengths, pairing.reshape(rows_here, -1)
        row_ids = place * rows_here + jnp.arange(rows_here, dtype=jnp.int32)
    tokens_here = rows * per_row
    tile = min(512, per_row)
    small_tile = min(256, per_row)

    gains = jnp.stack([attn_gain, ffn_gain])
    if row_mode:
        qkv_share = flipped(share_of(qkv_weight), "fsdp", 1)
        moved, qkv_share = tied([take(tokens, 1 - mine, 0), qkv_share])
        moved = flipped(moved, "fsdp", 1)
        qkv = from_shares(qkv_weight, qkv_share)
        gains = in_order([gains, flipped(gains, "fsdp", 1)], mine)
        gains = jnp.concatenate([gains[0], gains[1]], axis=1)
    else:
        qkv, swiglu = whole_weight(qkv_weight), whole_weight(swiglu_weight)
        gains = lax.all_gather(gains, "fsdp", axis=1, tiled=True)
    gain1, gain2 = gains[0:1].astype(F32), gains[1:2].astype(F32)

    order = jnp.arange(SEG, dtype=jnp.int32)
    ends = jnp.sum(jnp.where(order[None, :] <= order[:, None], lengths[:, None, :], 0), -1)
    starts = ends - lengths
    token = jnp.arange(row_len, dtype=jnp.int32)
    at = token[None, :, None]
    member = (at >= starts[:, None, :]) & (at < ends[:, None, :])
    first_of = jnp.max(jnp.where(at >= starts[:, None, :], starts[:, None, :], 0), -1)
    lane = jnp.arange(LANES, dtype=jnp.int32)
    frequency = ROPE_BASE ** (-2.0 * (lane % 32).astype(F32) / HDIM)
    angles = (token[None, :] - first_of).astype(F32)[..., None] * frequency
    cosine = jnp.cos(angles).reshape(-1, LANES)
    sine = (jnp.sin(angles) * jnp.where(lane % HDIM < 32, -1.0, 1.0)).reshape(-1, LANES)
    key_feat = jnp.where(member, 0.0, NEGATIVE)
    key_feat = jnp.concatenate([key_feat, jnp.ones((rows, row_len, 120), F32)], -1)
    key_feat = key_feat.astype(BF).reshape(-1, LANES)
    query_feat = jnp.pad(member.astype(BF), ((0, 0), (0, 0), (0, 120))).reshape(-1, LANES)

    def of_queries(table):
        if row_mode:
            return table
        table = table.reshape(rows, row_len, LANES)
        return lax.dynamic_slice_in_dim(table, query_start, per_row, 1).reshape(-1, LANES)

    tables_k = (cosine, sine)
    tables_q = (of_queries(cosine), of_queries(sine))
    query_feat = of_queries(query_feat)
    block_first = query_start + BQ * jnp.arange(per_row // BQ, dtype=jnp.int32)[None, :, None]
    low = jnp.max(jnp.where(block_first >= starts[:, None, :], starts[:, None, :], 0), -1)
    high = jnp.min(jnp.where(block_first + BQ - 1 < ends[:, None, :], ends[:, None, :], row_len), -1)
    low = low // LANES * LANES

    def spans_of(size):
        count = (high - low + size - 1) // size
        return jnp.stack([jnp.minimum(low, row_len - count * size), count], axis=-1).reshape(-1).astype(jnp.int32)

    spans, spans_back = spans_of(BK_FWD), spans_of(BK_BACK)

    if row_mode:
        tables = (*tables_q, qkv)
        share = share_of(swiglu_weight, zero_after(moved))
        share_came = flipped(share, "fsdp", 1)
        old = project(take(tokens, mine, 0), mine * shard_len, *tables, [], small_tile, [moved, share])
        *old, share_came = tied([*old, share_came])
        swiglu = from_shares(swiglu_weight, share_came)
        shift = zero_after(old[0])
        halves = [half_of(out_weight, shift), half_of(down_weight, shift)]
        firsts = [flipped(h, "fsdp", 1) for h in halves]
        query, key, value, x = project(moved, (1 - mine) * shard_len, *tables, old, small_tile, halves)
        key_all, value_all = key, value
    else:
        query, key, value, x = project(tokens.reshape(-1, width), 0, *tables_q, qkv, [], small_tile)

        def along_row(part):
            part = part.reshape(rows, per_row, width)
            return lax.all_gather(part, "fsdp", axis=1, tiled=True).reshape(-1, width)

        key_all, value_all = along_row(key), along_row(value)
    attended, lse = attend(query, key_all, value_all, key_feat, query_feat, spans, rows, PAIRS)
    if row_mode:
        attended, *firsts = tied([attended, *firsts], [lse])
        outer, down = from_halves(out_weight, firsts[0]), from_halves(down_weight, firsts[1])
        cot_send = take(cotangent, 1 - mine + zero_after(firsts[1]), 0)
        cots = [take(cotangent, mine, 0), flipped(cot_send, "fsdp", 1)]
        after = [cot_send]
    else:
        outer, down = whole_weight(out_weight), whole_weight(down_weight)
        cots, after = [cotangent.reshape(-1, width)], []
    low_normed, stat, hidden, *factors, output, sums = mix(
        attended, x, query_feat, gain1, gain2, (outer, swiglu, down), rows, small_tile, after
    )
    if row_mode:
        sums, cots[1] = tied([sums, cots[1]])
        output_came = flipped(lax.dynamic_slice_in_dim(output, (1 - mine) * shard_len, shard_len, 0), "fsdp", 1)
    else:
        layer_output = output.reshape(tokens.shape)
        sums = lax.psum(sums, "fsdp")
    loss, d_pool = contrast(sums, lengths, own_pairing, row_mode, row_ids)
    d_pool = jnp.pad(d_pool, ((0, 0), (0, LANES - SEG), (0, 0)))
    lse_columns = jnp.pad(lse.reshape(HEADS, tokens_here).T, ((0, 0), (0, LANES - HEADS)))

    d_ffn, d_gate_up, gain2_part = hidden_back(
        cots, lead, output, stat, query_feat, d_pool, factors, gain2, down, rows, small_tile
    )
    fast = row_mode and shares_fit(low_normed, hidden)
    if fast:
        share = feed_forward_shares(low_normed, d_gate_up, hidden, d_ffn)
        after = [share]
        share = lax.psum_scatter(share.reshape(-1, share.shape[-1]), ("blk", "fsdp"), scatter_dimension=0, tiled=True)
    else:
        swiglu_grad = plain_sum(dot_at(low_normed, d_gate_up).astype(BF))
        down_grad = plain_sum(dot_at(hidden, d_ffn).astype(BF))
        after = []
    d_branch, d_attended, back_feat, gain1_part = branch_back(
        d_ffn, low_normed, stat, query_feat, d_gate_up, attended, lse_columns, gain1, (outer, swiglu), rows, small_tile,
        after,
    )
    if row_mode:
        d_branch, output_came = tied([d_branch, output_came])
        layer_output = lax.dynamic_slice_in_dim(output, mine * shard_len, shard_len, 0)
        layer_output = in_order([layer_output, output_came], mine)
    part_rows = jnp.arange(width, dtype=jnp.int32) % (width // split)
    losses = jnp.where(part_rows == place, loss if row_mode else loss / split, 0.0)
    losses_high = lax.reduce_precision(losses, 8, 7)
    small = jnp.stack([jnp.sum(gain1_part, 0), jnp.sum(gain2_part, 0), losses_high, losses - losses_high], axis=1)
    small = jnp.pad(small, ((0, 0), (0, LANES - 4))).astype(BF)
    out_sum = Reduction(weight_grad([(attended, d_branch)], small))
    grads, running = [], [out_sum]
    for n in range(PAIRS // BACK_PAIRS):
        columns, _ = beside(
            lambda sent: attend_back(
                query, d_attended, key_all, value_all, key_feat, back_feat, spans_back, tables_q, tables_k, rows,
                BACK_PAIRS, n * BACK_PAIRS, BACK_PAIRS, sent,
            ),
            running,
        )
        if not row_mode:

            def own_part(grad):
                grad = grad.reshape(rows, row_len, -1)
                grad = lax.psum_scatter(grad, "fsdp", scatter_dimension=1, tiled=True)
                return grad.reshape(tokens_here, -1)

            columns = [columns[0], own_part(columns[1]), own_part(columns[2])]
        if fast and n == PAIRS // BACK_PAIRS - 1:
            *columns, share = tied([*columns, share])
            both = lax.all_gather(share, "blk", axis=0)
        grads += columns
        (part,), _ = beside(lambda sent: [weight_grad([(x, g) for g in columns], None, sent)], running)
        running.append(Reduction(part, True))
    qkv_sums = running[1:]
    if row_mode:
        (moved,), _ = beside(
            lambda sent: [
                input_grad_part(d_branch, grads, qkv, (1 - mine) * shard_len, shard_len, BF, small_tile, sent)
            ],
            running,
        )
        exchange = flipped(moved, "fsdp", 1)
        (kept,), _ = beside(
            lambda sent: [
                input_grad_part(d_branch, grads, qkv, mine * shard_len, shard_len, F32, small_tile, sent, True)
            ],
            running,
        )
        for _ in range(2):
            beside(lambda _: [], running)
        kept, exchange = tied([kept, exchange])
        (input_grad,), _ = beside(
            lambda _: [placed(exchange, kept, (1 - mine) * shard_len, small_tile)], running
        )
        input_grad = input_grad.reshape(tokens.shape)
    else:
        input_grad = input_grad_part(d_branch, grads, qkv, 0, tokens_here, F32, small_tile).reshape(tokens.shape)
    if fast:
        (swiglu_grad, down_grad), _ = beside(lambda _: spread(both, width), running)
    while any(not r.done for r in running):
        beside(lambda _: [], running)
    wide, groups = BACK_PAIRS * LANES, PAIRS // BACK_PAIRS
    qkv_columns = [(g, part * wide, wide) for part in range(3) for g in range(groups)]
    (qkv_grad,) = unfold([r.result for r in qkv_sums], [qkv_columns])
    out_grad, small = unfold([out_sum.result], [[(0, 0, width)], [(0, width, LANES)]])
    queries = lax.axis_size("blk") * pairing.shape[0]
    return (
        jnp.sum(small[:, 2:4]) / queries,
        layer_output,
        input_grad,
        qkv_grad,
        out_grad,
        swiglu_grad,
        down_grad,
        small[:, 0],
        small[:, 1],
    )


BACK_PAIRS = 3


def solution(mesh):
    in_specs = (
        P("blk", "fsdp", None),
        P("blk", "fsdp", None),
        P("blk", "fsdp"),
        P("blk", None),
        P("blk", "fsdp"),
        P("blk"),
        P("fsdp", None),
        P("fsdp", None),
        P("fsdp", None),
        P("fsdp", None),
        P("fsdp"),
        P("fsdp"),
    )
    out_specs = (
        P(),
        P("blk", "fsdp", None),
        P("blk", "fsdp", None),
        P("fsdp", None),
        P("fsdp", None),
        P("fsdp", None),
        P("fsdp", None),
        P("fsdp"),
        P("fsdp"),
    )
    return jax.shard_map(shards, mesh=mesh, in_specs=in_specs, out_specs=out_specs, check_vma=False)
```

```python
import functools
import math

import jax
import jax.numpy as jnp
from jax import lax
from jax.experimental import pallas as pl
from jax.experimental.pallas import tpu as pltpu
from jax.sharding import PartitionSpec as P

HEADS = 12
HDIM = 64
PAIRS = HEADS // 2
LANES = 128
SEG = 8

EPSILON = 1e-05
EMB_EPSILON = 1e-06
SOFTMAX_WARMTH = 0.05
ROPE_BASE = 1000.0
CONTRAST_WEIGHT = 512.0
NEGATIVE = -1e30

BF = jnp.bfloat16
F32 = jnp.float32
MIB = 1 << 20
CHEAP = pl.CostEstimate(flops=1024, bytes_accessed=1024, transcendentals=0)


def cost(flops):
    return pl.CostEstimate(flops=4 * flops, bytes_accessed=MIB, transcendentals=0)


def dot(a, b):
    return lax.dot_general(a, b, (((1,), (0,)), ((), ())), preferred_element_type=F32)


def dot_bt(a, b):
    return lax.dot_general(a, b, (((1,), (1,)), ((), ())), preferred_element_type=F32)


def dot_at(a, b):
    return lax.dot_general(a, b, (((0,), (0,)), ((), ())), preferred_element_type=F32)


def lane_iota(shape):
    return lax.broadcasted_iota(jnp.int32, shape, len(shape) - 1)


def halves_swapped(block):
    low = lane_iota(block.shape) % HDIM < HDIM // 2
    return jnp.where(low, pltpu.roll(block, LANES - 32, 1), pltpu.roll(block, 32, 1))


def flipped(block, axis, bit):
    route = [(i, i ^ bit) for i in range(lax.axis_size(axis))]
    return lax.ppermute(block, axis, route)


def take(array, index, dim):
    return lax.dynamic_index_in_dim(array, index, dim, keepdims=False)


class Weight:
    def __init__(self, pieces, offsets, shape):
        self.pieces, self.offsets, self.shape = pieces, offsets, shape


def whole_weight(weight):
    rows, cols = weight.shape
    shape = (rows * lax.axis_size("fsdp"), cols)
    return Weight([lax.all_gather(weight, "fsdp", axis=0, tiled=True)], [(0, 0)], shape)


def half_of(weight, shift):
    half = weight.shape[0] // 2
    return lax.dynamic_slice_in_dim(weight, lax.axis_index("blk") % 2 * half + shift, half, 0)


def from_halves(weight, first):
    rows, cols = weight.shape
    core, mine = lax.axis_index("blk") % 2, lax.axis_index("fsdp")
    second = flipped(first, "blk", 1)
    other = (1 - mine) * rows
    offsets = [
        (mine * rows, 0),
        (other + core * (rows // 2), 0),
        (other + (1 - core) * (rows // 2), 0),
    ]
    return Weight([weight, first, second], offsets, (2 * rows, cols))


def share_of(weight, shift=0):
    share = weight.shape[0] // lax.axis_size("blk")
    return lax.dynamic_slice_in_dim(weight, lax.axis_index("blk") * share + shift, share, 0)


def from_shares(weight, share):
    rows, cols = weight.shape
    mine = lax.axis_index("fsdp")
    other = lax.all_gather(share, "blk", axis=0, tiled=True)
    return Weight([weight, other], [(mine * rows, 0), ((1 - mine) * rows, 0)], (2 * rows, cols))


def as_table(offsets):
    return jnp.stack([jnp.asarray(v, jnp.int32) for pair in offsets for v in pair])


def weight_copies(table, base, pieces, whole, sems):
    copies = []
    for n, piece in enumerate(pieces):
        rows, cols = piece.shape
        row = pl.multiple_of(table[2 * (base + n)], 16)
        col = pl.multiple_of(table[2 * (base + n) + 1], LANES)
        copies.append(
            pltpu.make_async_copy(
                piece, whole.at[pl.ds(row, rows), pl.ds(col, cols)], sems.at[base + n]
            )
        )
    return copies


def grouped_copies(counts, table, pieces, wholes, sems):
    groups, base = [], 1
    for count, whole in zip(counts, wholes):
        groups.append(weight_copies(table, base, pieces[base - 1 : base - 1 + count], whole, sems))
        base += count
    return groups


def start_all(*groups):
    for group in groups:
        for copy in group:
            copy.start()


def wait_all(*groups):
    for group in groups:
        for copy in group:
            copy.wait()


def weight_operands(weights, lead, after=()):
    counts = [len(w.pieces) for w in weights] + [len(after)]
    pieces = [p for w in weights for p in w.pieces]
    table = as_table([lead] + [o for w in weights for o in w.offsets])
    scratch = [pltpu.VMEM(w.shape, BF) for w in weights]
    return counts, pieces + list(after), table, scratch + [pltpu.SemaphoreType.DMA((len(pieces) + 1,))]


def zero_after(array):
    return jnp.minimum(jnp.abs(array[(0,) * array.ndim].astype(F32)), 0.0).astype(jnp.int32)


ANY = pl.BlockSpec(memory_space=pl.ANY)


def params(limit_mib):
    return pltpu.CompilerParams(vmem_limit_bytes=limit_mib * MIB)


def tied_kernel(*refs):
    del refs


def tied(values, after=()):
    if len(values) + len(after) < 2:
        return list(values)
    return pl.pallas_call(
        tied_kernel,
        in_specs=[ANY] * (len(values) + len(after)),
        out_specs=[ANY] * len(values),
        out_shape=[jax.ShapeDtypeStruct(v.shape, v.dtype) for v in values],
        input_output_aliases={n: n for n in range(len(values))},
        cost_estimate=CHEAP,
    )(*values, *after)


def row_specs(parts, tile, width, steps):
    if len(parts) == 1:
        return [pl.BlockSpec((tile, width), lambda r, i, *_: (r * steps + i, 0))]
    half = steps // 2

    def kept(r, i, t):
        return jnp.where(i // half == t[0], i % half, jnp.where(t[0] == 0, half - 1, 0)), 0

    def moved(r, i, t):
        return jnp.where(i // half != t[0], i % half, jnp.where(t[0] == 0, 0, half - 1)), 0

    return [pl.BlockSpec((tile, width), kept), pl.BlockSpec((tile, width), moved)]


def row_tile(table, refs, rows):
    if len(refs) == 1:
        return refs[0][rows]
    own = pl.program_id(1) // (pl.num_programs(1) // 2) == table[0]
    return jnp.where(own, refs[0][rows], refs[1][rows])


def qkv_kernel(counts, old, table, cos_ref, sin_ref, in_ref, *rest):
    pieces, rest = rest[: sum(counts)], rest[sum(counts) + old :]
    q_ref, k_ref, v_ref, x_ref, whole, sems = rest
    width = q_ref.shape[1]

    @pl.when(pl.program_id(0) == 0)
    def _():
        groups = grouped_copies(counts, table, pieces, [whole], sems)
        start_all(*groups)
        wait_all(*groups)

    x = in_ref[...]
    x_ref[...] = x
    cosine, sine = cos_ref[...], sin_ref[...]
    for ref, start, factor in ((q_ref, 0, 1.0 / math.sqrt(HDIM)), (k_ref, width, 1.0)):
        projected = dot(x, whole[:, start : start + width])
        for b in range(0, width, LANES):
            block = projected[:, b : b + LANES]
            turned = block * cosine + halves_swapped(block) * sine
            ref[:, b : b + LANES] = turned.astype(BF) * jnp.asarray(factor, BF)
    v_ref[...] = dot(x, whole[:, 2 * width :]).astype(BF)


def project(x, start, cosine, sine, weight, old, tile, after=()):
    tokens, width = cosine.shape[0], weight.shape[0]
    counts, pieces, table, scratch = weight_operands([weight], (start // tile, 0), after)
    shifted = lambda i, t: (i + t[0], 0)
    narrow, wide = pl.BlockSpec((tile, LANES), shifted), pl.BlockSpec((tile, width), shifted)
    first = 4 + len(pieces)
    return pl.pallas_call(
        functools.partial(qkv_kernel, counts, len(old)),
        grid_spec=pltpu.PrefetchScalarGridSpec(
            num_scalar_prefetch=1,
            grid=(x.shape[0] // tile,),
            in_specs=[narrow, narrow, pl.BlockSpec((tile, width), lambda i, t: (i, 0))] + [ANY] * (len(pieces) + len(old)),
            out_specs=[wide] * 4,
            scratch_shapes=scratch,
        ),
        out_shape=[jax.ShapeDtypeStruct((tokens, width), BF)] * 4,
        input_output_aliases={first + n: n for n in range(len(old))},
        compiler_params=params(48),
        cost_estimate=cost(6 * x.shape[0] * width * width),
    )(table, cosine, sine, x, *pieces, *old)


def input_grad_kernel(counts, groups, table, dbr_ref, *rest):
    grads, rest = rest[: 3 * groups], rest[3 * groups :]
    pieces, (out_ref, whole, sems) = rest[: sum(counts)], rest[sum(counts) :]
    width = dbr_ref.shape[1]

    @pl.when(pl.program_id(0) == 0)
    def _():
        copies = grouped_copies(counts, table, pieces, [whole], sems)
        start_all(*copies)
        wait_all(*copies)

    total = dbr_ref[...].astype(F32)
    for n, ref in enumerate(grads):
        wide = ref.shape[1]
        start = n % 3 * width + n // 3 * wide
        total += dot_bt(ref[...], whole[:, start : start + wide])
    out_ref[...] = total.astype(out_ref.dtype)


def input_grad_part(dbr, grads, weight, start, tokens, dtype, tile, after=(), whole=False):
    width = dbr.shape[1]
    counts, pieces, table, scratch = weight_operands([weight], (start // tile, 0), after)
    shifted = lambda i, t: (i + t[0], 0)
    return pl.pallas_call(
        functools.partial(input_grad_kernel, counts, len(grads) // 3),
        grid_spec=pltpu.PrefetchScalarGridSpec(
            num_scalar_prefetch=1,
            grid=(tokens // tile,),
            in_specs=[pl.BlockSpec((tile, width), shifted)]
            + [pl.BlockSpec((tile, g.shape[1]), shifted) for g in grads]
            + [ANY] * len(pieces),
            out_specs=pl.BlockSpec((tile, width), shifted if whole else lambda i, t: (i, 0)),
            scratch_shapes=scratch,
        ),
        out_shape=jax.ShapeDtypeStruct((dbr.shape[0] if whole else tokens, width), dtype),
        compiler_params=params(48),
        cost_estimate=cost(6 * tokens * width * width),
    )(table, dbr, *grads, *pieces)


def place_kernel(table, in_ref, old_ref, out_ref):
    del table, old_ref
    out_ref[...] = in_ref[...].astype(out_ref.dtype)


def placed(part, array, start, tile):
    rows, width = part.shape
    return pl.pallas_call(
        place_kernel,
        grid_spec=pltpu.PrefetchScalarGridSpec(
            num_scalar_prefetch=1,
            grid=(rows // tile,),
            in_specs=[pl.BlockSpec((tile, width), lambda i, t: (i, 0)), ANY],
            out_specs=pl.BlockSpec((tile, width), lambda i, t: (i + t[0], 0)),
        ),
        out_shape=jax.ShapeDtypeStruct(array.shape, array.dtype),
        input_output_aliases={2: 0},
        cost_estimate=CHEAP,
    )((start // tile).astype(jnp.int32).reshape(1), part, array)


BQ = 256
BK_FWD = 512
BK_BACK = 256
VROWS = HDIM + 16


def lanes_where(condition):
    return jnp.where(condition(lane_iota((1, LANES))), 1.0, 0.0).astype(BF)


def spread_pairs(whole, source, features, group):
    for g in range(group):
        whole[:, 2 * g * LANES : (2 * g + 1) * LANES] = source[:, g * LANES : (g + 1) * LANES]
        whole[:, (2 * g + 1) * LANES : (2 * g + 2) * LANES] = features[...]


def staggered(count, load, work, finish):
    loaded, worked = load(0), None
    for g in range(count):
        ahead = load(g + 1) if g + 1 < count else None
        result = work(g, loaded)
        if worked is not None:
            finish(g - 1, worked)
        worked, loaded = result, ahead
    finish(count - 1, worked)


def attend_kernel(group, extra, spans, q_ref, k_ref, v_ref, kf_ref, qf_ref, *rest):
    o_ref, lse_ref, kx, vt, qx, best, accum = rest[extra:]
    block = pl.program_id(2)
    where = (pl.program_id(0) * pl.num_programs(2) + block) * 2
    row_len = k_ref.shape[0]

    @pl.when(block == 0)
    def _():
        spread_pairs(kx, k_ref, kf_ref, group)
        for g in range(group):
            for b in range(0, row_len, 256):
                turned = v_ref[b : b + 256, g * LANES : (g + 1) * LANES].astype(F32).T.astype(BF)
                for h in range(2):
                    vt[2 * g + h, :HDIM, b : b + 256] = turned[h * HDIM : (h + 1) * HDIM]
                    vt[2 * g + h, HDIM:, b : b + 256] = jnp.ones((16, 256), BF)

    qf = qf_ref[...]
    even, odd = lanes_where(lambda lane: lane < HDIM), lanes_where(lambda lane: lane >= HDIM)
    for g in range(group):
        q = q_ref[:, g * LANES : (g + 1) * LANES]
        qx[g, :BQ, :LANES] = q * even
        qx[g, BQ:, :LANES] = q * odd
        qx[g, :BQ, LANES:] = qf
        qx[g, BQ:, LANES:] = qf
    best[...] = jnp.full_like(best, NEGATIVE)
    accum[...] = jnp.zeros_like(accum)
    first, count = spans[where], spans[where + 1]

    def step(j, state):
        at = pl.multiple_of(first + j * BK_FWD, LANES)

        def load(g):
            return dot_bt(kx[pl.ds(at, BK_FWD), 2 * g * LANES : 2 * (g + 1) * LANES], qx[g])

        def work(g, scores):
            old = best[g]
            new = jnp.maximum(old, jnp.max(scores, axis=0, keepdims=True))
            best[g] = new
            return jnp.exp(scores - new).astype(BF), jnp.exp(old - new)

        def finish(g, worked):
            soft, factor = worked
            for h in range(2):
                cols = slice(h * BQ, (h + 1) * BQ)
                values = vt[2 * g + h, :, pl.ds(at, BK_FWD)]
                accum[g, :, cols] = accum[g, :, cols] * factor[:, cols] + dot(values, soft[:, cols])

        staggered(group, load, work, finish)
        return state

    lax.fori_loop(0, count, step, 0)
    for g in range(group):
        total = accum[g, HDIM : HDIM + 1]
        lse = best[g] + jnp.log(total)
        lse_ref[2 * g] = lse[:, :BQ]
        lse_ref[2 * g + 1] = lse[:, BQ:]
        turned = accum[g, :HDIM] / total
        turned = jnp.concatenate([turned[:, :BQ], turned[:, BQ:]], axis=0)
        o_ref[:, g * LANES : (g + 1) * LANES] = turned.T.astype(BF)


def attend(q, k, v, key_feat, query_feat, spans, rows, group, after=()):
    tokens, width = q.shape
    row_len = k.shape[0] // rows
    blocks = tokens // rows // BQ
    of_q = lambda r, p, i, *_: (r * blocks + i, p)
    of_k = lambda r, p, i, *_: (r, p)
    wide = group * LANES
    return pl.pallas_call(
        functools.partial(attend_kernel, group, len(after)),
        grid_spec=pltpu.PrefetchScalarGridSpec(
            num_scalar_prefetch=1,
            grid=(rows, PAIRS // group, blocks),
            in_specs=[
                pl.BlockSpec((BQ, wide), of_q),
                pl.BlockSpec((row_len, wide), of_k),
                pl.BlockSpec((row_len, wide), of_k),
                pl.BlockSpec((row_len, LANES), lambda r, p, i, *_: (r, 0)),
                pl.BlockSpec((BQ, LANES), lambda r, p, i, *_: (r * blocks + i, 0)),
            ]
            + [ANY] * len(after),
            out_specs=[
                pl.BlockSpec((BQ, wide), of_q),
                pl.BlockSpec((2 * group, 1, BQ), lambda r, p, i, *_: (p, 0, r * blocks + i)),
            ],
            scratch_shapes=[
                pltpu.VMEM((row_len, 2 * wide), BF),
                pltpu.VMEM((2 * group, VROWS, row_len), BF),
                pltpu.VMEM((group, 2 * BQ, 2 * LANES), BF),
                pltpu.VMEM((group, 1, 2 * BQ), F32),
                pltpu.VMEM((group, VROWS, 2 * BQ), F32),
            ],
        ),
        out_shape=[
            jax.ShapeDtypeStruct((tokens, width), BF),
            jax.ShapeDtypeStruct((HEADS, 1, tokens), F32),
        ],
        compiler_params=params(56),
        cost_estimate=cost(4 * tokens * row_len * width),
    )(spans, q, k, v, key_feat, query_feat, *after)


def attend_back_kernel(
    group, base, extra, spans, q_ref, do_ref, k_ref, v_ref, kf_ref, qf_ref, cq_ref, sq_ref, ck_ref, sk_ref, *rest,
):
    dq_ref, dk_ref, dv_ref, kx, vx, kt, qx, dox, dq_acc, dk_acc, dv_acc = rest[extra:]
    block = pl.program_id(2)
    pair = base + pl.program_id(1) * group
    where = (pl.program_id(0) * pl.num_programs(2) + block) * 2
    row_len = k_ref.shape[0]

    @pl.when(block == 0)
    def _():
        spread_pairs(kx, k_ref, kf_ref, group)
        spread_pairs(vx, v_ref, kf_ref, group)
        for g in range(group):
            for b in range(0, row_len, 256):
                turned = k_ref[b : b + 256, g * LANES : (g + 1) * LANES].astype(F32).T.astype(BF)
                kt[g * LANES : (g + 1) * LANES, b : b + 256] = turned
        dk_acc[...] = jnp.zeros_like(dk_acc)
        dv_acc[...] = jnp.zeros_like(dv_acc)

    qf = qf_ref[...]
    even, odd = lanes_where(lambda lane: lane < HDIM), lanes_where(lambda lane: lane >= HDIM)
    for g in range(group):
        cols = slice(g * LANES, (g + 1) * LANES)
        for whole, source in ((qx, q_ref[:, cols]), (dox, do_ref[:, cols])):
            whole[g, :BQ, :LANES] = source * even
            whole[g, BQ:, :LANES] = source * odd
        for h in range(2):
            head = 2 * (pair + g) + h

            def at(lane, starts):
                return functools.reduce(jnp.logical_or, [lane == start + head for start in starts])

            of_lse = lanes_where(lambda lane: (lane < SEG) | at(lane, (8, 20, 32)))
            of_delta = lanes_where(lambda lane: at(lane, (44, 56, 68)))
            qx[g, h * BQ : (h + 1) * BQ, LANES:] = qf * of_lse
            dox[g, h * BQ : (h + 1) * BQ, LANES:] = qf * of_delta
    dq_acc[...] = jnp.zeros_like(dq_acc)
    first, count = spans[where], spans[where + 1]

    def step(j, state):
        at = pl.multiple_of(first + j * BK_BACK, LANES)

        def load(g):
            twice = slice(2 * g * LANES, (2 * g + 2) * LANES)
            return dot_bt(kx[pl.ds(at, BK_BACK), twice], qx[g]), dot_bt(vx[pl.ds(at, BK_BACK), twice], dox[g])

        def work(g, loaded):
            probs = jnp.exp(loaded[0])
            return probs.astype(BF), (probs * loaded[1]).astype(BF)

        def finish(g, worked):
            probs, grad = worked
            cols = slice(g * LANES, (g + 1) * LANES)
            dv_acc[pl.ds(at, BK_BACK), cols] += dot(probs, dox[g, :, :LANES])
            dk_acc[pl.ds(at, BK_BACK), cols] += dot(grad, qx[g, :, :LANES])
            for h in range(2):
                rows = slice(g * LANES + h * HDIM, g * LANES + (h + 1) * HDIM)
                dq_acc[rows] += dot(kt[rows, pl.ds(at, BK_BACK)], grad[:, h * BQ : (h + 1) * BQ])

        staggered(group, load, work, finish)
        return state

    lax.fori_loop(0, count, step, 0)
    for g in range(group):
        cols = slice(g * LANES, (g + 1) * LANES)
        dq = dq_acc[cols].T * (1.0 / math.sqrt(HDIM))
        dq_ref[:, cols] = (dq * cq_ref[...] - halves_swapped(dq) * sq_ref[...]).astype(BF)

    @pl.when(block == pl.num_programs(2) - 1)
    def _():
        for b in range(0, row_len, 256):
            part = pl.ds(b, 256)
            cosine, sine = ck_ref[part, :], sk_ref[part, :]
            for g in range(group):
                cols = slice(g * LANES, (g + 1) * LANES)
                dk = dk_acc[part, cols]
                dk_ref[part, cols] = (dk * cosine - halves_swapped(dk) * sine).astype(BF)
            dv_ref[part, :] = dv_acc[part, :].astype(BF)


def attend_back(q, do, k, v, key_feat, query_feat, spans, tables_q, tables_k, rows, group, base, pairs, after=()):
    tokens, width = q.shape
    row_len = k.shape[0] // rows
    blocks = tokens // rows // BQ
    start = base // group
    of_q = lambda r, p, i, *_: (r * blocks + i, start + p)
    of_k = lambda r, p, i, *_: (r, start + p)
    per_q = pl.BlockSpec((BQ, LANES), lambda r, p, i, *_: (r * blocks + i, 0))
    per_k = pl.BlockSpec((row_len, LANES), lambda r, p, i, *_: (r, 0))
    wide = group * LANES
    return pl.pallas_call(
        functools.partial(attend_back_kernel, group, base, len(after)),
        grid_spec=pltpu.PrefetchScalarGridSpec(
            num_scalar_prefetch=1,
            grid=(rows, pairs // group, blocks),
            in_specs=[
                pl.BlockSpec((BQ, wide), of_q),
                pl.BlockSpec((BQ, wide), of_q),
                pl.BlockSpec((row_len, wide), of_k),
                pl.BlockSpec((row_len, wide), of_k),
                per_k,
                per_q,
                per_q,
                per_q,
                per_k,
                per_k,
            ]
            + [ANY] * len(after),
            out_specs=[
                pl.BlockSpec((BQ, wide), lambda r, p, i, *_: (r * blocks + i, p)),
                pl.BlockSpec((row_len, wide), lambda r, p, i, *_: (r, p)),
                pl.BlockSpec((row_len, wide), lambda r, p, i, *_: (r, p)),
            ],
            scratch_shapes=[
                pltpu.VMEM((row_len, 2 * wide), BF),
                pltpu.VMEM((row_len, 2 * wide), BF),
                pltpu.VMEM((wide, row_len), BF),
                pltpu.VMEM((group, 2 * BQ, 2 * LANES), BF),
                pltpu.VMEM((group, 2 * BQ, 2 * LANES), BF),
                pltpu.VMEM((wide, BQ), F32),
                pltpu.VMEM((row_len, wide), F32),
                pltpu.VMEM((row_len, wide), F32),
            ],
        ),
        out_shape=[
            jax.ShapeDtypeStruct((tokens, pairs * LANES), BF),
            jax.ShapeDtypeStruct((rows * row_len, pairs * LANES), BF),
            jax.ShapeDtypeStruct((rows * row_len, pairs * LANES), BF),
        ],
        compiler_params=params(56),
        cost_estimate=cost(8 * tokens * row_len * pairs * LANES),
    )(spans, q, do, k, v, key_feat, query_feat, *tables_q, *tables_k, *after)


FF_CHUNK = 512
SUB = 256


def normalize(hidden):
    average = jnp.mean(hidden, -1, keepdims=True)
    centred = hidden - average
    inverse = lax.rsqrt(jnp.mean(centred * centred, -1, keepdims=True) + EPSILON)
    return centred * inverse, inverse


def norm_back(scaled, normalized, inverse):
    return inverse * (
        scaled
        - jnp.mean(scaled, -1, keepdims=True)
        - normalized * jnp.mean(scaled * normalized, -1, keepdims=True)
    )


def split_two(value):
    high = value.astype(BF)
    return high, (value - high.astype(F32)).astype(BF)


def mix_kernel(counts, table, att_ref, x_ref, qf_ref, g1_ref, g2_ref, *rest):
    pieces, rest = rest[: sum(counts)], rest[sum(counts) :]
    nl_ref, stat_ref, hid_ref, fg_ref, fu_ref, out_ref, pool_ref, wo, ws, wd, sems = rest
    groups = grouped_copies(counts, table, pieces, (wo, ws, wd), sems)
    step, begin = pl.program_id(1), (pl.program_id(0) == 0) & (pl.program_id(1) == 0)

    @pl.when(begin)
    def _():
        start_all(*groups)
        wait_all(*groups)

    ff = wd.shape[0]
    tile, chunks = att_ref.shape[0], wd.shape[0] // FF_CHUNK
    subs, opened, pools = tile // SUB, [], []
    lanes = lane_iota((SUB, LANES))

    def open_next():
        rows = slice(len(opened) * SUB, (len(opened) + 1) * SUB)
        branch = dot(att_ref[rows], wo[...])
        unit, inverse1 = normalize(x_ref[rows].astype(F32) + branch)
        normed = unit * g1_ref[...]
        low = normed.astype(BF)
        nl_ref[rows] = low
        opened.append([low, normed, inverse1, rows])

    def close(sub):
        _, hidden_sum, inverse1, rows = opened[sub]
        unit2, inverse2 = normalize(hidden_sum)
        output = unit2 * g2_ref[...]
        out_ref[rows] = output.astype(BF)
        stat_ref[rows] = jnp.where(lanes == 0, inverse1, inverse2)
        high, rest_low = split_two(output)
        member = qf_ref[rows]
        pools.append((dot_at(member, high) + dot_at(member, rest_low))[:SEG])

    def load(n):
        low, c = opened[n // chunks][0], n % chunks
        cols = slice(c * FF_CHUNK, (c + 1) * FF_CHUNK)
        return dot(low, ws[:, cols]), dot(low, ws[:, ff + c * FF_CHUNK : ff + (c + 1) * FF_CHUNK])

    def work(n, loaded):
        sub, c = n // chunks, n % chunks
        if c == 1 and sub + 1 < subs:
            open_next()
        if c == 2 and sub > 0:
            close(sub - 1)
        rows, cols = opened[sub][3], slice(c * FF_CHUNK, (c + 1) * FF_CHUNK)
        gate, up = loaded
        sig = 0.5 + 0.5 * jnp.tanh(0.5 * gate)
        silu = gate * sig
        hidden = (silu * up).astype(BF)
        hid_ref[rows, cols] = hidden
        fg_ref[rows, cols] = (up * (sig + silu * (1.0 - sig))).astype(BF)
        fu_ref[rows, cols] = silu.astype(BF)
        return hidden

    def finish(n, hidden):
        c = n % chunks
        opened[n // chunks][1] = opened[n // chunks][1] + dot(hidden, wd[c * FF_CHUNK : (c + 1) * FF_CHUNK, :])

    open_next()
    staggered(subs * chunks, load, work, finish)
    close(subs - 1)
    sums = functools.reduce(jnp.add, pools)

    @pl.when(step == 0)
    def _():
        pool_ref[0] = sums

    @pl.when(step > 0)
    def _():
        pool_ref[0] += sums


def mix(attended, x, query_feat, gain1, gain2, weights, rows, tile, after):
    tokens, width = x.shape
    steps = tokens // rows // tile
    ff = weights[2].shape[0]
    counts, pieces, table, scratch = weight_operands(weights, (0, 0), after)
    wide, narrow = row_specs([None], tile, width, steps), row_specs([None], tile, LANES, steps)
    hidden, fixed = row_specs([None], tile, ff, steps), [pl.BlockSpec((1, width), lambda r, i, *_: (0, 0))]
    return pl.pallas_call(
        functools.partial(mix_kernel, counts),
        grid_spec=pltpu.PrefetchScalarGridSpec(
            num_scalar_prefetch=1,
            grid=(rows, steps),
            in_specs=wide * 2 + narrow + fixed * 2 + [ANY] * len(pieces),
            out_specs=wide + narrow + hidden * 3 + wide + [pl.BlockSpec((1, SEG, width), lambda r, i, *_: (r, 0, 0))],
            scratch_shapes=scratch,
        ),
        out_shape=[
            jax.ShapeDtypeStruct((tokens, width), BF),
            jax.ShapeDtypeStruct((tokens, LANES), F32),
            jax.ShapeDtypeStruct((tokens, ff), BF),
            jax.ShapeDtypeStruct((tokens, ff), BF),
            jax.ShapeDtypeStruct((tokens, ff), BF),
            jax.ShapeDtypeStruct((tokens, width), BF),
            jax.ShapeDtypeStruct((rows, SEG, width), F32),
        ],
        compiler_params=params(58),
        cost_estimate=cost(2 * tokens * width * (width + 3 * ff)),
    )(table, attended, x, query_feat, gain1, gain2, *pieces)


def hidden_back_kernel(counts, parts, table, *rest):
    cot_refs, rest = rest[:parts], rest[parts:]
    out_ref, stat_ref, qf_ref, dp_ref, fg_ref, fu_ref, g2_ref = rest[:7]
    pieces, rest = rest[7 : 7 + sum(counts)], rest[7 + sum(counts) :]
    dffn_ref, dgu_ref, gf_ref, wd, sems = rest
    groups = grouped_copies(counts, table, pieces, [wd], sems)
    begin = (pl.program_id(0) == 0) & (pl.program_id(1) == 0)

    @pl.when(begin)
    def _():
        start_all(*groups)
        gf_ref[...] = jnp.zeros_like(gf_ref)

    gain2 = g2_ref[...]
    high, rest_low = split_two(dp_ref[0])
    tile, width = out_ref.shape
    ff = wd.shape[0]
    subs, chunks, opened = tile // SUB, ff // FF_CHUNK, []

    def open_next():
        rows = slice(len(opened) * SUB, (len(opened) + 1) * SUB)
        member = qf_ref[rows]
        upstream = row_tile(table, cot_refs, rows).astype(F32) + dot(member, high) + dot(member, rest_low)
        unit2 = out_ref[rows].astype(F32) / gain2
        dffn = norm_back(upstream * gain2, unit2, stat_ref[rows, 1:2]).astype(BF)
        dffn_ref[rows] = dffn
        gf_ref[...] += jnp.sum((upstream * unit2).reshape(SUB // 8, 8, width), axis=0)
        opened.append((dffn, rows))

    def load(n):
        c = n % chunks
        return dot_bt(opened[n // chunks][0], wd[c * FF_CHUNK : (c + 1) * FF_CHUNK, :])

    def work(n, dhid):
        sub, c = n // chunks, n % chunks
        if c == 1 and sub + 1 < subs:
            open_next()
        rows, cols = opened[sub][1], slice(c * FF_CHUNK, (c + 1) * FF_CHUNK)
        dgu_ref[rows, cols] = (dhid * fg_ref[rows, cols].astype(F32)).astype(BF)
        after = slice(ff + c * FF_CHUNK, ff + (c + 1) * FF_CHUNK)
        dgu_ref[rows, after] = (dhid * fu_ref[rows, cols].astype(F32)).astype(BF)

    open_next()

    @pl.when(begin)
    def _():
        wait_all(*groups)

    staggered(subs * chunks, load, work, lambda n, worked: None)


def hidden_back(cots, lead, output, stat, query_feat, dpool, factors, gain2, down, rows, tile):
    tokens, width = output.shape
    ff = down.shape[0]
    steps = tokens // rows // tile
    counts, pieces, table, scratch = weight_operands([down], (lead, 0))
    wide, narrow = row_specs([None], tile, width, steps), row_specs([None], tile, LANES, steps)
    hidden = row_specs([None], tile, ff, steps)
    return pl.pallas_call(
        functools.partial(hidden_back_kernel, counts, len(cots)),
        grid_spec=pltpu.PrefetchScalarGridSpec(
            num_scalar_prefetch=1,
            grid=(rows, steps),
            in_specs=row_specs(cots, tile, width, steps)
            + wide
            + narrow * 2
            + [pl.BlockSpec((1, LANES, width), lambda r, i, *_: (r, 0, 0))]
            + hidden * 2
            + [pl.BlockSpec((1, width), lambda r, i, *_: (0, 0))]
            + [ANY] * len(pieces),
            out_specs=wide + row_specs([None], tile, 2 * ff, steps) + [pl.BlockSpec((8, width), lambda r, i, *_: (0, 0))],
            scratch_shapes=scratch,
        ),
        out_shape=[
            jax.ShapeDtypeStruct((tokens, width), BF),
            jax.ShapeDtypeStruct((tokens, 2 * ff), BF),
            jax.ShapeDtypeStruct((8, width), F32),
        ],
        compiler_params=params(58),
        cost_estimate=cost(4 * tokens * width * ff),
    )(table, *cots, output, stat, query_feat, dpool, *factors, gain2, *pieces)


def branch_back_kernel(counts, table, *refs):
    dffn_ref, nl_ref, stat_ref, qf_ref, dgu_ref, att_ref, lse_ref, g1_ref, head_ref = refs[:9]
    rest = refs[9:]
    pieces, rest = rest[: sum(counts)], rest[sum(counts) :]
    dbr_ref, datt_ref, feat_ref, ga_ref, wo, ws, sems = rest
    groups = grouped_copies(counts, table, pieces, (wo, ws), sems)
    begin = (pl.program_id(0) == 0) & (pl.program_id(1) == 0)

    @pl.when(begin)
    def _():
        start_all(*groups)
        ga_ref[...] = jnp.zeros_like(ga_ref)
        wait_all(*groups)

    gain1, heads = g1_ref[...], head_ref[...]
    width = nl_ref.shape[1]
    rows_of = lambda n: slice(n * SUB, (n + 1) * SUB)

    def load(n):
        rows = rows_of(n)
        return dffn_ref[rows].astype(F32) + dot_bt(dgu_ref[rows], ws[...])

    def work(n, dnormed):
        rows = rows_of(n)
        unit1 = nl_ref[rows].astype(F32) / gain1
        dbr = norm_back(dnormed * gain1, unit1, stat_ref[rows, 0:1]).astype(BF)
        dbr_ref[rows] = dbr
        ga_ref[...] += jnp.sum((dnormed * unit1).reshape(SUB // 8, 8, width), axis=0)
        return dbr

    def finish(n, dbr):
        rows = rows_of(n)
        datt = dot_bt(dbr, wo[...]).astype(BF)
        datt_ref[rows] = datt
        high, rest_low = split_two(datt.astype(F32) * att_ref[rows].astype(F32))
        delta = dot(high, heads) + dot(rest_low, heads)
        feat = qf_ref[rows].astype(F32)
        for value, start in ((lse_ref[rows], 8), (delta, 44)):
            left = -value
            for part_n in range(3):
                part = left.astype(BF).astype(F32)
                left = left - part
                feat = feat + pltpu.roll(part, start + HEADS * part_n, 1)
        feat_ref[rows] = feat.astype(BF)

    staggered(dgu_ref.shape[0] // SUB, load, work, finish)


def branch_back(dffn, low, stat, query_feat, dgu, attended, lse, gain1, weights, rows, tile, after=()):
    tokens, width = low.shape
    ff = dgu.shape[1] // 2
    steps = tokens // rows // tile
    counts, pieces, table, scratch = weight_operands(weights, (0, 0), after)
    wide, narrow = row_specs([None], tile, width, steps), row_specs([None], tile, LANES, steps)
    hidden = row_specs([None], tile, 2 * ff, steps)
    heads = (jnp.arange(width)[:, None] // HDIM == jnp.arange(LANES)[None, :]).astype(BF)
    return pl.pallas_call(
        functools.partial(branch_back_kernel, counts),
        grid_spec=pltpu.PrefetchScalarGridSpec(
            num_scalar_prefetch=1,
            grid=(rows, steps),
            in_specs=wide * 2
            + narrow * 2
            + hidden
            + wide
            + narrow
            + [pl.BlockSpec((1, width), lambda r, i, *_: (0, 0))]
            + [pl.BlockSpec((width, LANES), lambda r, i, *_: (0, 0))]
            + [ANY] * len(pieces),
            out_specs=wide * 2 + narrow + [pl.BlockSpec((8, width), lambda r, i, *_: (0, 0))],
            scratch_shapes=scratch,
        ),
        out_shape=[
            jax.ShapeDtypeStruct((tokens, width), BF),
            jax.ShapeDtypeStruct((tokens, width), BF),
            jax.ShapeDtypeStruct((tokens, LANES), BF),
            jax.ShapeDtypeStruct((8, width), F32),
        ],
        compiler_params=params(58),
        cost_estimate=cost(2 * tokens * width * (width + 2 * ff)),
    )(table, dffn, low, stat, query_feat, dgu, attended, lse, gain1, heads, *pieces)


def bits_of(axis):
    size, bit = lax.axis_size(axis), 1
    while bit < size:
        yield bit
        bit *= 2


def in_order(parts, index):
    shape = (2,) + (1,) * parts[0].ndim
    first = lax.broadcasted_iota(jnp.int32, shape, 0) == index
    return jnp.where(first, parts[0][None], parts[1][None])


def add(first, *others):
    total = first.astype(F32)
    for other in others:
        total = total + other.astype(F32)
    return total.astype(BF)


def reduction(part, short):
    rows, cols = part.shape
    shards = lax.axis_size("fsdp")
    mine, place = lax.axis_index("fsdp"), lax.axis_index("blk")
    core, side = place % 2, place // 2 % 2
    now = part.reshape(shards, 2, rows // shards // 2, cols)
    (came,) = yield [take(now, 1 - core, 1)], [("blk", 1)]
    now = add(take(now, core, 1), came)
    bit = shards // 2
    while bit:
        now = now.reshape(2, bit, -1, cols)
        own = mine // bit % 2
        (came,) = yield [take(now, 1 - own, 0)], [("fsdp", bit)]
        now = add(take(now, own, 0), came)
        bit //= 2
    now = now.reshape(2, -1, cols)
    (came,) = yield [take(now, 1 - side, 0)], [("blk", 2)]
    now = add(take(now, side, 0), came)
    bits = [bit for bit in bits_of("blk") if bit > 2]
    if short:
        for bit in bits:
            (came,) = yield [now], [("blk", bit)]
            now = add(now, came)
    else:
        for bit in bits:
            now = now.reshape(2, -1, cols)
            own = place // bit % 2
            (came,) = yield [take(now, 1 - own, 0)], [("blk", bit)]
            now = add(take(now, own, 0), came)
        for bit in bits[::-1]:
            (came,) = yield [now], [("blk", bit)]
            now = in_order([now, came], place // bit % 2).reshape(-1, cols)
    now = now.reshape(-1, cols)
    (came,) = yield [now], [("blk", 2)]
    now = in_order([now, came], side).reshape(-1, cols)
    (came,) = yield [now], [("blk", 1)]
    yield [now, came], None


class Reduction:
    def __init__(self, part, short=False):
        fsdp_bits, lines = len(list(bits_of("fsdp"))), len(list(bits_of("blk"))) - 2
        self.left = 4 + fsdp_bits + lines * (1 if short else 2)
        self.stages = reduction(part, short)
        self.sends, self.routes = next(self.stages)

    @property
    def done(self):
        return self.routes is None

    @property
    def result(self):
        return self.sends

    def launch(self):
        came = [flipped(a, *route) for a, route in zip(self.sends, self.routes)]
        return self.sends, came

    def take_in(self, came):
        self.left -= 1
        self.sends, self.routes = self.stages.send(came)


def beside(work, launches, joins=None):
    sent, flights = [], []
    for r in launches:
        if not r.done:
            sends, came = r.launch()
            sent += sends
            flights.append((r, came))
    values = list(work(sent))
    late = []
    if joins is not None:
        late = [f for f in flights if f[0] not in [j for j in joins if isinstance(j, Reduction)]]
        flights = [f for f in flights if f not in late] + [j for j in joins if not isinstance(j, Reduction)]
    count = len(values)
    both = tied(values + [a for _, came in flights for a in came])
    at = count
    for r, came in flights:
        r.take_in(both[at : at + len(came)])
        at += len(came)
    return both[:count], late


def turned(block):
    return block.astype(F32).T.astype(BF)


def swiglu_part_kernel(low_ref, grad_ref, out_ref, low_turned):
    tokens = low_ref.shape[0]

    @pl.when(pl.program_id(0) == 0)
    def _():
        for b in range(0, tokens, 256):
            low_turned[:, b : b + 256] = turned(low_ref[b : b + 256, :])

    part = dot(low_turned[...], grad_ref[...]).astype(BF)
    taken, split, rows, cols = out_ref.shape
    for n in range(taken):
        for f in range(split):
            out_ref[n, f] = part[f * rows : (f + 1) * rows, n * cols : (n + 1) * cols]


def down_part_kernel(hidden_ref, dffn_ref, old_ref, out_ref):
    del old_ref
    part = dot(turned(hidden_ref[...]), dffn_ref[...]).astype(BF)
    rows, cols = out_ref.shape[2:]
    across = part.shape[1] // cols
    for n in range(out_ref.shape[0]):
        down, along = n // across * rows, n % across * cols
        out_ref[n, 0] = part[down : down + rows, along : along + cols]


def shares_fit(low, hidden):
    blocks, split = lax.axis_size("blk"), lax.axis_size("fsdp")
    width, ff = low.shape[1], hidden.shape[1]
    cols = 2 * ff // blocks
    return cols % LANES == 0 and width % cols == 0 and ff * width // (split * blocks * cols) * 2 == width // split


def feed_forward_shares(low, d_gate_up, hidden, d_ffn):
    blocks, split = lax.axis_size("blk"), lax.axis_size("fsdp")
    tokens, width = low.shape
    ff = hidden.shape[1]
    cols, rows = 2 * ff // blocks, width // split
    down_rows = rows // 2
    across = width // cols
    shape = jax.ShapeDtypeStruct((blocks, split, rows + down_rows, cols), BF)
    whole = lambda a: pl.BlockSpec(a.shape, lambda *_: (0, 0))
    shares = pl.pallas_call(
        swiglu_part_kernel,
        grid=(blocks // 2,),
        in_specs=[whole(low), pl.BlockSpec((tokens, 2 * cols), lambda j: (0, j))],
        out_specs=pl.BlockSpec((2, split, rows, cols), lambda j: (j, 0, 0, 0)),
        out_shape=shape,
        scratch_shapes=[pltpu.VMEM((width, tokens), BF)],
        compiler_params=params(48),
        cost_estimate=cost(4 * tokens * width * ff),
    )(low, d_gate_up)
    taken = 2 * down_rows
    steps = ff // split // taken
    return pl.pallas_call(
        down_part_kernel,
        grid=(split, steps),
        in_specs=[pl.BlockSpec((tokens, taken), lambda f, j: (0, f * steps + j)), whole(d_ffn), ANY],
        out_specs=pl.BlockSpec((2 * across, 1, down_rows, cols), lambda f, j: (j, f, 2, 0)),
        out_shape=shape,
        input_output_aliases={2: 0},
        compiler_params=params(48),
        cost_estimate=cost(2 * tokens * width * ff),
    )(hidden, d_ffn, shares)


def plain_sum(part):
    part = lax.psum_scatter(part, "fsdp", scatter_dimension=0, tiled=True)
    return lax.psum(part, "blk").astype(F32)


def weight_grad(pairs, beside_it=None, after=()):
    arrays, left = [], []
    for a, b in pairs:
        place = [n for n, other in enumerate(arrays) if other is a]
        if not place:
            arrays.append(a)
            place = [len(arrays) - 1]
        arrays.append(b)
        left.append((place[0], len(arrays) - 1))
    cols = sum(b.shape[1] for _, b in pairs)
    last = []
    if beside_it is not None:
        last = [beside_it]
        cols += beside_it.shape[1]

    def kernel(*refs):
        out_ref, at = refs[-1], 0
        for a, b in left:
            part = dot_at(refs[a][...], refs[b][...]).astype(BF)
            out_ref[:, at : at + part.shape[1]] = part
            at += part.shape[1]
        if last:
            out_ref[:, at:] = refs[len(arrays)][...]

    whole = pl.BlockSpec(memory_space=pltpu.VMEM)
    return pl.pallas_call(
        kernel,
        in_specs=[whole] * (len(arrays) + len(last)) + [ANY] * len(after),
        out_shape=jax.ShapeDtypeStruct((pairs[0][0].shape[1], cols), BF),
        compiler_params=params(56),
        cost_estimate=cost(2 * pairs[0][0].shape[0] * pairs[0][0].shape[1] * cols),
    )(*arrays, *last, *after)


def unfold_kernel(kinds, columns, table, *refs):
    own = pl.program_id(0) == table[0]
    values, at = [], 0
    for kind in kinds:
        values.append(refs[at][...] if kind == 1 else jnp.where(own, refs[at][...], refs[at + 1][...]))
        at += kind
    for ref, parts in zip(refs[at:], columns):
        to = 0
        for n, start, wide in parts:
            ref[:, to : to + wide] = values[n][:, start : start + wide].astype(F32)
            to += wide


def unfold(results, columns):
    rows = sum(a.shape[0] for a in results[0]) // 2
    block = rows // 2 if rows % 32 == 0 else rows
    steps = rows // block
    maps = {2: lambda c, i, t: (i, 0), 1: lambda c, i, t: (c * steps + i, 0)}
    return pl.pallas_call(
        functools.partial(unfold_kernel, [len(r) for r in results], columns),
        grid_spec=pltpu.PrefetchScalarGridSpec(
            num_scalar_prefetch=1,
            grid=(2, steps),
            in_specs=[pl.BlockSpec((block, a.shape[1]), maps[len(r)]) for r in results for a in r],
            out_specs=[pl.BlockSpec((block, sum(p[2] for p in parts)), maps[1]) for parts in columns],
        ),
        out_shape=[jax.ShapeDtypeStruct((2 * rows, sum(p[2] for p in parts)), F32) for parts in columns],
        compiler_params=params(40),
        cost_estimate=CHEAP,
    )((lax.axis_index("blk") % 2).reshape(1), *[a for r in results for a in r])


def spread_kernel(both_ref, swiglu_ref, down_ref):
    rows = swiglu_ref.shape[0]
    swiglu_ref[...] = both_ref[0, :rows, :].astype(F32)
    down_ref[...] = both_ref[0, rows:, :].astype(F32)


def spread(both, width):
    blocks, height, cols = both.shape
    rows = height * 2 // 3
    across = width // cols
    return pl.pallas_call(
        spread_kernel,
        grid=(blocks,),
        in_specs=[pl.BlockSpec((1, height, cols), lambda n: (n, 0, 0))],
        out_specs=[
            pl.BlockSpec((rows, cols), lambda n: (0, n)),
            pl.BlockSpec((rows // 2, cols), lambda n: (n // across, n % across)),
        ],
        out_shape=[
            jax.ShapeDtypeStruct((rows, blocks * cols), F32),
            jax.ShapeDtypeStruct((blocks // across * (rows // 2), width), F32),
        ],
        compiler_params=params(40),
        cost_estimate=CHEAP,
    )(both)


def contrast(sums, lengths, pairing, row_mode, row_ids):
    rows, segs, width = sums.shape
    lengths = lengths.astype(F32)[..., None]
    pooled = sums / lengths
    inverse = lax.rsqrt(jnp.sum(pooled * pooled, -1, keepdims=True) + EMB_EPSILON)
    embedded = pooled * inverse
    own = rows * segs
    pair = jnp.stack([pairing, jnp.zeros_like(pairing)], axis=-1).reshape(own, 1)
    spare = jnp.concatenate([pair // 128, pair % 128, jnp.zeros((own, 126), jnp.int32)], axis=1)
    buffer = jnp.concatenate([embedded.reshape(own, width).astype(BF), spare.astype(BF)], axis=1)
    ids = row_ids
    for axis in ("fsdp", "blk") if row_mode else ("blk",):
        for bit in bits_of(axis):
            buffer = jnp.concatenate([buffer, flipped(buffer, axis, bit)], axis=0)
            if axis == "fsdp":
                ids = jnp.concatenate([ids, ids ^ bit])
            else:
                ids = jnp.concatenate([ids, ids ^ (bit * ROWS_PER_BLOCK)])
    total = buffer.shape[0]
    every = buffer[:, :width]
    pair_all = (buffer[:, width].astype(jnp.int32) * 128 + buffer[:, width + 1].astype(jnp.int32))[:, None]
    seg = jnp.arange(total, dtype=jnp.int32) % segs
    number = jnp.broadcast_to(ids[:, None], (total // segs, segs)).reshape(total) * (segs // 2) + seg // 2
    is_query = (seg % 2 == 0)[:, None]
    is_doc = (seg % 2 == 1)[None, :]
    target = is_query & is_doc & (pair_all == number[None, :])
    sims = dot_bt(every, every) / SOFTMAX_WARMTH
    masked = jnp.where(is_doc, sims, NEGATIVE)
    best = jnp.max(masked, -1, keepdims=True)
    log_total = best + jnp.log(jnp.sum(jnp.exp(masked - best), -1, keepdims=True))
    positive = jnp.sum(jnp.where(target, sims, 0.0), -1, keepdims=True)
    loss = jnp.sum(jnp.where(is_query[:own], log_total[:own] - positive[:own], 0.0))
    d_sims = CONTRAST_WEIGHT * (jnp.exp(masked - log_total) - target.astype(F32))
    d_sims = jnp.where(is_query, d_sims, 0.0).astype(BF)
    grad = (dot(d_sims[:own], every) + dot_at(d_sims[:, :own], every)) / SOFTMAX_WARMTH
    grad = grad.reshape(rows, segs, width)
    along = jnp.sum(embedded * grad, -1, keepdims=True)
    return loss, inverse * (grad - embedded * along) / lengths


ROWS_PER_BLOCK = 2


def shards(
    tokens,
    cotangent,
    segments,
    doc_lengths,
    positions,
    pairing,
    qkv_weight,
    out_weight,
    swiglu_weight,
    down_weight,
    attn_gain,
    ffn_gain,
):
    rows_here, shard_len, width = tokens.shape
    split = lax.axis_size("fsdp")
    mine = lax.axis_index("fsdp")
    place = lax.axis_index("blk")
    row_len = shard_len * split
    row_mode = split == rows_here == 2

    if row_mode:
        rows, per_row, query_start, lead = 1, row_len, 0, mine
        lengths = lax.dynamic_slice_in_dim(doc_lengths, mine, 1, 0)
        own_pairing = lax.dynamic_slice_in_dim(pairing.reshape(rows_here, -1), mine, 1, 0)
        row_ids = (place * rows_here + mine)[None]
    else:
        rows, per_row, query_start, lead = rows_here, shard_len, mine * shard_len, 0
        lengths, own_pairing = doc_lengths, pairing.reshape(rows_here, -1)
        row_ids = place * rows_here + jnp.arange(rows_here, dtype=jnp.int32)
    tokens_here = rows * per_row
    tile = min(512, per_row)
    small_tile = min(256, per_row)

    gains = jnp.stack([attn_gain, ffn_gain])
    if row_mode:
        qkv_share = flipped(share_of(qkv_weight), "fsdp", 1)
        (moved,) = tied([take(tokens, 1 - mine, 0)], [qkv_share])
        moved = flipped(moved, "fsdp", 1)
        qkv = from_shares(qkv_weight, qkv_share)
        gains = in_order([gains, flipped(gains, "fsdp", 1)], mine)
        gains = jnp.concatenate([gains[0], gains[1]], axis=1)
    else:
        qkv, swiglu = whole_weight(qkv_weight), whole_weight(swiglu_weight)
        gains = lax.all_gather(gains, "fsdp", axis=1, tiled=True)
    gain1, gain2 = gains[0:1].astype(F32), gains[1:2].astype(F32)

    order = jnp.arange(SEG, dtype=jnp.int32)
    ends = jnp.sum(jnp.where(order[None, :] <= order[:, None], lengths[:, None, :], 0), -1)
    starts = ends - lengths
    token = jnp.arange(row_len, dtype=jnp.int32)
    at = token[None, :, None]
    member = (at >= starts[:, None, :]) & (at < ends[:, None, :])
    first_of = jnp.max(jnp.where(at >= starts[:, None, :], starts[:, None, :], 0), -1)
    lane = jnp.arange(LANES, dtype=jnp.int32)
    frequency = ROPE_BASE ** (-2.0 * (lane % 32).astype(F32) / HDIM)
    angles = (token[None, :] - first_of).astype(F32)[..., None] * frequency
    cosine = jnp.cos(angles).reshape(-1, LANES)
    sine = (jnp.sin(angles) * jnp.where(lane % HDIM < 32, -1.0, 1.0)).reshape(-1, LANES)
    key_feat = jnp.where(member, 0.0, NEGATIVE)
    key_feat = jnp.concatenate([key_feat, jnp.ones((rows, row_len, 120), F32)], -1)
    key_feat = key_feat.astype(BF).reshape(-1, LANES)
    query_feat = jnp.pad(member.astype(BF), ((0, 0), (0, 0), (0, 120))).reshape(-1, LANES)

    def of_queries(table):
        if row_mode:
            return table
        table = table.reshape(rows, row_len, LANES)
        return lax.dynamic_slice_in_dim(table, query_start, per_row, 1).reshape(-1, LANES)

    tables_k = (cosine, sine)
    tables_q = (of_queries(cosine), of_queries(sine))
    query_feat = of_queries(query_feat)
    block_first = query_start + BQ * jnp.arange(per_row // BQ, dtype=jnp.int32)[None, :, None]
    low = jnp.max(jnp.where(block_first >= starts[:, None, :], starts[:, None, :], 0), -1)
    high = jnp.min(jnp.where(block_first + BQ - 1 < ends[:, None, :], ends[:, None, :], row_len), -1)
    low = low // LANES * LANES

    def spans_of(size):
        count = (high - low + size - 1) // size
        return jnp.stack([jnp.minimum(low, row_len - count * size), count], axis=-1).reshape(-1).astype(jnp.int32)

    spans, spans_back = spans_of(BK_FWD), spans_of(BK_BACK)

    if row_mode:
        tables = (*tables_q, qkv)
        share = share_of(swiglu_weight, zero_after(moved))
        share_came = flipped(share, "fsdp", 1)
        old = project(take(tokens, mine, 0), mine * shard_len, *tables, [], small_tile, [moved, share])
        *old, share_came = tied([*old, share_came])
        swiglu = from_shares(swiglu_weight, share_came)
        shift = zero_after(old[0])
        halves = [half_of(out_weight, shift), half_of(down_weight, shift)]
        firsts = [flipped(h, "fsdp", 1) for h in halves]
        query, key, value, x = project(moved, (1 - mine) * shard_len, *tables, old, small_tile, halves)
        key_all, value_all = key, value
    else:
        query, key, value, x = project(tokens.reshape(-1, width), 0, *tables_q, qkv, [], small_tile)

        def along_row(part):
            part = part.reshape(rows, per_row, width)
            return lax.all_gather(part, "fsdp", axis=1, tiled=True).reshape(-1, width)

        key_all, value_all = along_row(key), along_row(value)
    attended, lse = attend(query, key_all, value_all, key_feat, query_feat, spans, rows, PAIRS)
    if row_mode:
        attended, *firsts = tied([attended, *firsts], [lse])
        outer, down = from_halves(out_weight, firsts[0]), from_halves(down_weight, firsts[1])
        cot_send = take(cotangent, 1 - mine + zero_after(firsts[1]), 0)
        cots = [take(cotangent, mine, 0), flipped(cot_send, "fsdp", 1)]
        after = [cot_send]
    else:
        outer, down = whole_weight(out_weight), whole_weight(down_weight)
        cots, after = [cotangent.reshape(-1, width)], []
    low_normed, stat, hidden, *factors, output, sums = mix(
        attended, x, query_feat, gain1, gain2, (outer, swiglu, down), rows, tile, after
    )
    if row_mode:
        sums, cots[1] = tied([sums, cots[1]])
        output_came = flipped(lax.dynamic_slice_in_dim(output, (1 - mine) * shard_len, shard_len, 0), "fsdp", 1)
    else:
        layer_output = output.reshape(tokens.shape)
        sums = lax.psum(sums, "fsdp")
    loss, d_pool = contrast(sums, lengths, own_pairing, row_mode, row_ids)
    d_pool = jnp.pad(d_pool, ((0, 0), (0, LANES - SEG), (0, 0)))
    lse_columns = jnp.pad(lse.reshape(HEADS, tokens_here).T, ((0, 0), (0, LANES - HEADS)))

    d_ffn, d_gate_up, gain2_part = hidden_back(
        cots, lead, output, stat, query_feat, d_pool, factors, gain2, down, rows, tile
    )
    fast = row_mode and shares_fit(low_normed, hidden)
    if fast:
        share = feed_forward_shares(low_normed, d_gate_up, hidden, d_ffn)
        after = [share]
        share = lax.psum_scatter(share.reshape(-1, share.shape[-1]), ("blk", "fsdp"), scatter_dimension=0, tiled=True)
    else:
        swiglu_grad = plain_sum(dot_at(low_normed, d_gate_up).astype(BF))
        down_grad = plain_sum(dot_at(hidden, d_ffn).astype(BF))
        after = []
    d_branch, d_attended, back_feat, gain1_part = branch_back(
        d_ffn, low_normed, stat, query_feat, d_gate_up, attended, lse_columns, gain1, (outer, swiglu), rows, tile,
        after,
    )
    if row_mode:
        d_branch, output_came = tied([d_branch, output_came])
        layer_output = lax.dynamic_slice_in_dim(output, mine * shard_len, shard_len, 0)
        layer_output = in_order([layer_output, output_came], mine)
    part_rows = jnp.arange(width, dtype=jnp.int32) % (width // split)
    losses = jnp.where(part_rows == place, loss if row_mode else loss / split, 0.0)
    losses_high = lax.reduce_precision(losses, 8, 7)
    small = jnp.stack([jnp.sum(gain1_part, 0), jnp.sum(gain2_part, 0), losses_high, losses - losses_high], axis=1)
    small = jnp.pad(small, ((0, 0), (0, LANES - 4))).astype(BF)
    out_sum = Reduction(weight_grad([(attended, d_branch)], small))
    grads, running = [], [out_sum]
    for n in range(PAIRS // BACK_PAIRS):
        columns, _ = beside(
            lambda sent: attend_back(
                query, d_attended, key_all, value_all, key_feat, back_feat, spans_back, tables_q, tables_k, rows,
                BACK_PAIRS, n * BACK_PAIRS, BACK_PAIRS, sent,
            ),
            running,
        )
        if not row_mode:

            def own_part(grad):
                grad = grad.reshape(rows, row_len, -1)
                grad = lax.psum_scatter(grad, "fsdp", scatter_dimension=1, tiled=True)
                return grad.reshape(tokens_here, -1)

            columns = [columns[0], own_part(columns[1]), own_part(columns[2])]
        if fast and n == PAIRS // BACK_PAIRS - 1:
            *columns, share = tied([*columns, share])
            both = lax.all_gather(share, "blk", axis=0)
        grads += columns
        (part,), _ = beside(lambda sent: [weight_grad([(x, g) for g in columns], None, sent)], running)
        running.append(Reduction(part, True))
    qkv_sums = running[1:]
    if row_mode:
        (moved,), _ = beside(
            lambda sent: [
                input_grad_part(d_branch, grads, qkv, (1 - mine) * shard_len, shard_len, BF, small_tile, sent)
            ],
            running,
        )
        exchange = flipped(moved, "fsdp", 1)
        (kept,), _ = beside(
            lambda sent: [
                input_grad_part(d_branch, grads, qkv, mine * shard_len, shard_len, F32, small_tile, sent, True)
            ],
            running,
        )
        beside(lambda _: [], running)
        if fast:
            (swiglu_grad, down_grad), _ = beside(lambda _: spread(both, width), running)
        (layer_output,), _ = beside(lambda _: [layer_output], running)
        kept, exchange = tied([kept, exchange])
        (input_grad,), _ = beside(
            lambda _: [placed(exchange, kept, (1 - mine) * shard_len, small_tile)], running
        )
        input_grad = input_grad.reshape(tokens.shape)
    else:
        input_grad = input_grad_part(d_branch, grads, qkv, 0, tokens_here, F32, small_tile).reshape(tokens.shape)
    while any(not r.done for r in running):
        beside(lambda _: [], running)
    wide, groups = BACK_PAIRS * LANES, PAIRS // BACK_PAIRS
    qkv_columns = [(g, part * wide, wide) for part in range(3) for g in range(groups)]
    (qkv_grad,) = unfold([r.result for r in qkv_sums], [qkv_columns])
    out_grad, small = unfold([out_sum.result], [[(0, 0, width)], [(0, width, LANES)]])
    queries = lax.axis_size("blk") * pairing.shape[0]
    return (
        jnp.sum(small[:, 2:4]) / queries,
        layer_output,
        input_grad,
        qkv_grad,
        out_grad,
        swiglu_grad,
        down_grad,
        small[:, 0],
        small[:, 1],
    )


BACK_PAIRS = 3


def solution(mesh):
    in_specs = (
        P("blk", "fsdp", None),
        P("blk", "fsdp", None),
        P("blk", "fsdp"),
        P("blk", None),
        P("blk", "fsdp"),
        P("blk"),
        P("fsdp", None),
        P("fsdp", None),
        P("fsdp", None),
        P("fsdp", None),
        P("fsdp"),
        P("fsdp"),
    )
    out_specs = (
        P(),
        P("blk", "fsdp", None),
        P("blk", "fsdp", None),
        P("fsdp", None),
        P("fsdp", None),
        P("fsdp", None),
        P("fsdp", None),
        P("fsdp"),
        P("fsdp"),
    )
    return jax.shard_map(shards, mesh=mesh, in_specs=in_specs, out_specs=out_specs, check_vma=False)
```

```python
import functools
import math

import jax
import jax.numpy as jnp
from jax import lax
from jax.experimental import pallas as pl
from jax.experimental.pallas import tpu as pltpu
from jax.sharding import PartitionSpec as P

HEADS = 12
HDIM = 64
PAIRS = HEADS // 2
LANES = 128
SEG = 8

EPSILON = 1e-05
EMB_EPSILON = 1e-06
SOFTMAX_WARMTH = 0.05
ROPE_BASE = 1000.0
CONTRAST_WEIGHT = 512.0
NEGATIVE = -1e30

BF = jnp.bfloat16
F32 = jnp.float32
MIB = 1 << 20
CHEAP = pl.CostEstimate(flops=1024, bytes_accessed=1024, transcendentals=0)


def cost(flops):
    return pl.CostEstimate(flops=4 * flops, bytes_accessed=MIB, transcendentals=0)


def dot(a, b):
    return lax.dot_general(a, b, (((1,), (0,)), ((), ())), preferred_element_type=F32)


def dot_bt(a, b):
    return lax.dot_general(a, b, (((1,), (1,)), ((), ())), preferred_element_type=F32)


def dot_at(a, b):
    return lax.dot_general(a, b, (((0,), (0,)), ((), ())), preferred_element_type=F32)


def lane_iota(shape):
    return lax.broadcasted_iota(jnp.int32, shape, len(shape) - 1)


def halves_swapped(block):
    low = lane_iota(block.shape) % HDIM < HDIM // 2
    return jnp.where(low, pltpu.roll(block, LANES - 32, 1), pltpu.roll(block, 32, 1))


def flipped(block, axis, bit):
    route = [(i, i ^ bit) for i in range(lax.axis_size(axis))]
    return lax.ppermute(block, axis, route)


def take(array, index, dim):
    return lax.dynamic_index_in_dim(array, index, dim, keepdims=False)


class Weight:
    def __init__(self, pieces, offsets, shape):
        self.pieces, self.offsets, self.shape = pieces, offsets, shape


def whole_weight(weight):
    rows, cols = weight.shape
    shape = (rows * lax.axis_size("fsdp"), cols)
    return Weight([lax.all_gather(weight, "fsdp", axis=0, tiled=True)], [(0, 0)], shape)


def half_of(weight):
    half = weight.shape[0] // 2
    return lax.dynamic_slice_in_dim(weight, lax.axis_index("blk") % 2 * half, half, 0)


def from_halves(weight, first):
    rows, cols = weight.shape
    core, mine = lax.axis_index("blk") % 2, lax.axis_index("fsdp")
    second = flipped(first, "blk", 1)
    other = (1 - mine) * rows
    offsets = [
        (mine * rows, 0),
        (other + core * (rows // 2), 0),
        (other + (1 - core) * (rows // 2), 0),
    ]
    return Weight([weight, first, second], offsets, (2 * rows, cols))


def share_of(weight):
    share = weight.shape[0] // lax.axis_size("blk")
    return lax.dynamic_slice_in_dim(weight, lax.axis_index("blk") * share, share, 0)


def from_shares(weight, share):
    rows, cols = weight.shape
    mine = lax.axis_index("fsdp")
    other = lax.all_gather(share, "blk", axis=0, tiled=True)
    return Weight([weight, other], [(mine * rows, 0), ((1 - mine) * rows, 0)], (2 * rows, cols))


def as_table(offsets):
    return jnp.stack([jnp.asarray(v, jnp.int32) for pair in offsets for v in pair])


def weight_copies(table, base, pieces, whole, sems):
    copies = []
    for n, piece in enumerate(pieces):
        rows, cols = piece.shape
        row = pl.multiple_of(table[2 * (base + n)], 16)
        col = pl.multiple_of(table[2 * (base + n) + 1], LANES)
        copies.append(
            pltpu.make_async_copy(
                piece, whole.at[pl.ds(row, rows), pl.ds(col, cols)], sems.at[base + n]
            )
        )
    return copies


def grouped_copies(counts, table, pieces, wholes, sems):
    groups, base = [], 1
    for count, whole in zip(counts, wholes):
        groups.append(weight_copies(table, base, pieces[base - 1 : base - 1 + count], whole, sems))
        base += count
    return groups


def start_all(*groups):
    for group in groups:
        for copy in group:
            copy.start()


def wait_all(*groups):
    for group in groups:
        for copy in group:
            copy.wait()


def weight_operands(weights, lead, after=()):
    counts = [len(w.pieces) for w in weights] + [len(after)]
    pieces = [p for w in weights for p in w.pieces]
    table = as_table([lead] + [o for w in weights for o in w.offsets])
    scratch = [pltpu.VMEM(w.shape, BF) for w in weights]
    return counts, pieces + list(after), table, scratch + [pltpu.SemaphoreType.DMA((len(pieces) + 1,))]


def zero_after(array):
    return jnp.minimum(jnp.abs(array[(0,) * array.ndim].astype(F32)), 0.0).astype(jnp.int32)


ANY = pl.BlockSpec(memory_space=pl.ANY)


def params(limit_mib):
    return pltpu.CompilerParams(vmem_limit_bytes=limit_mib * MIB)


def tied_kernel(*refs):
    del refs


def tied(values, after=()):
    if len(values) + len(after) < 2:
        return list(values)
    return pl.pallas_call(
        tied_kernel,
        in_specs=[ANY] * (len(values) + len(after)),
        out_specs=[ANY] * len(values),
        out_shape=[jax.ShapeDtypeStruct(v.shape, v.dtype) for v in values],
        input_output_aliases={n: n for n in range(len(values))},
        cost_estimate=CHEAP,
    )(*values, *after)


def row_specs(parts, tile, width, steps):
    if len(parts) == 1:
        return [pl.BlockSpec((tile, width), lambda r, i, *_: (r * steps + i, 0))]
    half = steps // 2

    def kept(r, i, t):
        return jnp.where(i // half == t[0], i % half, jnp.where(t[0] == 0, half - 1, 0)), 0

    def moved(r, i, t):
        return jnp.where(i // half != t[0], i % half, jnp.where(t[0] == 0, 0, half - 1)), 0

    return [pl.BlockSpec((tile, width), kept), pl.BlockSpec((tile, width), moved)]


def row_tile(table, refs, rows):
    if len(refs) == 1:
        return refs[0][rows]
    own = pl.program_id(1) // (pl.num_programs(1) // 2) == table[0]
    return jnp.where(own, refs[0][rows], refs[1][rows])


def qkv_kernel(counts, parts, table, cos_ref, sin_ref, *rest):
    x_refs, rest = rest[:parts], rest[parts:]
    pieces, rest = rest[: sum(counts)], rest[sum(counts) :]
    q_ref, k_ref, v_ref, x_ref, whole, sems = rest
    width = q_ref.shape[1]

    @pl.when((pl.program_id(0) == 0) & (pl.program_id(1) == 0))
    def _():
        groups = grouped_copies(counts, table, pieces, [whole], sems)
        start_all(*groups)
        wait_all(*groups)

    x = row_tile(table, x_refs, slice(None))
    x_ref[...] = x
    cosine, sine = cos_ref[...], sin_ref[...]
    for ref, start, factor in ((q_ref, 0, 1.0 / math.sqrt(HDIM)), (k_ref, width, 1.0)):
        projected = dot(x, whole[:, start : start + width])
        for b in range(0, width, LANES):
            block = projected[:, b : b + LANES]
            turned = block * cosine + halves_swapped(block) * sine
            ref[:, b : b + LANES] = turned.astype(BF) * jnp.asarray(factor, BF)
    v_ref[...] = dot(x, whole[:, 2 * width :]).astype(BF)


def project(xs, lead, cosine, sine, weight, rows, tile, after=()):
    tokens, width = cosine.shape[0], weight.shape[0]
    steps = tokens // rows // tile
    counts, pieces, table, scratch = weight_operands([weight], (lead, 0), after)
    wide, narrow = row_specs([None], tile, width, steps), row_specs([None], tile, LANES, steps)
    return pl.pallas_call(
        functools.partial(qkv_kernel, counts, len(xs)),
        grid_spec=pltpu.PrefetchScalarGridSpec(
            num_scalar_prefetch=1,
            grid=(rows, steps),
            in_specs=narrow * 2 + row_specs(xs, tile, width, steps) + [ANY] * len(pieces),
            out_specs=wide * 4,
            scratch_shapes=scratch,
        ),
        out_shape=[jax.ShapeDtypeStruct((tokens, width), BF)] * 4,
        compiler_params=params(48),
        cost_estimate=cost(6 * tokens * width * width),
    )(table, cosine, sine, *xs, *pieces)


def input_grad_kernel(counts, groups, table, dbr_ref, *rest):
    grads, rest = rest[: 3 * groups], rest[3 * groups :]
    pieces, (out_ref, whole, sems) = rest[: sum(counts)], rest[sum(counts) :]
    width = dbr_ref.shape[1]

    @pl.when(pl.program_id(0) == 0)
    def _():
        copies = grouped_copies(counts, table, pieces, [whole], sems)
        start_all(*copies)
        wait_all(*copies)

    total = dbr_ref[...].astype(F32)
    for n in range(3):
        columns = jnp.concatenate([ref[...] for ref in grads[n::3]], axis=1)
        total += dot_bt(columns, whole[:, n * width : (n + 1) * width])
    out_ref[...] = total.astype(out_ref.dtype)


def input_grad_part(dbr, grads, weight, start, tokens, dtype, tile, after=(), whole=False):
    width = dbr.shape[1]
    counts, pieces, table, scratch = weight_operands([weight], (start // tile, 0), after)
    shifted = lambda i, t: (i + t[0], 0)
    return pl.pallas_call(
        functools.partial(input_grad_kernel, counts, len(grads) // 3),
        grid_spec=pltpu.PrefetchScalarGridSpec(
            num_scalar_prefetch=1,
            grid=(tokens // tile,),
            in_specs=[pl.BlockSpec((tile, width), shifted)]
            + [pl.BlockSpec((tile, g.shape[1]), shifted) for g in grads]
            + [ANY] * len(pieces),
            out_specs=pl.BlockSpec((tile, width), shifted if whole else lambda i, t: (i, 0)),
            scratch_shapes=scratch,
        ),
        out_shape=jax.ShapeDtypeStruct((dbr.shape[0] if whole else tokens, width), dtype),
        compiler_params=params(48),
        cost_estimate=cost(6 * tokens * width * width),
    )(table, dbr, *grads, *pieces)


def place_kernel(table, in_ref, old_ref, out_ref):
    del table, old_ref
    out_ref[...] = in_ref[...].astype(out_ref.dtype)


def placed(part, array, start, tile):
    rows, width = part.shape
    return pl.pallas_call(
        place_kernel,
        grid_spec=pltpu.PrefetchScalarGridSpec(
            num_scalar_prefetch=1,
            grid=(rows // tile,),
            in_specs=[pl.BlockSpec((tile, width), lambda i, t: (i, 0)), ANY],
            out_specs=pl.BlockSpec((tile, width), lambda i, t: (i + t[0], 0)),
        ),
        out_shape=jax.ShapeDtypeStruct(array.shape, array.dtype),
        input_output_aliases={2: 0},
        cost_estimate=CHEAP,
    )((start // tile).astype(jnp.int32).reshape(1), part, array)


BQ = 256
BK_FWD = 512
BK_BACK = 256
VROWS = HDIM + 16


def lanes_where(condition):
    return jnp.where(condition(lane_iota((1, LANES))), 1.0, 0.0).astype(BF)


def spread_pairs(whole, source, features, group):
    for g in range(group):
        whole[:, 2 * g * LANES : (2 * g + 1) * LANES] = source[:, g * LANES : (g + 1) * LANES]
        whole[:, (2 * g + 1) * LANES : (2 * g + 2) * LANES] = features[...]


def staggered(count, load, work, finish):
    loaded, worked = load(0), None
    for g in range(count):
        ahead = load(g + 1) if g + 1 < count else None
        result = work(g, loaded)
        if worked is not None:
            finish(g - 1, worked)
        worked, loaded = result, ahead
    finish(count - 1, worked)


def attend_kernel(group, extra, spans, q_ref, k_ref, v_ref, kf_ref, qf_ref, *rest):
    o_ref, lse_ref, kx, vt, qx, best, accum = rest[extra:]
    block = pl.program_id(2)
    where = (pl.program_id(0) * pl.num_programs(2) + block) * 2
    row_len = k_ref.shape[0]

    @pl.when(block == 0)
    def _():
        spread_pairs(kx, k_ref, kf_ref, group)
        for g in range(group):
            for b in range(0, row_len, 256):
                turned = v_ref[b : b + 256, g * LANES : (g + 1) * LANES].astype(F32).T.astype(BF)
                for h in range(2):
                    vt[2 * g + h, :HDIM, b : b + 256] = turned[h * HDIM : (h + 1) * HDIM]
                    vt[2 * g + h, HDIM:, b : b + 256] = jnp.ones((16, 256), BF)

    qf = qf_ref[...]
    even, odd = lanes_where(lambda lane: lane < HDIM), lanes_where(lambda lane: lane >= HDIM)
    for g in range(group):
        q = q_ref[:, g * LANES : (g + 1) * LANES]
        qx[g, :BQ, :LANES] = q * even
        qx[g, BQ:, :LANES] = q * odd
        qx[g, :BQ, LANES:] = qf
        qx[g, BQ:, LANES:] = qf
    best[...] = jnp.full_like(best, NEGATIVE)
    accum[...] = jnp.zeros_like(accum)
    first, count = spans[where], spans[where + 1]

    def step(j, state):
        at = pl.multiple_of(first + j * BK_FWD, LANES)

        def load(g):
            return dot_bt(kx[pl.ds(at, BK_FWD), 2 * g * LANES : 2 * (g + 1) * LANES], qx[g])

        def work(g, scores):
            old = best[g]
            new = jnp.maximum(old, jnp.max(scores, axis=0, keepdims=True))
            best[g] = new
            return jnp.exp(scores - new).astype(BF), jnp.exp(old - new)

        def finish(g, worked):
            soft, factor = worked
            for h in range(2):
                cols = slice(h * BQ, (h + 1) * BQ)
                values = vt[2 * g + h, :, pl.ds(at, BK_FWD)]
                accum[g, :, cols] = accum[g, :, cols] * factor[:, cols] + dot(values, soft[:, cols])

        staggered(group, load, work, finish)
        return state

    lax.fori_loop(0, count, step, 0)
    for g in range(group):
        total = accum[g, HDIM : HDIM + 1]
        lse = best[g] + jnp.log(total)
        lse_ref[2 * g] = lse[:, :BQ]
        lse_ref[2 * g + 1] = lse[:, BQ:]
        turned = accum[g, :HDIM] / total
        turned = jnp.concatenate([turned[:, :BQ], turned[:, BQ:]], axis=0)
        o_ref[:, g * LANES : (g + 1) * LANES] = turned.T.astype(BF)


def attend(q, k, v, key_feat, query_feat, spans, rows, group, after=()):
    tokens, width = q.shape
    row_len = k.shape[0] // rows
    blocks = tokens // rows // BQ
    of_q = lambda r, p, i, *_: (r * blocks + i, p)
    of_k = lambda r, p, i, *_: (r, p)
    wide = group * LANES
    return pl.pallas_call(
        functools.partial(attend_kernel, group, len(after)),
        grid_spec=pltpu.PrefetchScalarGridSpec(
            num_scalar_prefetch=1,
            grid=(rows, PAIRS // group, blocks),
            in_specs=[
                pl.BlockSpec((BQ, wide), of_q),
                pl.BlockSpec((row_len, wide), of_k),
                pl.BlockSpec((row_len, wide), of_k),
                pl.BlockSpec((row_len, LANES), lambda r, p, i, *_: (r, 0)),
                pl.BlockSpec((BQ, LANES), lambda r, p, i, *_: (r * blocks + i, 0)),
            ]
            + [ANY] * len(after),
            out_specs=[
                pl.BlockSpec((BQ, wide), of_q),
                pl.BlockSpec((2 * group, 1, BQ), lambda r, p, i, *_: (p, 0, r * blocks + i)),
            ],
            scratch_shapes=[
                pltpu.VMEM((row_len, 2 * wide), BF),
                pltpu.VMEM((2 * group, VROWS, row_len), BF),
                pltpu.VMEM((group, 2 * BQ, 2 * LANES), BF),
                pltpu.VMEM((group, 1, 2 * BQ), F32),
                pltpu.VMEM((group, VROWS, 2 * BQ), F32),
            ],
        ),
        out_shape=[
            jax.ShapeDtypeStruct((tokens, width), BF),
            jax.ShapeDtypeStruct((HEADS, 1, tokens), F32),
        ],
        compiler_params=params(56),
        cost_estimate=cost(4 * tokens * row_len * width),
    )(spans, q, k, v, key_feat, query_feat, *after)


def attend_back_kernel(
    group, base, extra, spans, q_ref, do_ref, k_ref, v_ref, kf_ref, qf_ref, cq_ref, sq_ref, ck_ref, sk_ref, *rest,
):
    dq_ref, dk_ref, dv_ref, kx, vx, kt, qx, dox, dq_acc, dk_acc, dv_acc = rest[extra:]
    block = pl.program_id(2)
    pair = base + pl.program_id(1) * group
    where = (pl.program_id(0) * pl.num_programs(2) + block) * 2
    row_len = k_ref.shape[0]

    @pl.when(block == 0)
    def _():
        spread_pairs(kx, k_ref, kf_ref, group)
        spread_pairs(vx, v_ref, kf_ref, group)
        for g in range(group):
            for b in range(0, row_len, 256):
                turned = k_ref[b : b + 256, g * LANES : (g + 1) * LANES].astype(F32).T.astype(BF)
                kt[g * LANES : (g + 1) * LANES, b : b + 256] = turned
        dk_acc[...] = jnp.zeros_like(dk_acc)
        dv_acc[...] = jnp.zeros_like(dv_acc)

    qf = qf_ref[...]
    even, odd = lanes_where(lambda lane: lane < HDIM), lanes_where(lambda lane: lane >= HDIM)
    for g in range(group):
        cols = slice(g * LANES, (g + 1) * LANES)
        for whole, source in ((qx, q_ref[:, cols]), (dox, do_ref[:, cols])):
            whole[g, :BQ, :LANES] = source * even
            whole[g, BQ:, :LANES] = source * odd
        for h in range(2):
            head = 2 * (pair + g) + h

            def at(lane, starts):
                return functools.reduce(jnp.logical_or, [lane == start + head for start in starts])

            of_lse = lanes_where(lambda lane: (lane < SEG) | at(lane, (8, 20, 32)))
            of_delta = lanes_where(lambda lane: at(lane, (44, 56, 68)))
            qx[g, h * BQ : (h + 1) * BQ, LANES:] = qf * of_lse
            dox[g, h * BQ : (h + 1) * BQ, LANES:] = qf * of_delta
    dq_acc[...] = jnp.zeros_like(dq_acc)
    first, count = spans[where], spans[where + 1]

    def step(j, state):
        at = pl.multiple_of(first + j * BK_BACK, LANES)

        def load(g):
            twice = slice(2 * g * LANES, (2 * g + 2) * LANES)
            return dot_bt(kx[pl.ds(at, BK_BACK), twice], qx[g]), dot_bt(vx[pl.ds(at, BK_BACK), twice], dox[g])

        def work(g, loaded):
            probs = jnp.exp(loaded[0])
            return probs.astype(BF), (probs * loaded[1]).astype(BF)

        def finish(g, worked):
            probs, grad = worked
            cols = slice(g * LANES, (g + 1) * LANES)
            dv_acc[pl.ds(at, BK_BACK), cols] += dot(probs, dox[g, :, :LANES])
            dk_acc[pl.ds(at, BK_BACK), cols] += dot(grad, qx[g, :, :LANES])
            for h in range(2):
                rows = slice(g * LANES + h * HDIM, g * LANES + (h + 1) * HDIM)
                dq_acc[rows] += dot(kt[rows, pl.ds(at, BK_BACK)], grad[:, h * BQ : (h + 1) * BQ])

        staggered(group, load, work, finish)
        return state

    lax.fori_loop(0, count, step, 0)
    for g in range(group):
        cols = slice(g * LANES, (g + 1) * LANES)
        dq = dq_acc[cols].T * (1.0 / math.sqrt(HDIM))
        dq_ref[:, cols] = (dq * cq_ref[...] - halves_swapped(dq) * sq_ref[...]).astype(BF)

    @pl.when(block == pl.num_programs(2) - 1)
    def _():
        for b in range(0, row_len, 256):
            part = pl.ds(b, 256)
            cosine, sine = ck_ref[part, :], sk_ref[part, :]
            for g in range(group):
                cols = slice(g * LANES, (g + 1) * LANES)
                dk = dk_acc[part, cols]
                dk_ref[part, cols] = (dk * cosine - halves_swapped(dk) * sine).astype(BF)
            dv_ref[part, :] = dv_acc[part, :].astype(BF)


def attend_back(q, do, k, v, key_feat, query_feat, spans, tables_q, tables_k, rows, group, base, pairs, after=()):
    tokens, width = q.shape
    row_len = k.shape[0] // rows
    blocks = tokens // rows // BQ
    start = base // group
    of_q = lambda r, p, i, *_: (r * blocks + i, start + p)
    of_k = lambda r, p, i, *_: (r, start + p)
    per_q = pl.BlockSpec((BQ, LANES), lambda r, p, i, *_: (r * blocks + i, 0))
    per_k = pl.BlockSpec((row_len, LANES), lambda r, p, i, *_: (r, 0))
    wide = group * LANES
    return pl.pallas_call(
        functools.partial(attend_back_kernel, group, base, len(after)),
        grid_spec=pltpu.PrefetchScalarGridSpec(
            num_scalar_prefetch=1,
            grid=(rows, pairs // group, blocks),
            in_specs=[
                pl.BlockSpec((BQ, wide), of_q),
                pl.BlockSpec((BQ, wide), of_q),
                pl.BlockSpec((row_len, wide), of_k),
                pl.BlockSpec((row_len, wide), of_k),
                per_k,
                per_q,
                per_q,
                per_q,
                per_k,
                per_k,
            ]
            + [ANY] * len(after),
            out_specs=[
                pl.BlockSpec((BQ, wide), lambda r, p, i, *_: (r * blocks + i, p)),
                pl.BlockSpec((row_len, wide), lambda r, p, i, *_: (r, p)),
                pl.BlockSpec((row_len, wide), lambda r, p, i, *_: (r, p)),
            ],
            scratch_shapes=[
                pltpu.VMEM((row_len, 2 * wide), BF),
                pltpu.VMEM((row_len, 2 * wide), BF),
                pltpu.VMEM((wide, row_len), BF),
                pltpu.VMEM((group, 2 * BQ, 2 * LANES), BF),
                pltpu.VMEM((group, 2 * BQ, 2 * LANES), BF),
                pltpu.VMEM((wide, BQ), F32),
                pltpu.VMEM((row_len, wide), F32),
                pltpu.VMEM((row_len, wide), F32),
            ],
        ),
        out_shape=[
            jax.ShapeDtypeStruct((tokens, pairs * LANES), BF),
            jax.ShapeDtypeStruct((rows * row_len, pairs * LANES), BF),
            jax.ShapeDtypeStruct((rows * row_len, pairs * LANES), BF),
        ],
        compiler_params=params(56),
        cost_estimate=cost(8 * tokens * row_len * pairs * LANES),
    )(spans, q, do, k, v, key_feat, query_feat, *tables_q, *tables_k, *after)


FF_CHUNK = 512
SUB = 256


def normalize(hidden):
    average = jnp.mean(hidden, -1, keepdims=True)
    centred = hidden - average
    inverse = lax.rsqrt(jnp.mean(centred * centred, -1, keepdims=True) + EPSILON)
    return centred * inverse, inverse


def norm_back(scaled, normalized, inverse):
    return inverse * (
        scaled
        - jnp.mean(scaled, -1, keepdims=True)
        - normalized * jnp.mean(scaled * normalized, -1, keepdims=True)
    )


def split_two(value):
    high = value.astype(BF)
    return high, (value - high.astype(F32)).astype(BF)


def mix_kernel(counts, table, att_ref, x_ref, qf_ref, g1_ref, g2_ref, *rest):
    pieces, rest = rest[: sum(counts)], rest[sum(counts) :]
    nl_ref, stat_ref, hid_ref, fg_ref, fu_ref, out_ref, pool_ref, wo, ws, wd, sems = rest
    groups = grouped_copies(counts, table, pieces, (wo, ws, wd), sems)
    step, begin = pl.program_id(1), (pl.program_id(0) == 0) & (pl.program_id(1) == 0)

    @pl.when(begin)
    def _():
        start_all(*groups)
        wait_all(*groups)

    ff = wd.shape[0]
    tile, chunks = att_ref.shape[0], wd.shape[0] // FF_CHUNK
    subs, opened, pools = tile // SUB, [], []
    lanes = lane_iota((SUB, LANES))

    def open_next():
        rows = slice(len(opened) * SUB, (len(opened) + 1) * SUB)
        branch = dot(att_ref[rows], wo[...])
        unit, inverse1 = normalize(x_ref[rows].astype(F32) + branch)
        normed = unit * g1_ref[...]
        low = normed.astype(BF)
        nl_ref[rows] = low
        opened.append([low, normed, inverse1, rows])

    def close(sub):
        _, hidden_sum, inverse1, rows = opened[sub]
        unit2, inverse2 = normalize(hidden_sum)
        output = unit2 * g2_ref[...]
        out_ref[rows] = output.astype(BF)
        stat_ref[rows] = jnp.where(lanes == 0, inverse1, inverse2)
        high, rest_low = split_two(output)
        member = qf_ref[rows]
        pools.append((dot_at(member, high) + dot_at(member, rest_low))[:SEG])

    def load(n):
        low, c = opened[n // chunks][0], n % chunks
        cols = slice(c * FF_CHUNK, (c + 1) * FF_CHUNK)
        return dot(low, ws[:, cols]), dot(low, ws[:, ff + c * FF_CHUNK : ff + (c + 1) * FF_CHUNK])

    def work(n, loaded):
        sub, c = n // chunks, n % chunks
        if c == 1 and sub + 1 < subs:
            open_next()
        if c == 2 and sub > 0:
            close(sub - 1)
        rows, cols = opened[sub][3], slice(c * FF_CHUNK, (c + 1) * FF_CHUNK)
        gate, up = loaded
        sig = 0.5 + 0.5 * jnp.tanh(0.5 * gate)
        silu = gate * sig
        hidden = (silu * up).astype(BF)
        hid_ref[rows, cols] = hidden
        fg_ref[rows, cols] = (up * (sig + silu * (1.0 - sig))).astype(BF)
        fu_ref[rows, cols] = silu.astype(BF)
        return hidden

    def finish(n, hidden):
        c = n % chunks
        opened[n // chunks][1] = opened[n // chunks][1] + dot(hidden, wd[c * FF_CHUNK : (c + 1) * FF_CHUNK, :])

    open_next()
    staggered(subs * chunks, load, work, finish)
    close(subs - 1)
    sums = functools.reduce(jnp.add, pools)

    @pl.when(step == 0)
    def _():
        pool_ref[0] = sums

    @pl.when(step > 0)
    def _():
        pool_ref[0] += sums


def mix(attended, x, query_feat, gain1, gain2, weights, rows, tile, after):
    tokens, width = x.shape
    steps = tokens // rows // tile
    ff = weights[2].shape[0]
    counts, pieces, table, scratch = weight_operands(weights, (0, 0), after)
    wide, narrow = row_specs([None], tile, width, steps), row_specs([None], tile, LANES, steps)
    hidden, fixed = row_specs([None], tile, ff, steps), [pl.BlockSpec((1, width), lambda r, i, *_: (0, 0))]
    return pl.pallas_call(
        functools.partial(mix_kernel, counts),
        grid_spec=pltpu.PrefetchScalarGridSpec(
            num_scalar_prefetch=1,
            grid=(rows, steps),
            in_specs=wide * 2 + narrow + fixed * 2 + [ANY] * len(pieces),
            out_specs=wide + narrow + hidden * 3 + wide + [pl.BlockSpec((1, SEG, width), lambda r, i, *_: (r, 0, 0))],
            scratch_shapes=scratch,
        ),
        out_shape=[
            jax.ShapeDtypeStruct((tokens, width), BF),
            jax.ShapeDtypeStruct((tokens, LANES), F32),
            jax.ShapeDtypeStruct((tokens, ff), BF),
            jax.ShapeDtypeStruct((tokens, ff), BF),
            jax.ShapeDtypeStruct((tokens, ff), BF),
            jax.ShapeDtypeStruct((tokens, width), BF),
            jax.ShapeDtypeStruct((rows, SEG, width), F32),
        ],
        compiler_params=params(58),
        cost_estimate=cost(2 * tokens * width * (width + 3 * ff)),
    )(table, attended, x, query_feat, gain1, gain2, *pieces)


def hidden_back_kernel(counts, parts, table, *rest):
    cot_refs, rest = rest[:parts], rest[parts:]
    out_ref, stat_ref, qf_ref, dp_ref, fg_ref, fu_ref, g2_ref = rest[:7]
    pieces, rest = rest[7 : 7 + sum(counts)], rest[7 + sum(counts) :]
    dffn_ref, dgu_ref, gf_ref, wd, sems = rest
    groups = grouped_copies(counts, table, pieces, [wd], sems)
    begin = (pl.program_id(0) == 0) & (pl.program_id(1) == 0)

    @pl.when(begin)
    def _():
        start_all(*groups)
        gf_ref[...] = jnp.zeros_like(gf_ref)

    gain2 = g2_ref[...]
    high, rest_low = split_two(dp_ref[0])
    tile, width = out_ref.shape
    ff = wd.shape[0]
    subs, chunks, opened = tile // SUB, ff // FF_CHUNK, []

    def open_next():
        rows = slice(len(opened) * SUB, (len(opened) + 1) * SUB)
        member = qf_ref[rows]
        upstream = row_tile(table, cot_refs, rows).astype(F32) + dot(member, high) + dot(member, rest_low)
        unit2 = out_ref[rows].astype(F32) / gain2
        dffn = norm_back(upstream * gain2, unit2, stat_ref[rows, 1:2]).astype(BF)
        dffn_ref[rows] = dffn
        gf_ref[...] += jnp.sum((upstream * unit2).reshape(SUB // 8, 8, width), axis=0)
        opened.append((dffn, rows))

    def load(n):
        c = n % chunks
        return dot_bt(opened[n // chunks][0], wd[c * FF_CHUNK : (c + 1) * FF_CHUNK, :])

    def work(n, dhid):
        sub, c = n // chunks, n % chunks
        if c == 1 and sub + 1 < subs:
            open_next()
        rows, cols = opened[sub][1], slice(c * FF_CHUNK, (c + 1) * FF_CHUNK)
        dgu_ref[rows, cols] = (dhid * fg_ref[rows, cols].astype(F32)).astype(BF)
        after = slice(ff + c * FF_CHUNK, ff + (c + 1) * FF_CHUNK)
        dgu_ref[rows, after] = (dhid * fu_ref[rows, cols].astype(F32)).astype(BF)

    open_next()

    @pl.when(begin)
    def _():
        wait_all(*groups)

    staggered(subs * chunks, load, work, lambda n, worked: None)


def hidden_back(cots, lead, output, stat, query_feat, dpool, factors, gain2, down, rows, tile):
    tokens, width = output.shape
    ff = down.shape[0]
    steps = tokens // rows // tile
    counts, pieces, table, scratch = weight_operands([down], (lead, 0))
    wide, narrow = row_specs([None], tile, width, steps), row_specs([None], tile, LANES, steps)
    hidden = row_specs([None], tile, ff, steps)
    return pl.pallas_call(
        functools.partial(hidden_back_kernel, counts, len(cots)),
        grid_spec=pltpu.PrefetchScalarGridSpec(
            num_scalar_prefetch=1,
            grid=(rows, steps),
            in_specs=row_specs(cots, tile, width, steps)
            + wide
            + narrow * 2
            + [pl.BlockSpec((1, LANES, width), lambda r, i, *_: (r, 0, 0))]
            + hidden * 2
            + [pl.BlockSpec((1, width), lambda r, i, *_: (0, 0))]
            + [ANY] * len(pieces),
            out_specs=wide + row_specs([None], tile, 2 * ff, steps) + [pl.BlockSpec((8, width), lambda r, i, *_: (0, 0))],
            scratch_shapes=scratch,
        ),
        out_shape=[
            jax.ShapeDtypeStruct((tokens, width), BF),
            jax.ShapeDtypeStruct((tokens, 2 * ff), BF),
            jax.ShapeDtypeStruct((8, width), F32),
        ],
        compiler_params=params(58),
        cost_estimate=cost(4 * tokens * width * ff),
    )(table, *cots, output, stat, query_feat, dpool, *factors, gain2, *pieces)


def branch_back_kernel(counts, table, *refs):
    dffn_ref, nl_ref, stat_ref, qf_ref, dgu_ref, att_ref, lse_ref, g1_ref, head_ref = refs[:9]
    rest = refs[9:]
    pieces, rest = rest[: sum(counts)], rest[sum(counts) :]
    dbr_ref, datt_ref, feat_ref, ga_ref, wo, ws, sems = rest
    groups = grouped_copies(counts, table, pieces, (wo, ws), sems)
    begin = (pl.program_id(0) == 0) & (pl.program_id(1) == 0)

    @pl.when(begin)
    def _():
        start_all(*groups)
        ga_ref[...] = jnp.zeros_like(ga_ref)
        wait_all(*groups)

    gain1, heads = g1_ref[...], head_ref[...]
    width = nl_ref.shape[1]
    rows_of = lambda n: slice(n * SUB, (n + 1) * SUB)

    def load(n):
        rows = rows_of(n)
        return dffn_ref[rows].astype(F32) + dot_bt(dgu_ref[rows], ws[...])

    def work(n, dnormed):
        rows = rows_of(n)
        unit1 = nl_ref[rows].astype(F32) / gain1
        dbr = norm_back(dnormed * gain1, unit1, stat_ref[rows, 0:1]).astype(BF)
        dbr_ref[rows] = dbr
        ga_ref[...] += jnp.sum((dnormed * unit1).reshape(SUB // 8, 8, width), axis=0)
        return dbr

    def finish(n, dbr):
        rows = rows_of(n)
        datt = dot_bt(dbr, wo[...]).astype(BF)
        datt_ref[rows] = datt
        high, rest_low = split_two(datt.astype(F32) * att_ref[rows].astype(F32))
        delta = dot(high, heads) + dot(rest_low, heads)
        feat = qf_ref[rows].astype(F32)
        for value, start in ((lse_ref[rows], 8), (delta, 44)):
            left = -value
            for part_n in range(3):
                part = left.astype(BF).astype(F32)
                left = left - part
                feat = feat + pltpu.roll(part, start + HEADS * part_n, 1)
        feat_ref[rows] = feat.astype(BF)

    staggered(dgu_ref.shape[0] // SUB, load, work, finish)


def branch_back(dffn, low, stat, query_feat, dgu, attended, lse, gain1, weights, rows, tile, after=()):
    tokens, width = low.shape
    ff = dgu.shape[1] // 2
    steps = tokens // rows // tile
    counts, pieces, table, scratch = weight_operands(weights, (0, 0), after)
    wide, narrow = row_specs([None], tile, width, steps), row_specs([None], tile, LANES, steps)
    hidden = row_specs([None], tile, 2 * ff, steps)
    heads = (jnp.arange(width)[:, None] // HDIM == jnp.arange(LANES)[None, :]).astype(BF)
    return pl.pallas_call(
        functools.partial(branch_back_kernel, counts),
        grid_spec=pltpu.PrefetchScalarGridSpec(
            num_scalar_prefetch=1,
            grid=(rows, steps),
            in_specs=wide * 2
            + narrow * 2
            + hidden
            + wide
            + narrow
            + [pl.BlockSpec((1, width), lambda r, i, *_: (0, 0))]
            + [pl.BlockSpec((width, LANES), lambda r, i, *_: (0, 0))]
            + [ANY] * len(pieces),
            out_specs=wide * 2 + narrow + [pl.BlockSpec((8, width), lambda r, i, *_: (0, 0))],
            scratch_shapes=scratch,
        ),
        out_shape=[
            jax.ShapeDtypeStruct((tokens, width), BF),
            jax.ShapeDtypeStruct((tokens, width), BF),
            jax.ShapeDtypeStruct((tokens, LANES), BF),
            jax.ShapeDtypeStruct((8, width), F32),
        ],
        compiler_params=params(58),
        cost_estimate=cost(2 * tokens * width * (width + 2 * ff)),
    )(table, dffn, low, stat, query_feat, dgu, attended, lse, gain1, heads, *pieces)


def bits_of(axis):
    size, bit = lax.axis_size(axis), 1
    while bit < size:
        yield bit
        bit *= 2


def in_order(parts, index):
    shape = (2,) + (1,) * parts[0].ndim
    first = lax.broadcasted_iota(jnp.int32, shape, 0) == index
    return jnp.where(first, parts[0][None], parts[1][None])


def add(first, *others):
    total = first.astype(F32)
    for other in others:
        total = total + other.astype(F32)
    return total.astype(BF)


def reduction(part, short):
    rows, cols = part.shape
    shards = lax.axis_size("fsdp")
    mine, place = lax.axis_index("fsdp"), lax.axis_index("blk")
    core, side = place % 2, place // 2 % 2
    now = part.reshape(shards, 2, rows // shards // 2, cols)
    (came,) = yield [take(now, 1 - core, 1)], [("blk", 1)]
    now = add(take(now, core, 1), came)
    bit = shards // 2
    while bit:
        now = now.reshape(2, bit, -1, cols)
        own = mine // bit % 2
        (came,) = yield [take(now, 1 - own, 0)], [("fsdp", bit)]
        now = add(take(now, own, 0), came)
        bit //= 2
    now = now.reshape(2, -1, cols)
    (came,) = yield [take(now, 1 - side, 0)], [("blk", 2)]
    now = add(take(now, side, 0), came)
    bits = [bit for bit in bits_of("blk") if bit > 2]
    if short:
        for bit in bits:
            (came,) = yield [now], [("blk", bit)]
            now = add(now, came)
    else:
        for bit in bits:
            now = now.reshape(2, -1, cols)
            own = place // bit % 2
            (came,) = yield [take(now, 1 - own, 0)], [("blk", bit)]
            now = add(take(now, own, 0), came)
        for bit in bits[::-1]:
            (came,) = yield [now], [("blk", bit)]
            now = in_order([now, came], place // bit % 2).reshape(-1, cols)
    now = now.reshape(-1, cols)
    (came,) = yield [now], [("blk", 2)]
    now = in_order([now, came], side).reshape(-1, cols)
    (came,) = yield [now], [("blk", 1)]
    yield [now, came], None


class Reduction:
    def __init__(self, part, short=False):
        fsdp_bits, lines = len(list(bits_of("fsdp"))), len(list(bits_of("blk"))) - 2
        self.left = 4 + fsdp_bits + lines * (1 if short else 2)
        self.stages = reduction(part, short)
        self.sends, self.routes = next(self.stages)

    @property
    def done(self):
        return self.routes is None

    @property
    def result(self):
        return self.sends

    def launch(self):
        came = [flipped(a, *route) for a, route in zip(self.sends, self.routes)]
        return self.sends, came

    def take_in(self, came):
        self.left -= 1
        self.sends, self.routes = self.stages.send(came)


def beside(work, launches, joins=None):
    sent, flights = [], []
    for r in launches:
        if not r.done:
            sends, came = r.launch()
            sent += sends
            flights.append((r, came))
    values = list(work(sent))
    late = []
    if joins is not None:
        late = [f for f in flights if f[0] not in [j for j in joins if isinstance(j, Reduction)]]
        flights = [f for f in flights if f not in late] + [j for j in joins if not isinstance(j, Reduction)]
    count = len(values)
    both = tied(values + [a for _, came in flights for a in came])
    at = count
    for r, came in flights:
        r.take_in(both[at : at + len(came)])
        at += len(came)
    return both[:count], late


def turned(block):
    return block.astype(F32).T.astype(BF)


def swiglu_part_kernel(low_ref, grad_ref, out_ref, low_turned):
    tokens = low_ref.shape[0]

    @pl.when(pl.program_id(0) == 0)
    def _():
        for b in range(0, tokens, 256):
            low_turned[:, b : b + 256] = turned(low_ref[b : b + 256, :])

    part = dot(low_turned[...], grad_ref[...]).astype(BF)
    taken, split, rows, cols = out_ref.shape
    for n in range(taken):
        for f in range(split):
            out_ref[n, f] = part[f * rows : (f + 1) * rows, n * cols : (n + 1) * cols]


def down_part_kernel(hidden_ref, dffn_ref, old_ref, out_ref):
    del old_ref
    part = dot(turned(hidden_ref[...]), dffn_ref[...]).astype(BF)
    rows, cols = out_ref.shape[2:]
    across = part.shape[1] // cols
    for n in range(out_ref.shape[0]):
        down, along = n // across * rows, n % across * cols
        out_ref[n, 0] = part[down : down + rows, along : along + cols]


def shares_fit(low, hidden):
    blocks, split = lax.axis_size("blk"), lax.axis_size("fsdp")
    width, ff = low.shape[1], hidden.shape[1]
    cols = 2 * ff // blocks
    return cols % LANES == 0 and width % cols == 0 and ff * width // (split * blocks * cols) * 2 == width // split


def feed_forward_shares(low, d_gate_up, hidden, d_ffn):
    blocks, split = lax.axis_size("blk"), lax.axis_size("fsdp")
    tokens, width = low.shape
    ff = hidden.shape[1]
    cols, rows = 2 * ff // blocks, width // split
    down_rows = rows // 2
    across = width // cols
    shape = jax.ShapeDtypeStruct((blocks, split, rows + down_rows, cols), BF)
    whole = lambda a: pl.BlockSpec(a.shape, lambda *_: (0, 0))
    shares = pl.pallas_call(
        swiglu_part_kernel,
        grid=(blocks // 2,),
        in_specs=[whole(low), pl.BlockSpec((tokens, 2 * cols), lambda j: (0, j))],
        out_specs=pl.BlockSpec((2, split, rows, cols), lambda j: (j, 0, 0, 0)),
        out_shape=shape,
        scratch_shapes=[pltpu.VMEM((width, tokens), BF)],
        compiler_params=params(48),
        cost_estimate=cost(4 * tokens * width * ff),
    )(low, d_gate_up)
    taken = 2 * down_rows
    steps = ff // split // taken
    return pl.pallas_call(
        down_part_kernel,
        grid=(split, steps),
        in_specs=[pl.BlockSpec((tokens, taken), lambda f, j: (0, f * steps + j)), whole(d_ffn), ANY],
        out_specs=pl.BlockSpec((2 * across, 1, down_rows, cols), lambda f, j: (j, f, 2, 0)),
        out_shape=shape,
        input_output_aliases={2: 0},
        compiler_params=params(48),
        cost_estimate=cost(2 * tokens * width * ff),
    )(hidden, d_ffn, shares)


def plain_sum(part):
    part = lax.psum_scatter(part, "fsdp", scatter_dimension=0, tiled=True)
    return lax.psum(part, "blk").astype(F32)


def weight_grad(pairs, beside_it=None, after=()):
    arrays, left = [], []
    for a, b in pairs:
        place = [n for n, other in enumerate(arrays) if other is a]
        if not place:
            arrays.append(a)
            place = [len(arrays) - 1]
        arrays.append(b)
        left.append((place[0], len(arrays) - 1))
    cols = sum(b.shape[1] for _, b in pairs)
    last = []
    if beside_it is not None:
        last = [beside_it]
        cols += beside_it.shape[1]

    (shared,) = {a for a, _ in left}

    def kernel(*refs):
        out_ref, flipped_ref, at = refs[-2], refs[-1], 0
        for b in range(0, flipped_ref.shape[1], 256):
            flipped_ref[:, b : b + 256] = turned(refs[shared][b : b + 256, :])
        for _, b in left:
            part = dot(flipped_ref[...], refs[b][...]).astype(BF)
            out_ref[:, at : at + part.shape[1]] = part
            at += part.shape[1]
        if last:
            out_ref[:, at:] = refs[len(arrays)][...]

    whole = pl.BlockSpec(memory_space=pltpu.VMEM)
    return pl.pallas_call(
        kernel,
        in_specs=[whole] * (len(arrays) + len(last)) + [ANY] * len(after),
        scratch_shapes=[pltpu.VMEM(pairs[0][0].shape[::-1], BF)],
        out_shape=jax.ShapeDtypeStruct((pairs[0][0].shape[1], cols), BF),
        compiler_params=params(56),
        cost_estimate=cost(2 * pairs[0][0].shape[0] * pairs[0][0].shape[1] * cols),
    )(*arrays, *last, *after)


def unfold_kernel(kinds, columns, table, *refs):
    own = pl.program_id(0) == table[0]
    values, at = [], 0
    for kind in kinds:
        values.append(refs[at][...] if kind == 1 else jnp.where(own, refs[at][...], refs[at + 1][...]))
        at += kind
    for ref, parts in zip(refs[at:], columns):
        to = 0
        for n, start, wide in parts:
            ref[:, to : to + wide] = values[n][:, start : start + wide].astype(F32)
            to += wide


def unfold(results, columns):
    rows = sum(a.shape[0] for a in results[0]) // 2
    block = rows // 2 if rows % 32 == 0 else rows
    steps = rows // block
    maps = {2: lambda c, i, t: (i, 0), 1: lambda c, i, t: (c * steps + i, 0)}
    return pl.pallas_call(
        functools.partial(unfold_kernel, [len(r) for r in results], columns),
        grid_spec=pltpu.PrefetchScalarGridSpec(
            num_scalar_prefetch=1,
            grid=(2, steps),
            in_specs=[pl.BlockSpec((block, a.shape[1]), maps[len(r)]) for r in results for a in r],
            out_specs=[pl.BlockSpec((block, sum(p[2] for p in parts)), maps[1]) for parts in columns],
        ),
        out_shape=[jax.ShapeDtypeStruct((2 * rows, sum(p[2] for p in parts)), F32) for parts in columns],
        compiler_params=params(40),
        cost_estimate=CHEAP,
    )((lax.axis_index("blk") % 2).reshape(1), *[a for r in results for a in r])


def spread_kernel(both_ref, swiglu_ref, down_ref):
    rows = swiglu_ref.shape[0]
    swiglu_ref[...] = both_ref[0, :rows, :].astype(F32)
    down_ref[...] = both_ref[0, rows:, :].astype(F32)


def spread(both, width):
    blocks, height, cols = both.shape
    rows = height * 2 // 3
    across = width // cols
    return pl.pallas_call(
        spread_kernel,
        grid=(blocks,),
        in_specs=[pl.BlockSpec((1, height, cols), lambda n: (n, 0, 0))],
        out_specs=[
            pl.BlockSpec((rows, cols), lambda n: (0, n)),
            pl.BlockSpec((rows // 2, cols), lambda n: (n // across, n % across)),
        ],
        out_shape=[
            jax.ShapeDtypeStruct((rows, blocks * cols), F32),
            jax.ShapeDtypeStruct((blocks // across * (rows // 2), width), F32),
        ],
        compiler_params=params(40),
        cost_estimate=CHEAP,
    )(both)


def contrast(sums, lengths, pairing, row_mode, row_ids):
    rows, segs, width = sums.shape
    lengths = lengths.astype(F32)[..., None]
    pooled = sums / lengths
    inverse = lax.rsqrt(jnp.sum(pooled * pooled, -1, keepdims=True) + EMB_EPSILON)
    embedded = pooled * inverse
    own = rows * segs
    pair = jnp.stack([pairing, jnp.zeros_like(pairing)], axis=-1).reshape(own, 1)
    spare = jnp.concatenate([pair // 128, pair % 128, jnp.zeros((own, 126), jnp.int32)], axis=1)
    buffer = jnp.concatenate([embedded.reshape(own, width).astype(BF), spare.astype(BF)], axis=1)
    ids = row_ids
    for axis in ("fsdp", "blk") if row_mode else ("blk",):
        for bit in bits_of(axis):
            buffer = jnp.concatenate([buffer, flipped(buffer, axis, bit)], axis=0)
            if axis == "fsdp":
                ids = jnp.concatenate([ids, ids ^ bit])
            else:
                ids = jnp.concatenate([ids, ids ^ (bit * ROWS_PER_BLOCK)])
    total = buffer.shape[0]
    every = buffer[:, :width]
    pair_all = (buffer[:, width].astype(jnp.int32) * 128 + buffer[:, width + 1].astype(jnp.int32))[:, None]
    seg = jnp.arange(total, dtype=jnp.int32) % segs
    number = jnp.broadcast_to(ids[:, None], (total // segs, segs)).reshape(total) * (segs // 2) + seg // 2
    is_query = (seg % 2 == 0)[:, None]
    is_doc = (seg % 2 == 1)[None, :]
    target = is_query & is_doc & (pair_all == number[None, :])
    sims = dot_bt(every, every) / SOFTMAX_WARMTH
    masked = jnp.where(is_doc, sims, NEGATIVE)
    best = jnp.max(masked, -1, keepdims=True)
    log_total = best + jnp.log(jnp.sum(jnp.exp(masked - best), -1, keepdims=True))
    positive = jnp.sum(jnp.where(target, sims, 0.0), -1, keepdims=True)
    loss = jnp.sum(jnp.where(is_query[:own], log_total[:own] - positive[:own], 0.0))
    d_sims = CONTRAST_WEIGHT * (jnp.exp(masked - log_total) - target.astype(F32))
    d_sims = jnp.where(is_query, d_sims, 0.0).astype(BF)
    grad = (dot(d_sims[:own], every) + dot_at(d_sims[:, :own], every)) / SOFTMAX_WARMTH
    grad = grad.reshape(rows, segs, width)
    along = jnp.sum(embedded * grad, -1, keepdims=True)
    return loss, inverse * (grad - embedded * along) / lengths


ROWS_PER_BLOCK = 2


def shards(
    tokens,
    cotangent,
    segments,
    doc_lengths,
    positions,
    pairing,
    qkv_weight,
    out_weight,
    swiglu_weight,
    down_weight,
    attn_gain,
    ffn_gain,
):
    rows_here, shard_len, width = tokens.shape
    split = lax.axis_size("fsdp")
    mine = lax.axis_index("fsdp")
    place = lax.axis_index("blk")
    row_len = shard_len * split
    row_mode = split == rows_here == 2

    if row_mode:
        rows, per_row, query_start, lead = 1, row_len, 0, mine
        lengths = lax.dynamic_slice_in_dim(doc_lengths, mine, 1, 0)
        own_pairing = lax.dynamic_slice_in_dim(pairing.reshape(rows_here, -1), mine, 1, 0)
        row_ids = (place * rows_here + mine)[None]
    else:
        rows, per_row, query_start, lead = rows_here, shard_len, mine * shard_len, 0
        lengths, own_pairing = doc_lengths, pairing.reshape(rows_here, -1)
        row_ids = place * rows_here + jnp.arange(rows_here, dtype=jnp.int32)
    tokens_here = rows * per_row
    tile = min(512, per_row)
    small_tile = min(256, per_row)

    gains = jnp.stack([attn_gain, ffn_gain])
    if row_mode:
        qkv_share = flipped(share_of(qkv_weight), "fsdp", 1)
        (moved,) = tied([take(tokens, 1 - mine, 0)], [qkv_share])
        moved = flipped(moved, "fsdp", 1)
        qkv = from_shares(qkv_weight, qkv_share)
        gains = in_order([gains, flipped(gains, "fsdp", 1)], mine)
        gains = jnp.concatenate([gains[0], gains[1]], axis=1)
    else:
        qkv, swiglu = whole_weight(qkv_weight), whole_weight(swiglu_weight)
        gains = lax.all_gather(gains, "fsdp", axis=1, tiled=True)
    gain1, gain2 = gains[0:1].astype(F32), gains[1:2].astype(F32)

    order = jnp.arange(SEG, dtype=jnp.int32)
    ends = jnp.sum(jnp.where(order[None, :] <= order[:, None], lengths[:, None, :], 0), -1)
    starts = ends - lengths
    token = jnp.arange(row_len, dtype=jnp.int32)
    at = token[None, :, None]
    member = (at >= starts[:, None, :]) & (at < ends[:, None, :])
    first_of = jnp.max(jnp.where(at >= starts[:, None, :], starts[:, None, :], 0), -1)
    lane = jnp.arange(LANES, dtype=jnp.int32)
    frequency = ROPE_BASE ** (-2.0 * (lane % 32).astype(F32) / HDIM)
    angles = (token[None, :] - first_of).astype(F32)[..., None] * frequency
    cosine = jnp.cos(angles).reshape(-1, LANES)
    sine = (jnp.sin(angles) * jnp.where(lane % HDIM < 32, -1.0, 1.0)).reshape(-1, LANES)
    key_feat = jnp.where(member, 0.0, NEGATIVE)
    key_feat = jnp.concatenate([key_feat, jnp.ones((rows, row_len, 120), F32)], -1)
    key_feat = key_feat.astype(BF).reshape(-1, LANES)
    query_feat = jnp.pad(member.astype(BF), ((0, 0), (0, 0), (0, 120))).reshape(-1, LANES)

    def of_queries(table):
        if row_mode:
            return table
        table = table.reshape(rows, row_len, LANES)
        return lax.dynamic_slice_in_dim(table, query_start, per_row, 1).reshape(-1, LANES)

    tables_k = (cosine, sine)
    tables_q = (of_queries(cosine), of_queries(sine))
    query_feat = of_queries(query_feat)
    block_first = query_start + BQ * jnp.arange(per_row // BQ, dtype=jnp.int32)[None, :, None]
    low = jnp.max(jnp.where(block_first >= starts[:, None, :], starts[:, None, :], 0), -1)
    high = jnp.min(jnp.where(block_first + BQ - 1 < ends[:, None, :], ends[:, None, :], row_len), -1)
    low = low // LANES * LANES

    def spans_of(size):
        count = (high - low + size - 1) // size
        return jnp.stack([jnp.minimum(low, row_len - count * size), count], axis=-1).reshape(-1).astype(jnp.int32)

    spans, spans_back = spans_of(BK_FWD), spans_of(BK_BACK)

    if row_mode:
        tables = (*tables_q, qkv)
        share, *halves = tied([share_of(swiglu_weight), half_of(out_weight), half_of(down_weight)], [moved])
        share_came = flipped(share, "fsdp", 1)
        firsts = [flipped(h, "fsdp", 1) for h in halves]
        xs = [take(tokens, mine, 0), moved]
        projected = project(xs, lead, *tables, rows, small_tile, [share, *halves])
        query, key, value, x, share_came = tied([*projected, share_came])
        swiglu = from_shares(swiglu_weight, share_came)
        key_all, value_all = key, value
    else:
        query, key, value, x = project([tokens.reshape(-1, width)], 0, *tables_q, qkv, rows, small_tile)

        def along_row(part):
            part = part.reshape(rows, per_row, width)
            return lax.all_gather(part, "fsdp", axis=1, tiled=True).reshape(-1, width)

        key_all, value_all = along_row(key), along_row(value)
    attended, lse = attend(query, key_all, value_all, key_feat, query_feat, spans, rows, PAIRS)
    if row_mode:
        attended, *firsts = tied([attended, *firsts], [lse])
        outer, down = from_halves(out_weight, firsts[0]), from_halves(down_weight, firsts[1])
        cot_send = take(cotangent, 1 - mine + zero_after(firsts[1]), 0)
        cots = [take(cotangent, mine, 0), flipped(cot_send, "fsdp", 1)]
        after = [cot_send]
    else:
        outer, down = whole_weight(out_weight), whole_weight(down_weight)
        cots, after = [cotangent.reshape(-1, width)], []
    low_normed, stat, hidden, *factors, output, sums = mix(
        attended, x, query_feat, gain1, gain2, (outer, swiglu, down), rows, tile, after
    )
    if row_mode:
        sums, cots[1] = tied([sums, cots[1]])
        output_came = flipped(lax.dynamic_slice_in_dim(output, (1 - mine) * shard_len, shard_len, 0), "fsdp", 1)
    else:
        layer_output = output.reshape(tokens.shape)
        sums = lax.psum(sums, "fsdp")
    loss, d_pool = contrast(sums, lengths, own_pairing, row_mode, row_ids)
    d_pool = jnp.pad(d_pool, ((0, 0), (0, LANES - SEG), (0, 0)))
    lse_columns = jnp.pad(lse.reshape(HEADS, tokens_here).T, ((0, 0), (0, LANES - HEADS)))

    d_ffn, d_gate_up, gain2_part = hidden_back(
        cots, lead, output, stat, query_feat, d_pool, factors, gain2, down, rows, tile
    )
    fast = row_mode and shares_fit(low_normed, hidden)
    if fast:
        share = feed_forward_shares(low_normed, d_gate_up, hidden, d_ffn)
        after = [share]
        share = lax.psum_scatter(share.reshape(-1, share.shape[-1]), ("blk", "fsdp"), scatter_dimension=0, tiled=True)
    else:
        swiglu_grad = plain_sum(dot_at(low_normed, d_gate_up).astype(BF))
        down_grad = plain_sum(dot_at(hidden, d_ffn).astype(BF))
        after = []
    d_branch, d_attended, back_feat, gain1_part = branch_back(
        d_ffn, low_normed, stat, query_feat, d_gate_up, attended, lse_columns, gain1, (outer, swiglu), rows, tile,
        after,
    )
    if row_mode:
        d_branch, output_came = tied([d_branch, output_came])
        layer_output = lax.dynamic_slice_in_dim(output, mine * shard_len, shard_len, 0)
        layer_output = in_order([layer_output, output_came], mine)
    part_rows = jnp.arange(width, dtype=jnp.int32) % (width // split)
    losses = jnp.where(part_rows == place, loss if row_mode else loss / split, 0.0)
    losses_high = lax.reduce_precision(losses, 8, 7)
    small = jnp.stack([jnp.sum(gain1_part, 0), jnp.sum(gain2_part, 0), losses_high, losses - losses_high], axis=1)
    small = jnp.pad(small, ((0, 0), (0, LANES - 4))).astype(BF)
    out_sum = Reduction(weight_grad([(attended, d_branch)], small))
    grads, running = [], [out_sum]
    for n in range(PAIRS // BACK_PAIRS):
        columns, _ = beside(
            lambda sent: attend_back(
                query, d_attended, key_all, value_all, key_feat, back_feat, spans_back, tables_q, tables_k, rows,
                BACK_PAIRS, n * BACK_PAIRS, BACK_PAIRS, sent,
            ),
            running,
        )
        if not row_mode:

            def own_part(grad):
                grad = grad.reshape(rows, row_len, -1)
                grad = lax.psum_scatter(grad, "fsdp", scatter_dimension=1, tiled=True)
                return grad.reshape(tokens_here, -1)

            columns = [columns[0], own_part(columns[1]), own_part(columns[2])]
        if fast and n == PAIRS // BACK_PAIRS - 1:
            *columns, share = tied([*columns, share])
            both = lax.all_gather(share, "blk", axis=0)
        grads += columns
        (part,), _ = beside(lambda sent: [weight_grad([(x, g) for g in columns], None, sent)], running)
        running.append(Reduction(part, True))
    qkv_sums = running[1:]
    if row_mode:
        (moved,), _ = beside(
            lambda sent: [
                input_grad_part(d_branch, grads, qkv, (1 - mine) * shard_len, shard_len, BF, small_tile, sent)
            ],
            running,
        )
        exchange = flipped(moved, "fsdp", 1)
        (kept,), _ = beside(
            lambda sent: [
                input_grad_part(d_branch, grads, qkv, mine * shard_len, shard_len, F32, small_tile, sent, True)
            ],
            running,
        )
        beside(lambda _: [], running)
        if fast:
            (swiglu_grad, down_grad), _ = beside(lambda _: spread(both, width), running)
        (layer_output,), _ = beside(lambda _: [layer_output], running)
        kept, exchange = tied([kept, exchange])
        (input_grad,), _ = beside(
            lambda _: [placed(exchange, kept, (1 - mine) * shard_len, small_tile)], running
        )
        input_grad = input_grad.reshape(tokens.shape)
    else:
        input_grad = input_grad_part(d_branch, grads, qkv, 0, tokens_here, F32, small_tile).reshape(tokens.shape)
    while any(not r.done for r in running):
        beside(lambda _: [], running)
    wide, groups = BACK_PAIRS * LANES, PAIRS // BACK_PAIRS
    qkv_columns = [(g, part * wide, wide) for part in range(3) for g in range(groups)]
    (qkv_grad,) = unfold([r.result for r in qkv_sums], [qkv_columns])
    out_grad, small = unfold([out_sum.result], [[(0, 0, width)], [(0, width, LANES)]])
    queries = lax.axis_size("blk") * pairing.shape[0]
    return (
        jnp.sum(small[:, 2:4]) / queries,
        layer_output,
        input_grad,
        qkv_grad,
        out_grad,
        swiglu_grad,
        down_grad,
        small[:, 0],
        small[:, 1],
    )


BACK_PAIRS = 3


def solution(mesh):
    in_specs = (
        P("blk", "fsdp", None),
        P("blk", "fsdp", None),
        P("blk", "fsdp"),
        P("blk", None),
        P("blk", "fsdp"),
        P("blk"),
        P("fsdp", None),
        P("fsdp", None),
        P("fsdp", None),
        P("fsdp", None),
        P("fsdp"),
        P("fsdp"),
    )
    out_specs = (
        P(),
        P("blk", "fsdp", None),
        P("blk", "fsdp", None),
        P("fsdp", None),
        P("fsdp", None),
        P("fsdp", None),
        P("fsdp", None),
        P("fsdp"),
        P("fsdp"),
    )
    return jax.shard_map(shards, mesh=mesh, in_specs=in_specs, out_specs=out_specs, check_vma=False)
```

```python
import functools
import math

import jax
import jax.numpy as jnp
from jax import lax
from jax.experimental import pallas as pl
from jax.experimental.pallas import tpu as pltpu
from jax.sharding import PartitionSpec as P

HEADS = 12
HDIM = 64
PAIRS = HEADS // 2
LANES = 128
SEG = 8

EPSILON = 1e-05
EMB_EPSILON = 1e-06
SOFTMAX_WARMTH = 0.05
ROPE_BASE = 1000.0
CONTRAST_WEIGHT = 512.0
NEGATIVE = -1e30

BF = jnp.bfloat16
F32 = jnp.float32
MIB = 1 << 20
CHEAP = pl.CostEstimate(flops=1024, bytes_accessed=1024, transcendentals=0)


def cost(flops):
    return pl.CostEstimate(flops=4 * flops, bytes_accessed=MIB, transcendentals=0)


def dot(a, b):
    return lax.dot_general(a, b, (((1,), (0,)), ((), ())), preferred_element_type=F32)


def dot_bt(a, b):
    return lax.dot_general(a, b, (((1,), (1,)), ((), ())), preferred_element_type=F32)


def dot_at(a, b):
    return lax.dot_general(a, b, (((0,), (0,)), ((), ())), preferred_element_type=F32)


def lane_iota(shape):
    return lax.broadcasted_iota(jnp.int32, shape, len(shape) - 1)


def halves_swapped(block):
    low = lane_iota(block.shape) % HDIM < HDIM // 2
    return jnp.where(low, pltpu.roll(block, LANES - 32, 1), pltpu.roll(block, 32, 1))


def flipped(block, axis, bit):
    route = [(i, i ^ bit) for i in range(lax.axis_size(axis))]
    return lax.ppermute(block, axis, route)


def take(array, index, dim):
    return lax.dynamic_index_in_dim(array, index, dim, keepdims=False)


class Weight:
    def __init__(self, pieces, offsets, shape):
        self.pieces, self.offsets, self.shape = pieces, offsets, shape


def whole_weight(weight):
    rows, cols = weight.shape
    shape = (rows * lax.axis_size("fsdp"), cols)
    return Weight([lax.all_gather(weight, "fsdp", axis=0, tiled=True)], [(0, 0)], shape)


def half_of(weight):
    half = weight.shape[0] // 2
    return lax.dynamic_slice_in_dim(weight, lax.axis_index("blk") % 2 * half, half, 0)


def from_halves(weight, first):
    rows, cols = weight.shape
    core, mine = lax.axis_index("blk") % 2, lax.axis_index("fsdp")
    second = flipped(first, "blk", 1)
    other = (1 - mine) * rows
    offsets = [
        (mine * rows, 0),
        (other + core * (rows // 2), 0),
        (other + (1 - core) * (rows // 2), 0),
    ]
    return Weight([weight, first, second], offsets, (2 * rows, cols))


def share_of(weight):
    share = weight.shape[0] // lax.axis_size("blk")
    return lax.dynamic_slice_in_dim(weight, lax.axis_index("blk") * share, share, 0)


def from_shares(weight, share):
    rows, cols = weight.shape
    mine = lax.axis_index("fsdp")
    other = lax.all_gather(share, "blk", axis=0, tiled=True)
    return Weight([weight, other], [(mine * rows, 0), ((1 - mine) * rows, 0)], (2 * rows, cols))


def as_table(offsets):
    return jnp.stack([jnp.asarray(v, jnp.int32) for pair in offsets for v in pair])


def weight_copies(table, base, pieces, whole, sems):
    copies = []
    for n, piece in enumerate(pieces):
        rows, cols = piece.shape
        row = pl.multiple_of(table[2 * (base + n)], 16)
        col = pl.multiple_of(table[2 * (base + n) + 1], LANES)
        copies.append(
            pltpu.make_async_copy(
                piece, whole.at[pl.ds(row, rows), pl.ds(col, cols)], sems.at[base + n]
            )
        )
    return copies


def grouped_copies(counts, table, pieces, wholes, sems):
    groups, base = [], 1
    for count, whole in zip(counts, wholes):
        groups.append(weight_copies(table, base, pieces[base - 1 : base - 1 + count], whole, sems))
        base += count
    return groups


def start_all(*groups):
    for group in groups:
        for copy in group:
            copy.start()


def wait_all(*groups):
    for group in groups:
        for copy in group:
            copy.wait()


def weight_operands(weights, lead, after=()):
    counts = [len(w.pieces) for w in weights] + [len(after)]
    pieces = [p for w in weights for p in w.pieces]
    table = as_table([lead] + [o for w in weights for o in w.offsets])
    scratch = [pltpu.VMEM(w.shape, BF) for w in weights]
    return counts, pieces + list(after), table, scratch + [pltpu.SemaphoreType.DMA((len(pieces) + 1,))]


def zero_after(array):
    return jnp.minimum(jnp.abs(array[(0,) * array.ndim].astype(F32)), 0.0).astype(jnp.int32)


ANY = pl.BlockSpec(memory_space=pl.ANY)


def params(limit_mib):
    return pltpu.CompilerParams(vmem_limit_bytes=limit_mib * MIB)


def tied_kernel(*refs):
    del refs


def tied(values, after=()):
    if len(values) + len(after) < 2:
        return list(values)
    return pl.pallas_call(
        tied_kernel,
        in_specs=[ANY] * (len(values) + len(after)),
        out_specs=[ANY] * len(values),
        out_shape=[jax.ShapeDtypeStruct(v.shape, v.dtype) for v in values],
        input_output_aliases={n: n for n in range(len(values))},
        cost_estimate=CHEAP,
    )(*values, *after)


def row_specs(parts, tile, width, steps):
    if len(parts) == 1:
        return [pl.BlockSpec((tile, width), lambda r, i, *_: (r * steps + i, 0))]
    half = steps // 2

    def kept(r, i, t):
        return jnp.where(i // half == t[0], i % half, jnp.where(t[0] == 0, half - 1, 0)), 0

    def moved(r, i, t):
        return jnp.where(i // half != t[0], i % half, jnp.where(t[0] == 0, 0, half - 1)), 0

    return [pl.BlockSpec((tile, width), kept), pl.BlockSpec((tile, width), moved)]


def row_tile(table, refs, rows):
    if len(refs) == 1:
        return refs[0][rows]
    own = pl.program_id(1) // (pl.num_programs(1) // 2) == table[0]
    return jnp.where(own, refs[0][rows], refs[1][rows])


def qkv_kernel(counts, parts, table, cos_ref, sin_ref, *rest):
    x_refs, rest = rest[:parts], rest[parts:]
    pieces, rest = rest[: sum(counts)], rest[sum(counts) :]
    q_ref, k_ref, v_ref, x_ref, whole, sems = rest
    width = q_ref.shape[1]

    @pl.when((pl.program_id(0) == 0) & (pl.program_id(1) == 0))
    def _():
        groups = grouped_copies(counts, table, pieces, [whole], sems)
        start_all(*groups)
        wait_all(*groups)

    x = row_tile(table, x_refs, slice(None))
    x_ref[...] = x
    cosine, sine = cos_ref[...], sin_ref[...]
    for ref, start, factor in ((q_ref, 0, 1.0 / math.sqrt(HDIM)), (k_ref, width, 1.0)):
        projected = dot(x, whole[:, start : start + width])
        for b in range(0, width, LANES):
            block = projected[:, b : b + LANES]
            turned = block * cosine + halves_swapped(block) * sine
            ref[:, b : b + LANES] = turned.astype(BF) * jnp.asarray(factor, BF)
    v_ref[...] = dot(x, whole[:, 2 * width :]).astype(BF)


def project(xs, lead, cosine, sine, weight, rows, tile, after=()):
    tokens, width = cosine.shape[0], weight.shape[0]
    steps = tokens // rows // tile
    counts, pieces, table, scratch = weight_operands([weight], (lead, 0), after)
    wide, narrow = row_specs([None], tile, width, steps), row_specs([None], tile, LANES, steps)
    return pl.pallas_call(
        functools.partial(qkv_kernel, counts, len(xs)),
        grid_spec=pltpu.PrefetchScalarGridSpec(
            num_scalar_prefetch=1,
            grid=(rows, steps),
            in_specs=narrow * 2 + row_specs(xs, tile, width, steps) + [ANY] * len(pieces),
            out_specs=wide * 4,
            scratch_shapes=scratch,
        ),
        out_shape=[jax.ShapeDtypeStruct((tokens, width), BF)] * 4,
        compiler_params=params(48),
        cost_estimate=cost(6 * tokens * width * width),
    )(table, cosine, sine, *xs, *pieces)


def input_grad_kernel(counts, groups, table, dbr_ref, *rest):
    grads, rest = rest[: 3 * groups], rest[3 * groups :]
    pieces, (out_ref, whole, sems) = rest[: sum(counts)], rest[sum(counts) :]
    width = dbr_ref.shape[1]

    @pl.when(pl.program_id(0) == 0)
    def _():
        copies = grouped_copies(counts, table, pieces, [whole], sems)
        start_all(*copies)
        wait_all(*copies)

    total = dbr_ref[...].astype(F32)
    for n in range(3):
        columns = jnp.concatenate([ref[...] for ref in grads[n::3]], axis=1)
        total += dot_bt(columns, whole[:, n * width : (n + 1) * width])
    out_ref[...] = total.astype(out_ref.dtype)


def input_grad_part(dbr, grads, weight, start, tokens, dtype, tile, after=(), whole=False):
    width = dbr.shape[1]
    counts, pieces, table, scratch = weight_operands([weight], (start // tile, 0), after)
    shifted = lambda i, t: (i + t[0], 0)
    return pl.pallas_call(
        functools.partial(input_grad_kernel, counts, len(grads) // 3),
        grid_spec=pltpu.PrefetchScalarGridSpec(
            num_scalar_prefetch=1,
            grid=(tokens // tile,),
            in_specs=[pl.BlockSpec((tile, width), shifted)]
            + [pl.BlockSpec((tile, g.shape[1]), shifted) for g in grads]
            + [ANY] * len(pieces),
            out_specs=pl.BlockSpec((tile, width), shifted if whole else lambda i, t: (i, 0)),
            scratch_shapes=scratch,
        ),
        out_shape=jax.ShapeDtypeStruct((dbr.shape[0] if whole else tokens, width), dtype),
        compiler_params=params(48),
        cost_estimate=cost(6 * tokens * width * width),
    )(table, dbr, *grads, *pieces)


def place_kernel(table, in_ref, old_ref, out_ref):
    del table, old_ref
    out_ref[...] = in_ref[...].astype(out_ref.dtype)


def placed(part, array, start, tile):
    rows, width = part.shape
    return pl.pallas_call(
        place_kernel,
        grid_spec=pltpu.PrefetchScalarGridSpec(
            num_scalar_prefetch=1,
            grid=(rows // tile,),
            in_specs=[pl.BlockSpec((tile, width), lambda i, t: (i, 0)), ANY],
            out_specs=pl.BlockSpec((tile, width), lambda i, t: (i + t[0], 0)),
        ),
        out_shape=jax.ShapeDtypeStruct(array.shape, array.dtype),
        input_output_aliases={2: 0},
        cost_estimate=CHEAP,
    )((start // tile).astype(jnp.int32).reshape(1), part, array)


BQ = 256
BK_FWD = 512
BK_BACK = 256
VROWS = HDIM + 16


def lanes_where(condition):
    return jnp.where(condition(lane_iota((1, LANES))), 1.0, 0.0).astype(BF)


def spread_pairs(whole, source, features, group):
    for g in range(group):
        whole[:, 2 * g * LANES : (2 * g + 1) * LANES] = source[:, g * LANES : (g + 1) * LANES]
        whole[:, (2 * g + 1) * LANES : (2 * g + 2) * LANES] = features[...]


def staggered(count, load, work, finish, depth=1):
    loaded = [load(g) for g in range(min(depth, count))]
    worked = None
    for g in range(count):
        if g + depth < count:
            loaded.append(load(g + depth))
        result = work(g, loaded.pop(0))
        if worked is not None:
            finish(g - 1, worked)
        worked = result
    finish(count - 1, worked)


def attend_kernel(group, extra, spans, q_ref, k_ref, v_ref, kf_ref, qf_ref, *rest):
    o_ref, lse_ref, kx, vt, qx, best, accum = rest[extra:]
    block = pl.program_id(2)
    where = (pl.program_id(0) * pl.num_programs(2) + block) * 2
    row_len = k_ref.shape[0]

    @pl.when(block == 0)
    def _():
        spread_pairs(kx, k_ref, kf_ref, group)
        for g in range(group):
            for b in range(0, row_len, 256):
                turned = v_ref[b : b + 256, g * LANES : (g + 1) * LANES].astype(F32).T.astype(BF)
                for h in range(2):
                    vt[2 * g + h, :HDIM, b : b + 256] = turned[h * HDIM : (h + 1) * HDIM]
                    vt[2 * g + h, HDIM:, b : b + 256] = jnp.ones((16, 256), BF)

    qf = qf_ref[...]
    even, odd = lanes_where(lambda lane: lane < HDIM), lanes_where(lambda lane: lane >= HDIM)
    for g in range(group):
        q = q_ref[:, g * LANES : (g + 1) * LANES]
        qx[g, :BQ, :LANES] = q * even
        qx[g, BQ:, :LANES] = q * odd
        qx[g, :BQ, LANES:] = qf
        qx[g, BQ:, LANES:] = qf
    best[...] = jnp.full_like(best, NEGATIVE)
    accum[...] = jnp.zeros_like(accum)
    first, count = spans[where], spans[where + 1]

    def step(j, state):
        at = pl.multiple_of(first + j * BK_FWD, LANES)

        def load(g):
            return dot_bt(kx[pl.ds(at, BK_FWD), 2 * g * LANES : 2 * (g + 1) * LANES], qx[g])

        def work(g, scores):
            old = best[g]
            new = jnp.maximum(old, jnp.max(scores, axis=0, keepdims=True))
            best[g] = new
            return jnp.exp(scores - new).astype(BF), jnp.exp(old - new)

        def finish(g, worked):
            soft, factor = worked
            for h in range(2):
                cols = slice(h * BQ, (h + 1) * BQ)
                values = vt[2 * g + h, :, pl.ds(at, BK_FWD)]
                accum[g, :, cols] = accum[g, :, cols] * factor[:, cols] + dot(values, soft[:, cols])

        staggered(group, load, work, finish, 2)
        return state

    lax.fori_loop(0, count, step, 0)
    for g in range(group):
        total = accum[g, HDIM : HDIM + 1]
        lse = best[g] + jnp.log(total)
        lse_ref[2 * g] = lse[:, :BQ]
        lse_ref[2 * g + 1] = lse[:, BQ:]
        turned = accum[g, :HDIM] / total
        turned = jnp.concatenate([turned[:, :BQ], turned[:, BQ:]], axis=0)
        o_ref[:, g * LANES : (g + 1) * LANES] = turned.T.astype(BF)


def attend(q, k, v, key_feat, query_feat, spans, rows, group, after=()):
    tokens, width = q.shape
    row_len = k.shape[0] // rows
    blocks = tokens // rows // BQ
    of_q = lambda r, p, i, *_: (r * blocks + i, p)
    of_k = lambda r, p, i, *_: (r, p)
    wide = group * LANES
    return pl.pallas_call(
        functools.partial(attend_kernel, group, len(after)),
        grid_spec=pltpu.PrefetchScalarGridSpec(
            num_scalar_prefetch=1,
            grid=(rows, PAIRS // group, blocks),
            in_specs=[
                pl.BlockSpec((BQ, wide), of_q),
                pl.BlockSpec((row_len, wide), of_k),
                pl.BlockSpec((row_len, wide), of_k),
                pl.BlockSpec((row_len, LANES), lambda r, p, i, *_: (r, 0)),
                pl.BlockSpec((BQ, LANES), lambda r, p, i, *_: (r * blocks + i, 0)),
            ]
            + [ANY] * len(after),
            out_specs=[
                pl.BlockSpec((BQ, wide), of_q),
                pl.BlockSpec((2 * group, 1, BQ), lambda r, p, i, *_: (p, 0, r * blocks + i)),
            ],
            scratch_shapes=[
                pltpu.VMEM((row_len, 2 * wide), BF),
                pltpu.VMEM((2 * group, VROWS, row_len), BF),
                pltpu.VMEM((group, 2 * BQ, 2 * LANES), BF),
                pltpu.VMEM((group, 1, 2 * BQ), F32),
                pltpu.VMEM((group, VROWS, 2 * BQ), F32),
            ],
        ),
        out_shape=[
            jax.ShapeDtypeStruct((tokens, width), BF),
            jax.ShapeDtypeStruct((HEADS, 1, tokens), F32),
        ],
        compiler_params=params(56),
        cost_estimate=cost(4 * tokens * row_len * width),
    )(spans, q, k, v, key_feat, query_feat, *after)


def attend_back_kernel(
    group, base, extra, spans, q_ref, do_ref, k_ref, v_ref, kf_ref, qf_ref, cq_ref, sq_ref, ck_ref, sk_ref, *rest,
):
    dq_ref, dk_ref, dv_ref, kx, vx, kt, qx, dox, dq_acc, dk_acc, dv_acc = rest[extra:]
    block = pl.program_id(2)
    pair = base + pl.program_id(1) * group
    where = (pl.program_id(0) * pl.num_programs(2) + block) * 2
    row_len = k_ref.shape[0]

    @pl.when(block == 0)
    def _():
        spread_pairs(kx, k_ref, kf_ref, group)
        spread_pairs(vx, v_ref, kf_ref, group)
        for g in range(group):
            for b in range(0, row_len, 256):
                turned = k_ref[b : b + 256, g * LANES : (g + 1) * LANES].astype(F32).T.astype(BF)
                kt[g * LANES : (g + 1) * LANES, b : b + 256] = turned
        dk_acc[...] = jnp.zeros_like(dk_acc)
        dv_acc[...] = jnp.zeros_like(dv_acc)

    qf = qf_ref[...]
    even, odd = lanes_where(lambda lane: lane < HDIM), lanes_where(lambda lane: lane >= HDIM)
    for g in range(group):
        cols = slice(g * LANES, (g + 1) * LANES)
        for whole, source in ((qx, q_ref[:, cols]), (dox, do_ref[:, cols])):
            whole[g, :BQ, :LANES] = source * even
            whole[g, BQ:, :LANES] = source * odd
        for h in range(2):
            head = 2 * (pair + g) + h

            def at(lane, starts):
                return functools.reduce(jnp.logical_or, [lane == start + head for start in starts])

            of_lse = lanes_where(lambda lane: (lane < SEG) | at(lane, (8, 20, 32)))
            of_delta = lanes_where(lambda lane: at(lane, (44, 56, 68)))
            qx[g, h * BQ : (h + 1) * BQ, LANES:] = qf * of_lse
            dox[g, h * BQ : (h + 1) * BQ, LANES:] = qf * of_delta
    dq_acc[...] = jnp.zeros_like(dq_acc)
    first, count = spans[where], spans[where + 1]

    def step(j, state):
        at = pl.multiple_of(first + j * BK_BACK, LANES)

        def load(g):
            twice = slice(2 * g * LANES, (2 * g + 2) * LANES)
            return dot_bt(kx[pl.ds(at, BK_BACK), twice], qx[g]), dot_bt(vx[pl.ds(at, BK_BACK), twice], dox[g])

        def work(g, loaded):
            probs = jnp.exp(loaded[0])
            return probs.astype(BF), (probs * loaded[1]).astype(BF)

        def finish(g, worked):
            probs, grad = worked
            cols = slice(g * LANES, (g + 1) * LANES)
            dv_acc[pl.ds(at, BK_BACK), cols] += dot(probs, dox[g, :, :LANES])
            dk_acc[pl.ds(at, BK_BACK), cols] += dot(grad, qx[g, :, :LANES])
            for h in range(2):
                rows = slice(g * LANES + h * HDIM, g * LANES + (h + 1) * HDIM)
                dq_acc[rows] += dot(kt[rows, pl.ds(at, BK_BACK)], grad[:, h * BQ : (h + 1) * BQ])

        staggered(group, load, work, finish)
        return state

    lax.fori_loop(0, count, step, 0)
    for g in range(group):
        cols = slice(g * LANES, (g + 1) * LANES)
        dq = dq_acc[cols].T * (1.0 / math.sqrt(HDIM))
        dq_ref[:, cols] = (dq * cq_ref[...] - halves_swapped(dq) * sq_ref[...]).astype(BF)

    @pl.when(block == pl.num_programs(2) - 1)
    def _():
        for b in range(0, row_len, 256):
            part = pl.ds(b, 256)
            cosine, sine = ck_ref[part, :], sk_ref[part, :]
            for g in range(group):
                cols = slice(g * LANES, (g + 1) * LANES)
                dk = dk_acc[part, cols]
                dk_ref[part, cols] = (dk * cosine - halves_swapped(dk) * sine).astype(BF)
            dv_ref[part, :] = dv_acc[part, :].astype(BF)


def attend_back(q, do, k, v, key_feat, query_feat, spans, tables_q, tables_k, rows, group, base, pairs, after=()):
    tokens, width = q.shape
    row_len = k.shape[0] // rows
    blocks = tokens // rows // BQ
    start = base // group
    of_q = lambda r, p, i, *_: (r * blocks + i, start + p)
    of_k = lambda r, p, i, *_: (r, start + p)
    per_q = pl.BlockSpec((BQ, LANES), lambda r, p, i, *_: (r * blocks + i, 0))
    per_k = pl.BlockSpec((row_len, LANES), lambda r, p, i, *_: (r, 0))
    wide = group * LANES
    return pl.pallas_call(
        functools.partial(attend_back_kernel, group, base, len(after)),
        grid_spec=pltpu.PrefetchScalarGridSpec(
            num_scalar_prefetch=1,
            grid=(rows, pairs // group, blocks),
            in_specs=[
                pl.BlockSpec((BQ, wide), of_q),
                pl.BlockSpec((BQ, wide), of_q),
                pl.BlockSpec((row_len, wide), of_k),
                pl.BlockSpec((row_len, wide), of_k),
                per_k,
                per_q,
                per_q,
                per_q,
                per_k,
                per_k,
            ]
            + [ANY] * len(after),
            out_specs=[
                pl.BlockSpec((BQ, wide), lambda r, p, i, *_: (r * blocks + i, p)),
                pl.BlockSpec((row_len, wide), lambda r, p, i, *_: (r, p)),
                pl.BlockSpec((row_len, wide), lambda r, p, i, *_: (r, p)),
            ],
            scratch_shapes=[
                pltpu.VMEM((row_len, 2 * wide), BF),
                pltpu.VMEM((row_len, 2 * wide), BF),
                pltpu.VMEM((wide, row_len), BF),
                pltpu.VMEM((group, 2 * BQ, 2 * LANES), BF),
                pltpu.VMEM((group, 2 * BQ, 2 * LANES), BF),
                pltpu.VMEM((wide, BQ), F32),
                pltpu.VMEM((row_len, wide), F32),
                pltpu.VMEM((row_len, wide), F32),
            ],
        ),
        out_shape=[
            jax.ShapeDtypeStruct((tokens, pairs * LANES), BF),
            jax.ShapeDtypeStruct((rows * row_len, pairs * LANES), BF),
            jax.ShapeDtypeStruct((rows * row_len, pairs * LANES), BF),
        ],
        compiler_params=params(56),
        cost_estimate=cost(8 * tokens * row_len * pairs * LANES),
    )(spans, q, do, k, v, key_feat, query_feat, *tables_q, *tables_k, *after)


FF_CHUNK = 512
SUB = 256


def normalize(hidden):
    average = jnp.mean(hidden, -1, keepdims=True)
    centred = hidden - average
    inverse = lax.rsqrt(jnp.mean(centred * centred, -1, keepdims=True) + EPSILON)
    return centred * inverse, inverse


def norm_back(scaled, normalized, inverse):
    return inverse * (
        scaled
        - jnp.mean(scaled, -1, keepdims=True)
        - normalized * jnp.mean(scaled * normalized, -1, keepdims=True)
    )


def split_two(value):
    high = value.astype(BF)
    return high, (value - high.astype(F32)).astype(BF)


def mix_kernel(counts, table, att_ref, x_ref, qf_ref, g1_ref, g2_ref, *rest):
    pieces, rest = rest[: sum(counts)], rest[sum(counts) :]
    nl_ref, stat_ref, hid_ref, fg_ref, fu_ref, out_ref, pool_ref, wo, ws, wd, sems = rest
    groups = grouped_copies(counts, table, pieces, (wo, ws, wd), sems)
    step, begin = pl.program_id(1), (pl.program_id(0) == 0) & (pl.program_id(1) == 0)

    @pl.when(begin)
    def _():
        start_all(*groups)
        wait_all(*groups)

    ff = wd.shape[0]
    tile, chunks = att_ref.shape[0], wd.shape[0] // FF_CHUNK
    subs, opened, pools = tile // SUB, [], []
    lanes = lane_iota((SUB, LANES))

    def open_next():
        rows = slice(len(opened) * SUB, (len(opened) + 1) * SUB)
        branch = dot(att_ref[rows], wo[...])
        unit, inverse1 = normalize(x_ref[rows].astype(F32) + branch)
        normed = unit * g1_ref[...]
        low = normed.astype(BF)
        nl_ref[rows] = low
        opened.append([low, normed, inverse1, rows])

    def close(sub):
        _, hidden_sum, inverse1, rows = opened[sub]
        unit2, inverse2 = normalize(hidden_sum)
        output = unit2 * g2_ref[...]
        out_ref[rows] = output.astype(BF)
        stat_ref[rows] = jnp.where(lanes == 0, inverse1, inverse2)
        high, rest_low = split_two(output)
        member = qf_ref[rows]
        pools.append((dot_at(member, high) + dot_at(member, rest_low))[:SEG])

    def load(n):
        low, c = opened[n // chunks][0], n % chunks
        cols = slice(c * FF_CHUNK, (c + 1) * FF_CHUNK)
        return dot(low, ws[:, cols]), dot(low, ws[:, ff + c * FF_CHUNK : ff + (c + 1) * FF_CHUNK])

    def work(n, loaded):
        sub, c = n // chunks, n % chunks
        if c == 1 and sub + 1 < subs:
            open_next()
        if c == 2 and sub > 0:
            close(sub - 1)
        rows, cols = opened[sub][3], slice(c * FF_CHUNK, (c + 1) * FF_CHUNK)
        gate, up = loaded
        sig = 0.5 + 0.5 * jnp.tanh(0.5 * gate)
        silu = gate * sig
        hidden = (silu * up).astype(BF)
        hid_ref[rows, cols] = hidden
        fg_ref[rows, cols] = (up * (sig + silu * (1.0 - sig))).astype(BF)
        fu_ref[rows, cols] = silu.astype(BF)
        return hidden

    def finish(n, hidden):
        c = n % chunks
        opened[n // chunks][1] = opened[n // chunks][1] + dot(hidden, wd[c * FF_CHUNK : (c + 1) * FF_CHUNK, :])

    open_next()
    staggered(subs * chunks, load, work, finish)
    close(subs - 1)
    sums = functools.reduce(jnp.add, pools)

    @pl.when(step == 0)
    def _():
        pool_ref[0] = sums

    @pl.when(step > 0)
    def _():
        pool_ref[0] += sums


def mix(attended, x, query_feat, gain1, gain2, weights, rows, tile, after):
    tokens, width = x.shape
    steps = tokens // rows // tile
    ff = weights[2].shape[0]
    counts, pieces, table, scratch = weight_operands(weights, (0, 0), after)
    wide, narrow = row_specs([None], tile, width, steps), row_specs([None], tile, LANES, steps)
    hidden, fixed = row_specs([None], tile, ff, steps), [pl.BlockSpec((1, width), lambda r, i, *_: (0, 0))]
    return pl.pallas_call(
        functools.partial(mix_kernel, counts),
        grid_spec=pltpu.PrefetchScalarGridSpec(
            num_scalar_prefetch=1,
            grid=(rows, steps),
            in_specs=wide * 2 + narrow + fixed * 2 + [ANY] * len(pieces),
            out_specs=wide + narrow + hidden * 3 + wide + [pl.BlockSpec((1, SEG, width), lambda r, i, *_: (r, 0, 0))],
            scratch_shapes=scratch,
        ),
        out_shape=[
            jax.ShapeDtypeStruct((tokens, width), BF),
            jax.ShapeDtypeStruct((tokens, LANES), F32),
            jax.ShapeDtypeStruct((tokens, ff), BF),
            jax.ShapeDtypeStruct((tokens, ff), BF),
            jax.ShapeDtypeStruct((tokens, ff), BF),
            jax.ShapeDtypeStruct((tokens, width), BF),
            jax.ShapeDtypeStruct((rows, SEG, width), F32),
        ],
        compiler_params=params(58),
        cost_estimate=cost(2 * tokens * width * (width + 3 * ff)),
    )(table, attended, x, query_feat, gain1, gain2, *pieces)


def hidden_back_kernel(counts, parts, table, *rest):
    cot_refs, rest = rest[:parts], rest[parts:]
    out_ref, stat_ref, qf_ref, dp_ref, fg_ref, fu_ref, g2_ref = rest[:7]
    pieces, rest = rest[7 : 7 + sum(counts)], rest[7 + sum(counts) :]
    dffn_ref, dgu_ref, gf_ref, wd, sems = rest
    groups = grouped_copies(counts, table, pieces, [wd], sems)
    begin = (pl.program_id(0) == 0) & (pl.program_id(1) == 0)

    @pl.when(begin)
    def _():
        start_all(*groups)
        gf_ref[...] = jnp.zeros_like(gf_ref)

    gain2 = g2_ref[...]
    high, rest_low = split_two(dp_ref[0])
    tile, width = out_ref.shape
    ff = wd.shape[0]
    subs, chunks, opened = tile // SUB, ff // FF_CHUNK, []

    def open_next():
        rows = slice(len(opened) * SUB, (len(opened) + 1) * SUB)
        member = qf_ref[rows]
        upstream = row_tile(table, cot_refs, rows).astype(F32) + dot(member, high) + dot(member, rest_low)
        unit2 = out_ref[rows].astype(F32) / gain2
        dffn = norm_back(upstream * gain2, unit2, stat_ref[rows, 1:2]).astype(BF)
        dffn_ref[rows] = dffn
        gf_ref[...] += jnp.sum((upstream * unit2).reshape(SUB // 8, 8, width), axis=0)
        opened.append((dffn, rows))

    def load(n):
        c = n % chunks
        return dot_bt(opened[n // chunks][0], wd[c * FF_CHUNK : (c + 1) * FF_CHUNK, :])

    def work(n, dhid):
        sub, c = n // chunks, n % chunks
        if c == 1 and sub + 1 < subs:
            open_next()
        rows, cols = opened[sub][1], slice(c * FF_CHUNK, (c + 1) * FF_CHUNK)
        dgu_ref[rows, cols] = (dhid * fg_ref[rows, cols].astype(F32)).astype(BF)
        after = slice(ff + c * FF_CHUNK, ff + (c + 1) * FF_CHUNK)
        dgu_ref[rows, after] = (dhid * fu_ref[rows, cols].astype(F32)).astype(BF)

    open_next()

    @pl.when(begin)
    def _():
        wait_all(*groups)

    staggered(subs * chunks, load, work, lambda n, worked: None)


def hidden_back(cots, lead, output, stat, query_feat, dpool, factors, gain2, down, rows, tile):
    tokens, width = output.shape
    ff = down.shape[0]
    steps = tokens // rows // tile
    counts, pieces, table, scratch = weight_operands([down], (lead, 0))
    wide, narrow = row_specs([None], tile, width, steps), row_specs([None], tile, LANES, steps)
    hidden = row_specs([None], tile, ff, steps)
    return pl.pallas_call(
        functools.partial(hidden_back_kernel, counts, len(cots)),
        grid_spec=pltpu.PrefetchScalarGridSpec(
            num_scalar_prefetch=1,
            grid=(rows, steps),
            in_specs=row_specs(cots, tile, width, steps)
            + wide
            + narrow * 2
            + [pl.BlockSpec((1, LANES, width), lambda r, i, *_: (r, 0, 0))]
            + hidden * 2
            + [pl.BlockSpec((1, width), lambda r, i, *_: (0, 0))]
            + [ANY] * len(pieces),
            out_specs=wide + row_specs([None], tile, 2 * ff, steps) + [pl.BlockSpec((8, width), lambda r, i, *_: (0, 0))],
            scratch_shapes=scratch,
        ),
        out_shape=[
            jax.ShapeDtypeStruct((tokens, width), BF),
            jax.ShapeDtypeStruct((tokens, 2 * ff), BF),
            jax.ShapeDtypeStruct((8, width), F32),
        ],
        compiler_params=params(58),
        cost_estimate=cost(4 * tokens * width * ff),
    )(table, *cots, output, stat, query_feat, dpool, *factors, gain2, *pieces)


def branch_back_kernel(counts, table, *refs):
    dffn_ref, nl_ref, stat_ref, qf_ref, dgu_ref, att_ref, lse_ref, g1_ref, head_ref = refs[:9]
    rest = refs[9:]
    pieces, rest = rest[: sum(counts)], rest[sum(counts) :]
    dbr_ref, datt_ref, feat_ref, ga_ref, wo, ws, sems = rest
    groups = grouped_copies(counts, table, pieces, (wo, ws), sems)
    begin = (pl.program_id(0) == 0) & (pl.program_id(1) == 0)

    @pl.when(begin)
    def _():
        start_all(*groups)
        ga_ref[...] = jnp.zeros_like(ga_ref)
        wait_all(*groups)

    gain1, heads = g1_ref[...], head_ref[...]
    width = nl_ref.shape[1]
    rows_of = lambda n: slice(n * SUB, (n + 1) * SUB)

    def load(n):
        rows = rows_of(n)
        return dffn_ref[rows].astype(F32) + dot_bt(dgu_ref[rows], ws[...])

    def work(n, dnormed):
        rows = rows_of(n)
        unit1 = nl_ref[rows].astype(F32) / gain1
        dbr = norm_back(dnormed * gain1, unit1, stat_ref[rows, 0:1]).astype(BF)
        dbr_ref[rows] = dbr
        ga_ref[...] += jnp.sum((dnormed * unit1).reshape(SUB // 8, 8, width), axis=0)
        return dbr

    def finish(n, dbr):
        rows = rows_of(n)
        datt = dot_bt(dbr, wo[...]).astype(BF)
        datt_ref[rows] = datt
        high, rest_low = split_two(datt.astype(F32) * att_ref[rows].astype(F32))
        delta = dot(high, heads) + dot(rest_low, heads)
        feat = qf_ref[rows].astype(F32)
        for value, start in ((lse_ref[rows], 8), (delta, 44)):
            left = -value
            for part_n in range(3):
                part = left.astype(BF).astype(F32)
                left = left - part
                feat = feat + pltpu.roll(part, start + HEADS * part_n, 1)
        feat_ref[rows] = feat.astype(BF)

    staggered(dgu_ref.shape[0] // SUB, load, work, finish)


def branch_back(dffn, low, stat, query_feat, dgu, attended, lse, gain1, weights, rows, tile, after=()):
    tokens, width = low.shape
    ff = dgu.shape[1] // 2
    steps = tokens // rows // tile
    counts, pieces, table, scratch = weight_operands(weights, (0, 0), after)
    wide, narrow = row_specs([None], tile, width, steps), row_specs([None], tile, LANES, steps)
    hidden = row_specs([None], tile, 2 * ff, steps)
    heads = (jnp.arange(width)[:, None] // HDIM == jnp.arange(LANES)[None, :]).astype(BF)
    return pl.pallas_call(
        functools.partial(branch_back_kernel, counts),
        grid_spec=pltpu.PrefetchScalarGridSpec(
            num_scalar_prefetch=1,
            grid=(rows, steps),
            in_specs=wide * 2
            + narrow * 2
            + hidden
            + wide
            + narrow
            + [pl.BlockSpec((1, width), lambda r, i, *_: (0, 0))]
            + [pl.BlockSpec((width, LANES), lambda r, i, *_: (0, 0))]
            + [ANY] * len(pieces),
            out_specs=wide * 2 + narrow + [pl.BlockSpec((8, width), lambda r, i, *_: (0, 0))],
            scratch_shapes=scratch,
        ),
        out_shape=[
            jax.ShapeDtypeStruct((tokens, width), BF),
            jax.ShapeDtypeStruct((tokens, width), BF),
            jax.ShapeDtypeStruct((tokens, LANES), BF),
            jax.ShapeDtypeStruct((8, width), F32),
        ],
        compiler_params=params(58),
        cost_estimate=cost(2 * tokens * width * (width + 2 * ff)),
    )(table, dffn, low, stat, query_feat, dgu, attended, lse, gain1, heads, *pieces)


def bits_of(axis):
    size, bit = lax.axis_size(axis), 1
    while bit < size:
        yield bit
        bit *= 2


def in_order(parts, index):
    shape = (2,) + (1,) * parts[0].ndim
    first = lax.broadcasted_iota(jnp.int32, shape, 0) == index
    return jnp.where(first, parts[0][None], parts[1][None])


def add(first, *others):
    total = first.astype(F32)
    for other in others:
        total = total + other.astype(F32)
    return total.astype(BF)


def reduction(part, short):
    rows, cols = part.shape
    shards = lax.axis_size("fsdp")
    mine, place = lax.axis_index("fsdp"), lax.axis_index("blk")
    core, side = place % 2, place // 2 % 2
    now = part.reshape(shards, 2, rows // shards // 2, cols)
    (came,) = yield [take(now, 1 - core, 1)], [("blk", 1)]
    now = add(take(now, core, 1), came)
    bit = shards // 2
    while bit:
        now = now.reshape(2, bit, -1, cols)
        own = mine // bit % 2
        (came,) = yield [take(now, 1 - own, 0)], [("fsdp", bit)]
        now = add(take(now, own, 0), came)
        bit //= 2
    now = now.reshape(2, -1, cols)
    (came,) = yield [take(now, 1 - side, 0)], [("blk", 2)]
    now = add(take(now, side, 0), came)
    bits = [bit for bit in bits_of("blk") if bit > 2]
    if short:
        for bit in bits:
            (came,) = yield [now], [("blk", bit)]
            now = add(now, came)
    else:
        for bit in bits:
            now = now.reshape(2, -1, cols)
            own = place // bit % 2
            (came,) = yield [take(now, 1 - own, 0)], [("blk", bit)]
            now = add(take(now, own, 0), came)
        for bit in bits[::-1]:
            (came,) = yield [now], [("blk", bit)]
            now = in_order([now, came], place // bit % 2).reshape(-1, cols)
    now = now.reshape(-1, cols)
    (came,) = yield [now], [("blk", 2)]
    now = in_order([now, came], side).reshape(-1, cols)
    (came,) = yield [now], [("blk", 1)]
    yield [now, came], None


class Reduction:
    def __init__(self, part, short=False):
        fsdp_bits, lines = len(list(bits_of("fsdp"))), len(list(bits_of("blk"))) - 2
        self.left = 4 + fsdp_bits + lines * (1 if short else 2)
        self.stages = reduction(part, short)
        self.sends, self.routes = next(self.stages)

    @property
    def done(self):
        return self.routes is None

    @property
    def result(self):
        return self.sends

    def launch(self):
        came = [flipped(a, *route) for a, route in zip(self.sends, self.routes)]
        return self.sends, came

    def take_in(self, came):
        self.left -= 1
        self.sends, self.routes = self.stages.send(came)


def beside(work, launches, joins=None):
    sent, flights = [], []
    for r in launches:
        if not r.done:
            sends, came = r.launch()
            sent += sends
            flights.append((r, came))
    values = list(work(sent))
    late = []
    if joins is not None:
        late = [f for f in flights if f[0] not in [j for j in joins if isinstance(j, Reduction)]]
        flights = [f for f in flights if f not in late] + [j for j in joins if not isinstance(j, Reduction)]
    count = len(values)
    both = tied(values + [a for _, came in flights for a in came])
    at = count
    for r, came in flights:
        r.take_in(both[at : at + len(came)])
        at += len(came)
    return both[:count], late


def turned(block):
    return block.astype(F32).T.astype(BF)


def swiglu_part_kernel(low_ref, grad_ref, out_ref, low_turned):
    tokens = low_ref.shape[0]

    @pl.when(pl.program_id(0) == 0)
    def _():
        for b in range(0, tokens, 256):
            low_turned[:, b : b + 256] = turned(low_ref[b : b + 256, :])

    part = dot(low_turned[...], grad_ref[...]).astype(BF)
    taken, split, rows, cols = out_ref.shape
    for n in range(taken):
        for f in range(split):
            out_ref[n, f] = part[f * rows : (f + 1) * rows, n * cols : (n + 1) * cols]


def down_part_kernel(hidden_ref, dffn_ref, old_ref, out_ref):
    del old_ref
    part = dot(turned(hidden_ref[...]), dffn_ref[...]).astype(BF)
    rows, cols = out_ref.shape[2:]
    across = part.shape[1] // cols
    for n in range(out_ref.shape[0]):
        down, along = n // across * rows, n % across * cols
        out_ref[n, 0] = part[down : down + rows, along : along + cols]


def shares_fit(low, hidden):
    blocks, split = lax.axis_size("blk"), lax.axis_size("fsdp")
    width, ff = low.shape[1], hidden.shape[1]
    cols = 2 * ff // blocks
    return cols % LANES == 0 and width % cols == 0 and ff * width // (split * blocks * cols) * 2 == width // split


def feed_forward_shares(low, d_gate_up, hidden, d_ffn):
    blocks, split = lax.axis_size("blk"), lax.axis_size("fsdp")
    tokens, width = low.shape
    ff = hidden.shape[1]
    cols, rows = 2 * ff // blocks, width // split
    down_rows = rows // 2
    across = width // cols
    shape = jax.ShapeDtypeStruct((blocks, split, rows + down_rows, cols), BF)
    whole = lambda a: pl.BlockSpec(a.shape, lambda *_: (0, 0))
    shares = pl.pallas_call(
        swiglu_part_kernel,
        grid=(blocks // 2,),
        in_specs=[whole(low), pl.BlockSpec((tokens, 2 * cols), lambda j: (0, j))],
        out_specs=pl.BlockSpec((2, split, rows, cols), lambda j: (j, 0, 0, 0)),
        out_shape=shape,
        scratch_shapes=[pltpu.VMEM((width, tokens), BF)],
        compiler_params=params(48),
        cost_estimate=cost(4 * tokens * width * ff),
    )(low, d_gate_up)
    taken = 2 * down_rows
    steps = ff // split // taken
    return pl.pallas_call(
        down_part_kernel,
        grid=(split, steps),
        in_specs=[pl.BlockSpec((tokens, taken), lambda f, j: (0, f * steps + j)), whole(d_ffn), ANY],
        out_specs=pl.BlockSpec((2 * across, 1, down_rows, cols), lambda f, j: (j, f, 2, 0)),
        out_shape=shape,
        input_output_aliases={2: 0},
        compiler_params=params(48),
        cost_estimate=cost(2 * tokens * width * ff),
    )(hidden, d_ffn, shares)


def plain_sum(part):
    part = lax.psum_scatter(part, "fsdp", scatter_dimension=0, tiled=True)
    return lax.psum(part, "blk").astype(F32)


def weight_grad(pairs, beside_it=None, after=()):
    arrays, left = [], []
    for a, b in pairs:
        place = [n for n, other in enumerate(arrays) if other is a]
        if not place:
            arrays.append(a)
            place = [len(arrays) - 1]
        arrays.append(b)
        left.append((place[0], len(arrays) - 1))
    cols = sum(b.shape[1] for _, b in pairs)
    last = []
    if beside_it is not None:
        last = [beside_it]
        cols += beside_it.shape[1]

    (shared,) = {a for a, _ in left}

    def kernel(*refs):
        out_ref, flipped_ref, at = refs[-2], refs[-1], 0
        for b in range(0, flipped_ref.shape[1], 256):
            flipped_ref[:, b : b + 256] = turned(refs[shared][b : b + 256, :])
        for _, b in left:
            part = dot(flipped_ref[...], refs[b][...]).astype(BF)
            out_ref[:, at : at + part.shape[1]] = part
            at += part.shape[1]
        if last:
            out_ref[:, at:] = refs[len(arrays)][...]

    whole = pl.BlockSpec(memory_space=pltpu.VMEM)
    return pl.pallas_call(
        kernel,
        in_specs=[whole] * (len(arrays) + len(last)) + [ANY] * len(after),
        scratch_shapes=[pltpu.VMEM(pairs[0][0].shape[::-1], BF)],
        out_shape=jax.ShapeDtypeStruct((pairs[0][0].shape[1], cols), BF),
        compiler_params=params(56),
        cost_estimate=cost(2 * pairs[0][0].shape[0] * pairs[0][0].shape[1] * cols),
    )(*arrays, *last, *after)


def unfold_kernel(kinds, columns, table, *refs):
    own = pl.program_id(0) == table[0]
    values, at = [], 0
    for kind in kinds:
        values.append(refs[at][...] if kind == 1 else jnp.where(own, refs[at][...], refs[at + 1][...]))
        at += kind
    for ref, parts in zip(refs[at:], columns):
        to = 0
        for n, start, wide in parts:
            ref[:, to : to + wide] = values[n][:, start : start + wide].astype(F32)
            to += wide


def unfold(results, columns):
    rows = sum(a.shape[0] for a in results[0]) // 2
    block = rows // 2 if rows % 32 == 0 else rows
    steps = rows // block
    maps = {2: lambda c, i, t: (i, 0), 1: lambda c, i, t: (c * steps + i, 0)}
    return pl.pallas_call(
        functools.partial(unfold_kernel, [len(r) for r in results], columns),
        grid_spec=pltpu.PrefetchScalarGridSpec(
            num_scalar_prefetch=1,
            grid=(2, steps),
            in_specs=[pl.BlockSpec((block, a.shape[1]), maps[len(r)]) for r in results for a in r],
            out_specs=[pl.BlockSpec((block, sum(p[2] for p in parts)), maps[1]) for parts in columns],
        ),
        out_shape=[jax.ShapeDtypeStruct((2 * rows, sum(p[2] for p in parts)), F32) for parts in columns],
        compiler_params=params(40),
        cost_estimate=CHEAP,
    )((lax.axis_index("blk") % 2).reshape(1), *[a for r in results for a in r])


def spread_kernel(both_ref, swiglu_ref, down_ref):
    rows = swiglu_ref.shape[0]
    swiglu_ref[...] = both_ref[0, :rows, :].astype(F32)
    down_ref[...] = both_ref[0, rows:, :].astype(F32)


def spread(both, width):
    blocks, height, cols = both.shape
    rows = height * 2 // 3
    across = width // cols
    return pl.pallas_call(
        spread_kernel,
        grid=(blocks,),
        in_specs=[pl.BlockSpec((1, height, cols), lambda n: (n, 0, 0))],
        out_specs=[
            pl.BlockSpec((rows, cols), lambda n: (0, n)),
            pl.BlockSpec((rows // 2, cols), lambda n: (n // across, n % across)),
        ],
        out_shape=[
            jax.ShapeDtypeStruct((rows, blocks * cols), F32),
            jax.ShapeDtypeStruct((blocks // across * (rows // 2), width), F32),
        ],
        compiler_params=params(40),
        cost_estimate=CHEAP,
    )(both)


def contrast(sums, lengths, pairing, row_mode, row_ids):
    rows, segs, width = sums.shape
    lengths = lengths.astype(F32)[..., None]
    pooled = sums / lengths
    inverse = lax.rsqrt(jnp.sum(pooled * pooled, -1, keepdims=True) + EMB_EPSILON)
    embedded = pooled * inverse
    own = rows * segs
    pair = jnp.stack([pairing, jnp.zeros_like(pairing)], axis=-1).reshape(own, 1)
    spare = jnp.concatenate([pair // 128, pair % 128, jnp.zeros((own, 126), jnp.int32)], axis=1)
    buffer = jnp.concatenate([embedded.reshape(own, width).astype(BF), spare.astype(BF)], axis=1)
    ids = row_ids
    for axis in ("fsdp", "blk") if row_mode else ("blk",):
        for bit in bits_of(axis):
            buffer = jnp.concatenate([buffer, flipped(buffer, axis, bit)], axis=0)
            if axis == "fsdp":
                ids = jnp.concatenate([ids, ids ^ bit])
            else:
                ids = jnp.concatenate([ids, ids ^ (bit * ROWS_PER_BLOCK)])
    total = buffer.shape[0]
    every = buffer[:, :width]
    pair_all = (buffer[:, width].astype(jnp.int32) * 128 + buffer[:, width + 1].astype(jnp.int32))[:, None]
    seg = jnp.arange(total, dtype=jnp.int32) % segs
    number = jnp.broadcast_to(ids[:, None], (total // segs, segs)).reshape(total) * (segs // 2) + seg // 2
    is_query = (seg % 2 == 0)[:, None]
    is_doc = (seg % 2 == 1)[None, :]
    target = is_query & is_doc & (pair_all == number[None, :])
    sims = dot_bt(every, every) / SOFTMAX_WARMTH
    masked = jnp.where(is_doc, sims, NEGATIVE)
    best = jnp.max(masked, -1, keepdims=True)
    log_total = best + jnp.log(jnp.sum(jnp.exp(masked - best), -1, keepdims=True))
    positive = jnp.sum(jnp.where(target, sims, 0.0), -1, keepdims=True)
    loss = jnp.sum(jnp.where(is_query[:own], log_total[:own] - positive[:own], 0.0))
    d_sims = CONTRAST_WEIGHT * (jnp.exp(masked - log_total) - target.astype(F32))
    d_sims = jnp.where(is_query, d_sims, 0.0).astype(BF)
    grad = (dot(d_sims[:own], every) + dot_at(d_sims[:, :own], every)) / SOFTMAX_WARMTH
    grad = grad.reshape(rows, segs, width)
    along = jnp.sum(embedded * grad, -1, keepdims=True)
    return loss, inverse * (grad - embedded * along) / lengths


ROWS_PER_BLOCK = 2


def shards(
    tokens,
    cotangent,
    segments,
    doc_lengths,
    positions,
    pairing,
    qkv_weight,
    out_weight,
    swiglu_weight,
    down_weight,
    attn_gain,
    ffn_gain,
):
    rows_here, shard_len, width = tokens.shape
    split = lax.axis_size("fsdp")
    mine = lax.axis_index("fsdp")
    place = lax.axis_index("blk")
    row_len = shard_len * split
    row_mode = split == rows_here == 2

    if row_mode:
        rows, per_row, query_start, lead = 1, row_len, 0, mine
        lengths = lax.dynamic_slice_in_dim(doc_lengths, mine, 1, 0)
        own_pairing = lax.dynamic_slice_in_dim(pairing.reshape(rows_here, -1), mine, 1, 0)
        row_ids = (place * rows_here + mine)[None]
    else:
        rows, per_row, query_start, lead = rows_here, shard_len, mine * shard_len, 0
        lengths, own_pairing = doc_lengths, pairing.reshape(rows_here, -1)
        row_ids = place * rows_here + jnp.arange(rows_here, dtype=jnp.int32)
    tokens_here = rows * per_row
    tile = min(512, per_row)
    small_tile = min(256, per_row)

    gains = jnp.stack([attn_gain, ffn_gain])
    if row_mode:
        qkv_share = flipped(share_of(qkv_weight), "fsdp", 1)
        (moved,) = tied([take(tokens, 1 - mine, 0)], [qkv_share])
        moved = flipped(moved, "fsdp", 1)
        qkv = from_shares(qkv_weight, qkv_share)
        gains = in_order([gains, flipped(gains, "fsdp", 1)], mine)
        gains = jnp.concatenate([gains[0], gains[1]], axis=1)
    else:
        qkv, swiglu = whole_weight(qkv_weight), whole_weight(swiglu_weight)
        gains = lax.all_gather(gains, "fsdp", axis=1, tiled=True)
    gain1, gain2 = gains[0:1].astype(F32), gains[1:2].astype(F32)

    order = jnp.arange(SEG, dtype=jnp.int32)
    ends = jnp.sum(jnp.where(order[None, :] <= order[:, None], lengths[:, None, :], 0), -1)
    starts = ends - lengths
    token = jnp.arange(row_len, dtype=jnp.int32)
    at = token[None, :, None]
    member = (at >= starts[:, None, :]) & (at < ends[:, None, :])
    first_of = jnp.max(jnp.where(at >= starts[:, None, :], starts[:, None, :], 0), -1)
    lane = jnp.arange(LANES, dtype=jnp.int32)
    frequency = ROPE_BASE ** (-2.0 * (lane % 32).astype(F32) / HDIM)
    angles = (token[None, :] - first_of).astype(F32)[..., None] * frequency
    cosine = jnp.cos(angles).reshape(-1, LANES)
    sine = (jnp.sin(angles) * jnp.where(lane % HDIM < 32, -1.0, 1.0)).reshape(-1, LANES)
    key_feat = jnp.where(member, 0.0, NEGATIVE)
    key_feat = jnp.concatenate([key_feat, jnp.ones((rows, row_len, 120), F32)], -1)
    key_feat = key_feat.astype(BF).reshape(-1, LANES)
    query_feat = jnp.pad(member.astype(BF), ((0, 0), (0, 0), (0, 120))).reshape(-1, LANES)

    def of_queries(table):
        if row_mode:
            return table
        table = table.reshape(rows, row_len, LANES)
        return lax.dynamic_slice_in_dim(table, query_start, per_row, 1).reshape(-1, LANES)

    tables_k = (cosine, sine)
    tables_q = (of_queries(cosine), of_queries(sine))
    query_feat = of_queries(query_feat)
    block_first = query_start + BQ * jnp.arange(per_row // BQ, dtype=jnp.int32)[None, :, None]
    low = jnp.max(jnp.where(block_first >= starts[:, None, :], starts[:, None, :], 0), -1)
    high = jnp.min(jnp.where(block_first + BQ - 1 < ends[:, None, :], ends[:, None, :], row_len), -1)
    low = low // LANES * LANES

    def spans_of(size):
        count = (high - low + size - 1) // size
        return jnp.stack([jnp.minimum(low, row_len - count * size), count], axis=-1).reshape(-1).astype(jnp.int32)

    spans, spans_back = spans_of(BK_FWD), spans_of(BK_BACK)

    if row_mode:
        tables = (*tables_q, qkv)
        share, *halves = tied([share_of(swiglu_weight), half_of(out_weight), half_of(down_weight)], [moved])
        share_came = flipped(share, "fsdp", 1)
        firsts = [flipped(h, "fsdp", 1) for h in halves]
        xs = [take(tokens, mine, 0), moved]
        projected = project(xs, lead, *tables, rows, small_tile, [share, *halves])
        query, key, value, x, share_came = tied([*projected, share_came])
        swiglu = from_shares(swiglu_weight, share_came)
        key_all, value_all = key, value
    else:
        query, key, value, x = project([tokens.reshape(-1, width)], 0, *tables_q, qkv, rows, small_tile)

        def along_row(part):
            part = part.reshape(rows, per_row, width)
            return lax.all_gather(part, "fsdp", axis=1, tiled=True).reshape(-1, width)

        key_all, value_all = along_row(key), along_row(value)
    attended, lse = attend(query, key_all, value_all, key_feat, query_feat, spans, rows, PAIRS)
    if row_mode:
        attended, *firsts = tied([attended, *firsts], [lse])
        outer, down = from_halves(out_weight, firsts[0]), from_halves(down_weight, firsts[1])
        cot_send = take(cotangent, 1 - mine + zero_after(firsts[1]), 0)
        cots = [take(cotangent, mine, 0), flipped(cot_send, "fsdp", 1)]
        after = [cot_send]
    else:
        outer, down = whole_weight(out_weight), whole_weight(down_weight)
        cots, after = [cotangent.reshape(-1, width)], []
    low_normed, stat, hidden, *factors, output, sums = mix(
        attended, x, query_feat, gain1, gain2, (outer, swiglu, down), rows, tile, after
    )
    if row_mode:
        sums, cots[1] = tied([sums, cots[1]])
        output_came = flipped(lax.dynamic_slice_in_dim(output, (1 - mine) * shard_len, shard_len, 0), "fsdp", 1)
    else:
        layer_output = output.reshape(tokens.shape)
        sums = lax.psum(sums, "fsdp")
    loss, d_pool = contrast(sums, lengths, own_pairing, row_mode, row_ids)
    d_pool = jnp.pad(d_pool, ((0, 0), (0, LANES - SEG), (0, 0)))
    lse_columns = jnp.pad(lse.reshape(HEADS, tokens_here).T, ((0, 0), (0, LANES - HEADS)))

    d_ffn, d_gate_up, gain2_part = hidden_back(
        cots, lead, output, stat, query_feat, d_pool, factors, gain2, down, rows, tile
    )
    fast = row_mode and shares_fit(low_normed, hidden)
    if fast:
        share = feed_forward_shares(low_normed, d_gate_up, hidden, d_ffn)
        after = [share]
        share = lax.psum_scatter(share.reshape(-1, share.shape[-1]), ("blk", "fsdp"), scatter_dimension=0, tiled=True)
    else:
        swiglu_grad = plain_sum(dot_at(low_normed, d_gate_up).astype(BF))
        down_grad = plain_sum(dot_at(hidden, d_ffn).astype(BF))
        after = []
    d_branch, d_attended, back_feat, gain1_part = branch_back(
        d_ffn, low_normed, stat, query_feat, d_gate_up, attended, lse_columns, gain1, (outer, swiglu), rows, tile,
        after,
    )
    if row_mode:
        d_branch, output_came = tied([d_branch, output_came])
        layer_output = lax.dynamic_slice_in_dim(output, mine * shard_len, shard_len, 0)
        layer_output = in_order([layer_output, output_came], mine)
    part_rows = jnp.arange(width, dtype=jnp.int32) % (width // split)
    losses = jnp.where(part_rows == place, loss if row_mode else loss / split, 0.0)
    losses_high = lax.reduce_precision(losses, 8, 7)
    small = jnp.stack([jnp.sum(gain1_part, 0), jnp.sum(gain2_part, 0), losses_high, losses - losses_high], axis=1)
    small = jnp.pad(small, ((0, 0), (0, LANES - 4))).astype(BF)
    out_sum = Reduction(weight_grad([(attended, d_branch)], small))
    grads, running = [], [out_sum]
    for n in range(PAIRS // BACK_PAIRS):
        columns, _ = beside(
            lambda sent: attend_back(
                query, d_attended, key_all, value_all, key_feat, back_feat, spans_back, tables_q, tables_k, rows,
                BACK_PAIRS, n * BACK_PAIRS, BACK_PAIRS, sent,
            ),
            running,
        )
        if not row_mode:

            def own_part(grad):
                grad = grad.reshape(rows, row_len, -1)
                grad = lax.psum_scatter(grad, "fsdp", scatter_dimension=1, tiled=True)
                return grad.reshape(tokens_here, -1)

            columns = [columns[0], own_part(columns[1]), own_part(columns[2])]
        if fast and n == PAIRS // BACK_PAIRS - 1:
            *columns, share = tied([*columns, share])
            both = lax.all_gather(share, "blk", axis=0)
        grads += columns
        (part,), _ = beside(lambda sent: [weight_grad([(x, g) for g in columns], None, sent)], running)
        running.append(Reduction(part, True))
    qkv_sums = running[1:]
    if row_mode:
        (moved,), _ = beside(
            lambda sent: [
                input_grad_part(d_branch, grads, qkv, (1 - mine) * shard_len, shard_len, BF, small_tile, sent)
            ],
            running,
        )
        exchange = flipped(moved, "fsdp", 1)
        (kept,), _ = beside(
            lambda sent: [
                input_grad_part(d_branch, grads, qkv, mine * shard_len, shard_len, F32, small_tile, sent, True)
            ],
            running,
        )
        beside(lambda _: [], running)
        if fast:
            (swiglu_grad, down_grad), _ = beside(lambda _: spread(both, width), running)
        (layer_output,), _ = beside(lambda _: [layer_output], running)
        kept, exchange = tied([kept, exchange])
        (input_grad,), _ = beside(
            lambda _: [placed(exchange, kept, (1 - mine) * shard_len, small_tile)], running
        )
        input_grad = input_grad.reshape(tokens.shape)
    else:
        input_grad = input_grad_part(d_branch, grads, qkv, 0, tokens_here, F32, small_tile).reshape(tokens.shape)
    while any(not r.done for r in running):
        beside(lambda _: [], running)
    wide, groups = BACK_PAIRS * LANES, PAIRS // BACK_PAIRS
    qkv_columns = [(g, part * wide, wide) for part in range(3) for g in range(groups)]
    (qkv_grad,) = unfold([r.result for r in qkv_sums], [qkv_columns])
    out_grad, small = unfold([out_sum.result], [[(0, 0, width)], [(0, width, LANES)]])
    queries = lax.axis_size("blk") * pairing.shape[0]
    return (
        jnp.sum(small[:, 2:4]) / queries,
        layer_output,
        input_grad,
        qkv_grad,
        out_grad,
        swiglu_grad,
        down_grad,
        small[:, 0],
        small[:, 1],
    )


BACK_PAIRS = 3


def solution(mesh):
    in_specs = (
        P("blk", "fsdp", None),
        P("blk", "fsdp", None),
        P("blk", "fsdp"),
        P("blk", None),
        P("blk", "fsdp"),
        P("blk"),
        P("fsdp", None),
        P("fsdp", None),
        P("fsdp", None),
        P("fsdp", None),
        P("fsdp"),
        P("fsdp"),
    )
    out_specs = (
        P(),
        P("blk", "fsdp", None),
        P("blk", "fsdp", None),
        P("fsdp", None),
        P("fsdp", None),
        P("fsdp", None),
        P("fsdp", None),
        P("fsdp"),
        P("fsdp"),
    )
    return jax.shard_map(shards, mesh=mesh, in_specs=in_specs, out_specs=out_specs, check_vma=False)
```
